32 devices in a mesh: seq: 4 (over y, x), frame: 8 (over z, core).
Axes of the slice: x: 2, y: 2, z: 4, core: 2. Of those that a mesh axis runs over, the one named last changes fastest.
Arguments:
- value_grad: bfloat16 [8, 4096, 512], P('frame', 'seq'), may hold values from -6 to 6
- w_value: bfloat16 [8192, 512], P('seq'), may hold values from -0.25 to 0.25
- norm_gain: float32 [8192], P('seq'), may hold values from 0.1 to 1.9
- vis_pos: int32 [8, 128], P('frame'), may hold values from 0 to 4095, as said below
- frame_owner: int32 [8, 128, 1], P('frame'), may hold values from 0 to 7; in each aligned block of 128 rows (0 to 127, 128 to 255, ..., all dimensions but the last counted through in order) at most 32 rows name the same one
- ques_span: int32 [8, 2], P('frame'), may hold values from 0 to 32, as said below
- vis_proj: bfloat16 [8, 128, 8192], P('frame', None, 'seq')
- vis_resid: bfloat16 [8, 128, 8192], P('frame', None, 'seq'), may hold values from -6 to 6
- ques_hidden: bfloat16 [8, 32, 8192], P('frame', None, 'seq'), may hold values from -6 to 6
- w_down: bfloat16 [8192, 8192], P(None, 'seq'), may hold values from -0.0625 to 0.0625
- pre_owned: bfloat16 [8, 8192, 256], P('frame', 'seq'), may hold values from -6 to 6
Outputs:
- pre_grad: bfloat16 [8, 8192, 256], P('frame', 'seq')
- ques_grad: bfloat16 [8, 32, 8192], P('frame', None, 'seq')
The draws below stay inside these ranges and needn't reach their ends.
Inputs may be any that keep to these rules, and one draw needn't show every extreme that they name: `vis_pos`: each row is distinct and increasing. `frame_owner`: in each sequence at most 32 visual tokens name the same owner. `ques_span`: column 1 is at least 1, and column 0 plus column 1 is at most 32.
All inputs are finite; a program needn't handle non-finite values.
Results may differ from the reference program's by a relative error of at most 0.015.
Values may be sent and summed in bfloat16 or wider, within the bound.
No kernel may reach another device: no remote copies, remote signals or barrier semaphores. Data moves between devices by JAX's collectives and lax.ppermute only.
A program may use at most 128 MiB of HBM per device.

```python
import math
import jax
import jax.numpy as jnp
import numpy as np
from jax import lax

D = 8192
KV = 512
HID = 8192
NV = 128
QLEN = 32
SEQS = 8
SEQ_LEN = 4096
CAP = 32
SLOTS = 256
N_SEQ = 4
N_FRAME = 8


def draw_vis_pos(key, part):
    row_keys = jax.random.split(jax.random.fold_in(key, 11), SEQS)

    def one_row(row_key):
        return jnp.sort(jax.random.permutation(row_key, SEQ_LEN)[:NV]).astype(jnp.int32)
    return jax.vmap(one_row)(row_keys)


def draw_ques_span(key, part):
    first_key, second_key = jax.random.split(jax.random.fold_in(key, 23))
    lengths = jax.random.randint(first_key, (SEQS,), 1, QLEN + 1)
    lengths = lengths.at[0].set(QLEN)
    shifts = jax.random.randint(second_key, (SEQS,), 0, 1 << 20)
    starts = shifts % (QLEN - lengths + 1)
    return jnp.stack([starts, lengths], axis=1).astype(jnp.int32)


def draw_vis_proj(key, part):
    base_key, column_key, row_key = jax.random.split(jax.random.fold_in(key, 37), 3)
    column_pos = jnp.arange(D, dtype=jnp.float32) / (D - 1)
    column_scale = 3.0 ** column_pos * 3.0 ** jax.random.uniform(column_key, (D,), dtype=jnp.float32) / 3.0
    base = jax.random.normal(base_key, (SEQS, NV, D), dtype=jnp.float32)
    row_scale = 10.0 ** (jax.random.uniform(row_key, (SEQS, NV, 1), dtype=jnp.float32) - 0.5)
    return (base * column_scale[None, None, :] * row_scale).astype(jnp.bfloat16)


def levels(own_key, extent, shards, least, high):
    loudness, own = 1.0, jax.random.fold_in(own_key, 6)
    for dim, blocks in shards:
        steps = jnp.exp(jax.random.uniform(jax.random.fold_in(own, dim), (blocks,), jnp.float32, least / len(shards), high / len(shards)))
        loudness = loudness * jnp.repeat(steps, extent[dim] // blocks).reshape([-1 if axis == dim else 1 for axis in range(len(extent))])
    return loudness


def shared_out(key, own, number, rows, amount, top, most, skew):
    ranking = jax.random.permutation(key, amount)
    heavy_load, common = load_shares(amount, rows * top, most, skew, True), load_shares(amount, rows * top, most, skew, False)
    places = jnp.arange(amount)

    def named(sizes, offset_by):
        used = int((sizes > 0).sum())
        fixed = max(1, used // 4)
        moved = fixed + (places - fixed + offset_by * (used - fixed)) % max(1, amount - fixed)
        return jnp.zeros((amount,), jnp.int32).at[ranking[jnp.where(places < fixed, places, moved)]].set(jnp.asarray(sizes, jnp.int32))

    sizes = jnp.where(number % 4 == 0, named(heavy_load, number // 4), named(common, number - number // 4 - 1))
    mixed = jax.random.permutation(jax.random.fold_in(own, 3), amount)
    donor, receiver = mixed[0:amount // 2 * 2:2], mixed[1:amount // 2 * 2:2]
    slack = jnp.minimum(sizes[donor] - 1, most - sizes[receiver]) // 2
    slack = jnp.where((donor == ranking[0]) | (receiver == ranking[0]) | (sizes[receiver] == 0), 0, jnp.maximum(slack, 0))
    moved = jax.random.randint(jax.random.fold_in(own, 4), (amount // 2,), 0, 1 << 20) % (slack + 1)
    sizes = sizes.at[donor].add(-moved).at[receiver].add(moved)
    labels = jnp.searchsorted(jnp.cumsum(sizes), jnp.arange(rows * top), side="right").astype(jnp.int32)
    listing = labels.reshape(top, rows).T
    listing = listing[jax.random.permutation(jax.random.fold_in(own, 1), rows)]
    offset_by = jax.random.randint(jax.random.fold_in(own, 2), (rows, 1), 0, top)
    return jnp.take_along_axis(listing, (jnp.arange(top)[None, :] + offset_by) % top, axis=1)


def load_shares(count, total, bound, lean, full):
    portions = [(1 << 20) // math.isqrt(grade ** lean) + 1 for grade in range(1, count + 1)]
    largest = bound if full else min(bound, max(-(-total // count), total * portions[0] // sum(portions)))
    least = 1 if total - largest >= count - 1 else 0
    given, surplus = [largest] + [least] * (count - 1), total - largest - least * (count - 1)
    while surplus > 0:
        candidates = [i for i in range(1, count) if given[i] < largest] or [i for i in range(1, count) if given[i] < bound]
        mass, budget = sum([portions[i] for i in candidates]), surplus
        for i in candidates:
            more = min(bound - given[i], max(1, budget * portions[i] // mass), surplus)
            given[i] = given[i] + more
            surplus = surplus - more
    return np.array(given)


def bell_draw(key, shape, deviation, most, pieces=(), kind=jnp.bfloat16):
    result = jax.random.normal(key, shape, jnp.float32) * deviation
    if len(pieces) > 0:
        result = levels(key, shape, pieces, -0.22, 0.18) * result
    return jnp.clip(result, min=-most, max=most).astype(kind)


def setup_inputs(seed: int = 0) -> dict:
    seeds = jax.random.split(jax.random.key(seed), 12)
    value_grad = bell_draw(seeds[0], (SEQS, SEQ_LEN, KV), 1.0, 6.0, ((0, 8), (1, 4)))
    w_value = bell_draw(seeds[1], (D, KV), KV ** -0.5, 0.25, ((0, 4),))
    norm_gain = jnp.clip(1.0 + 0.18 * jax.random.normal(seeds[2], (D,), jnp.float32), 0.1, 1.9)
    vis_pos = draw_vis_pos(jax.random.fold_in(seeds[11], 71), 0)
    frame_owner_keys = jax.random.split(jax.random.fold_in(seeds[4], 1), SEQS * NV // NV)
    frame_owner_turns = jax.random.permutation(jax.random.fold_in(seeds[4], 3), SEQS * NV // NV)
    frame_owner = jax.vmap(lambda own, number: shared_out(jax.random.fold_in(seeds[4], 2), own, number, NV, N_FRAME, 1, CAP, 2))(frame_owner_keys, frame_owner_turns).reshape((SEQS, NV, 1))
    ques_span = draw_ques_span(jax.random.fold_in(seeds[11], 71), 0)
    vis_proj = draw_vis_proj(jax.random.fold_in(seeds[11], 71), 0)
    vis_resid = bell_draw(seeds[7], (SEQS, NV, D), 1.0, 6.0, ((0, 8), (2, 4)))
    ques_hidden = bell_draw(seeds[8], (SEQS, QLEN, D), 1.0, 6.0, ((0, 8), (2, 4)))
    w_down = bell_draw(seeds[9], (HID, D), D ** -0.5, 0.0625, ((1, 4),))
    pre_owned = bell_draw(seeds[10], (SEQS, HID, SLOTS), 1.0, 6.0, ((0, 8), (1, 4)))
    return {"value_grad": value_grad, "w_value": w_value, "norm_gain": norm_gain, "vis_pos": vis_pos, "frame_owner": frame_owner, "ques_span": ques_span, "vis_proj": vis_proj, "vis_resid": vis_resid, "ques_hidden": ques_hidden, "w_down": w_down, "pre_owned": pre_owned}


epsilon = 1e-06

def gelu_slope(pre_act):
    normal_cdf = 0.5 * (1.0 + lax.erf(pre_act * 0.7071067811865476))
    density = jnp.exp(-0.5 * pre_act * pre_act) * 0.3989422804014327
    return normal_cdf + pre_act * density

def reference(value_grad, w_value, norm_gain, vis_pos, frame_owner, ques_span, vis_proj, vis_resid, ques_hidden, w_down, pre_owned):
    picked = jnp.take_along_axis(value_grad, vis_pos.astype(jnp.int32)[:, :, None], axis=1)
    normed_grad = jnp.einsum('bjk,dk->bjd', picked.astype(jnp.float32), w_value.astype(jnp.float32))
    projected = vis_proj.astype(jnp.float32)
    residual = vis_resid.astype(jnp.float32)
    norm_scale = norm_gain.astype(jnp.float32)
    span_start = ques_span[:, 0]
    span_count = ques_span[:, 1]
    places = jnp.arange(QLEN, dtype=jnp.int32)
    span_mask = ((places[None, :] >= span_start[:, None]) & (places[None, :] < (span_start + span_count)[:, None])).astype(jnp.float32)
    count_value = span_count.astype(jnp.float32)
    quest_mean = jnp.einsum('bt,btd->bd', span_mask, ques_hidden.astype(jnp.float32)) / count_value[:, None]
    gate_scale = 4.0 / math.sqrt(D)
    sum_query = lax.optimization_barrier(jnp.sum(projected * quest_mean[:, None, :], axis=-1))
    sum_square = lax.optimization_barrier(jnp.sum(projected * projected, axis=-1))
    sum_norm = lax.optimization_barrier(jnp.sum(norm_scale * normed_grad * projected, axis=-1))
    sum_resid = lax.optimization_barrier(jnp.sum(residual * projected, axis=-1))
    gate_value = jax.nn.sigmoid(gate_scale * sum_query)
    inv_rms = lax.rsqrt(gate_value * gate_value * sum_square / D + epsilon)
    inner_sum = gate_value * sum_norm
    coef_value = gate_value * inv_rms * inv_rms * inv_rms * inner_sum / D
    input_grad = residual + inv_rms[..., None] * norm_scale * normed_grad - coef_value[..., None] * projected
    gate_grad = sum_resid + inv_rms * sum_norm - coef_value * sum_square
    logit_grad = gate_grad * gate_value * (1.0 - gate_value)
    proj_grad = (gate_value[..., None] * input_grad + (logit_grad * gate_scale)[..., None] * quest_mean[:, None, :]).astype(jnp.bfloat16)
    quest_grad = lax.optimization_barrier(jnp.sum((logit_grad * gate_scale)[..., None] * projected, axis=1))
    ques_out = (span_mask[:, :, None] * quest_grad[:, None, :] / count_value[:, None, None]).astype(jnp.bfloat16)
    owners = frame_owner[:, :, 0].astype(jnp.int32)
    owner_hot = (owners[:, :, None] == jnp.arange(N_FRAME, dtype=jnp.int32)[None, None, :]).astype(jnp.int32)
    earlier = jnp.cumsum(owner_hot, axis=1) - owner_hot
    rank_in_owner = lax.optimization_barrier(jnp.sum(earlier * owner_hot, axis=2))
    rank_hot = (rank_in_owner[:, :, None] == jnp.arange(CAP, dtype=jnp.int32)[None, None, :]).astype(jnp.float32)
    routed = jnp.einsum('bjo,bjc,bjd->obcd', owner_hot.astype(jnp.float32), rank_hot, proj_grad.astype(jnp.float32))
    routed = routed.reshape(N_FRAME, SEQS * CAP, D).astype(jnp.bfloat16)
    weight_split = w_down.astype(jnp.float32).reshape(HID, N_SEQ, D // N_SEQ)

    def owner_work(pairs):
        owner_rows, pre_slots = pairs
        rows_split = owner_rows.astype(jnp.float32).reshape(SEQS * CAP, N_SEQ, D // N_SEQ)
        partial_value = jnp.einsum('nsd,hsd->shn', rows_split, weight_split)
        rounded = lax.optimization_barrier(partial_value.astype(jnp.bfloat16))
        hidden_grad = lax.optimization_barrier(jnp.sum(rounded.astype(jnp.float32), axis=0))
        pre_act = pre_slots.astype(jnp.float32)
        return (hidden_grad * gelu_slope(pre_act)).astype(jnp.bfloat16)
    pre_out = lax.map(owner_work, (routed, pre_owned))
    return (pre_out, ques_out)
```

```python
import functools
import math

import jax
import jax.numpy as jnp
from jax import lax
from jax.experimental import pallas as pl
from jax.experimental.pallas import tpu as pltpu
from jax.sharding import PartitionSpec as P

EPSILON = 1e-06
F32 = jnp.float32
BF16 = jnp.bfloat16
CHUNKS = 4
VMEM_BYTES = 48 * 1024 * 1024


def params():
    return pltpu.CompilerParams(vmem_limit_bytes=VMEM_BYTES)


def whole(shape):
    return pl.BlockSpec(shape, lambda *_: (0,) * len(shape))


def smem():
    return pl.BlockSpec(memory_space=pltpu.SMEM)


def exchange(value, axis, count):
    return [
        lax.ppermute(value, axis, [(i, i ^ step) for i in range(count)])
        for step in range(1, count)
    ]


def to_column(row):
    tokens = row.shape[1]
    return jnp.transpose(jnp.broadcast_to(row, (128, tokens)), (1, 0))


def lane_sums(value):
    width = value.shape[1]
    folded = value[:, :128]
    for at in range(128, width, 128):
        folded = folded + value[:, at : at + 128]
    return jnp.sum(jnp.transpose(folded, (1, 0)), axis=0, keepdims=True)


def spread(column, width):
    return jnp.concatenate([column] * (width // 128), axis=1)


def pick_kernel(pos_ref, rows_ref, own_ref):
    tokens, shard_len = pos_ref.shape[1], rows_ref.shape[1]
    offset = lax.axis_index("seq") * shard_len
    column = to_column(pos_ref[...] - offset)
    places = lax.broadcasted_iota(jnp.int32, (tokens, shard_len), 1)
    select = (spread(column, shard_len) == places).astype(BF16)
    own_ref[...] = jnp.dot(select, rows_ref[0], preferred_element_type=F32).astype(BF16)


def sums_kernel(span_ref, hidden_ref, proj_ref, resid_ref, stats_ref, mean_ref):
    start, count = span_ref[0, 0], span_ref[0, 1]
    length = hidden_ref.shape[1]
    places = lax.broadcasted_iota(jnp.int32, (length, 1), 0)
    mask = ((places >= start) & (places < start + count)).astype(F32)
    mean = jnp.sum(hidden_ref[0].astype(F32) * mask, axis=0, keepdims=True) / count.astype(F32)
    mean_ref[...] = mean
    proj = proj_ref[0].astype(F32)
    resid = resid_ref[0].astype(F32)
    stats_ref[0:1, :] = lane_sums(proj * mean)
    stats_ref[1:2, :] = lane_sums(proj * proj)
    stats_ref[2:3, :] = lane_sums(resid * proj)
    stats_ref[3:8, :] = jnp.zeros((5, stats_ref.shape[1]), F32)


def norm_kernel(*refs):
    *own_refs, weight_ref, gain_ref, proj_ref, scaled_ref, norm_ref = refs
    picked = own_refs[0][...].astype(F32)
    for ref in own_refs[1:]:
        picked = picked + ref[...].astype(F32)
    normed = lax.dot_general(
        picked.astype(BF16), weight_ref[...], (((1,), (1,)), ((), ())), preferred_element_type=F32
    )
    scaled = normed * gain_ref[...]
    scaled_ref[...] = scaled
    norm_ref[...] = jnp.broadcast_to(lane_sums(scaled * proj_ref[0].astype(F32)), norm_ref.shape)


def gate_kernel(features, peers, *refs):
    stats_refs = refs[:peers]
    norm_refs = refs[peers : 2 * peers]
    proj_ref, resid_ref, scaled_ref, mean_ref, grad_ref, logit_ref = refs[2 * peers :]
    stats = sum([ref[...] for ref in stats_refs[1:]], stats_refs[0][...])
    sum_norm = sum([ref[0:1, :] for ref in norm_refs[1:]], norm_refs[0][0:1, :])
    sum_query, sum_square, sum_resid = stats[0:1], stats[1:2], stats[2:3]
    gate_scale = 4.0 / math.sqrt(features)
    gate = jax.nn.sigmoid(gate_scale * sum_query)
    inv_rms = lax.rsqrt(gate * gate * sum_square / features + EPSILON)
    coef = gate * inv_rms * inv_rms * inv_rms * (gate * sum_norm) / features
    gate_grad = sum_resid + inv_rms * sum_norm - coef * sum_square
    logit = gate_grad * gate * (1.0 - gate) * gate_scale
    logit_ref[...] = jnp.broadcast_to(logit, logit_ref.shape)
    width = proj_ref.shape[2]
    gate_c, inv_c, coef_c, logit_c = map(to_column, (gate, inv_rms, coef, logit))
    for at in range(0, width, 128):
        cut = slice(at, at + 128)
        proj = proj_ref[0, :, cut].astype(F32)
        resid = resid_ref[0, :, cut].astype(F32)
        grad = gate_c * (resid + inv_c * scaled_ref[:, cut] - coef_c * proj)
        grad_ref[:, cut] = (grad + logit_c * mean_ref[:, cut]).astype(BF16)


def ques_kernel(span_ref, logit_ref, proj_ref, out_ref):
    start, count = span_ref[0, 0], span_ref[0, 1]
    length, width = out_ref.shape[1], out_ref.shape[2]
    places = lax.broadcasted_iota(jnp.int32, (length, 128), 0)
    mask = ((places >= start) & (places < start + count)).astype(F32)
    column = to_column(logit_ref[0:1, :])
    for at in range(0, width, 128):
        cut = slice(at, at + 128)
        total = jnp.sum(column * proj_ref[0, :, cut].astype(F32), axis=0, keepdims=True)
        out_ref[0, :, cut] = (mask * total / count.astype(F32)).astype(BF16)


def down_kernel(inner, weight_ref, grad_ref, *out_refs):
    step, part = pl.program_id(0), pl.program_id(1)
    block = weight_ref.shape[0]
    value = lax.dot_general(
        weight_ref[...], grad_ref[...], (((1,), (1,)), ((), ())), preferred_element_type=F32
    ).astype(BF16)
    for index, ref in enumerate(out_refs):
        @pl.when(step == index)
        def _():
            ref[pl.ds(pl.multiple_of(part * block, block), block), :] = value


def down_chunk(weight, grad, peers, chunk, chunks):
    hidden, width = weight.shape
    tokens = grad.shape[0]
    quarter = hidden // peers
    rows = quarter // chunks
    block = min(rows, 256)
    inner = rows // block

    def weight_map(step, part):
        owner = lax.axis_index("seq") ^ step
        return (owner * (quarter // block) + chunk * inner + part, 0)

    return pl.pallas_call(
        functools.partial(down_kernel, inner),
        grid=(peers, inner),
        in_specs=[pl.BlockSpec((block, width), weight_map), whole(grad.shape)],
        out_specs=[whole((rows, tokens))] * peers,
        out_shape=[jax.ShapeDtypeStruct((rows, tokens), BF16)] * peers,
        compiler_params=params(),
        cost_estimate=pl.CostEstimate(
            flops=2 * peers * rows * width * tokens,
            bytes_accessed=2 * peers * rows * width,
            transcendentals=0,
        ),
    )(weight, grad)


def place_kernel(slots, capacity, mine, *refs):
    owner_ref = refs[0]
    part_refs, out_refs = refs[1 : 1 + mine], refs[1 + mine :]
    tokens = owner_ref.shape[1]
    owner = owner_ref[...]
    column = to_column(owner)
    above = lax.broadcasted_iota(jnp.int32, (tokens, tokens), 0)
    below = lax.broadcasted_iota(jnp.int32, (tokens, tokens), 1)
    earlier = jnp.where((spread(column, tokens) == owner) & (above < below), 1.0, 0.0)
    rank = jnp.sum(earlier, axis=0, keepdims=True).astype(jnp.int32)
    target = (owner ^ lax.axis_index("frame")) * capacity + rank
    places = lax.broadcasted_iota(jnp.int32, (slots, tokens), 0)
    placing = (places == target).astype(BF16)
    total = part_refs[0][...].astype(F32)
    for ref in part_refs[1:]:
        total = total + ref[...].astype(F32)
    placed = lax.dot_general(
        placing, total.astype(BF16), (((1,), (1,)), ((), ())), preferred_element_type=F32
    ).astype(BF16)
    size = slots // len(out_refs)
    for index, ref in enumerate(out_refs):
        ref[...] = placed[index * size : (index + 1) * size, :]


def place(owner, parts, slots, capacity, pieces):
    rows, tokens = parts[0].shape
    return pl.pallas_call(
        functools.partial(place_kernel, slots, capacity, len(parts)),
        in_specs=[whole(owner.shape)] + [whole((rows, tokens))] * len(parts),
        out_specs=[whole((slots // pieces, rows))] * pieces,
        out_shape=[jax.ShapeDtypeStruct((slots // pieces, rows), BF16)] * pieces,
        grid=(1,),
        compiler_params=params(),
    )(owner, *parts)


def slope(pre_act):
    normal_cdf = 0.5 * (1.0 + lax.erf(pre_act * 0.7071067811865476))
    density = jnp.exp(-0.5 * pre_act * pre_act) * 0.3989422804014327
    return normal_cdf + pre_act * density


def final_kernel(capacity, aliased, *refs):
    out_ref = refs[-1]
    pre_ref = refs[0]
    part_refs = refs[1:-2] if aliased else refs[1:-1]
    slots = pre_ref.shape[2]
    joined = jnp.concatenate([ref[...] for ref in part_refs], axis=0)
    source = lax.broadcasted_iota(jnp.int32, (slots, slots), 0)
    goal = lax.broadcasted_iota(jnp.int32, (slots, slots), 1)
    moved = (goal ^ (lax.axis_index("frame") * capacity)) == source
    hidden = lax.dot_general(
        joined, moved.astype(BF16), (((0,), (0,)), ((), ())), preferred_element_type=F32
    )
    out_ref[0] = (hidden * slope(pre_ref[0].astype(F32))).astype(BF16)


def final(pre_owned, parts, held, capacity, chunk, chunks):
    rows = pre_owned.shape[1] // chunks
    slots = pre_owned.shape[2]
    block = pl.BlockSpec((1, rows, slots), lambda *_: (0, chunk, 0))
    aliased = held is not None
    return pl.pallas_call(
        functools.partial(final_kernel, capacity, aliased),
        grid=(1,),
        in_specs=[block]
        + [whole(part.shape) for part in parts]
        + [pl.BlockSpec(memory_space=pl.ANY)] * aliased,
        out_specs=block,
        out_shape=jax.ShapeDtypeStruct(pre_owned.shape, BF16),
        input_output_aliases={1 + len(parts): 0} if aliased else {},
        compiler_params=params(),
    )(pre_owned, *parts, *([held] if aliased else []))


def body(
    peers,
    owners_count,
    value_grad,
    w_value,
    norm_gain,
    vis_pos,
    frame_owner,
    ques_span,
    vis_proj,
    vis_resid,
    ques_hidden,
    w_down,
    pre_owned,
):
    _, tokens, width = vis_proj.shape
    key_width = w_value.shape[1]
    features = peers * width
    slots = pre_owned.shape[2]
    capacity = slots // owners_count
    gain = norm_gain.reshape(1, width)
    owner = frame_owner.reshape(1, tokens)
    row = jax.ShapeDtypeStruct((8, tokens), F32)

    own = pl.pallas_call(
        pick_kernel,
        out_shape=jax.ShapeDtypeStruct((tokens, key_width), BF16),
        compiler_params=params(),
    )(vis_pos, value_grad)
    own_all = [own] + exchange(own, "seq", peers)

    vmem = pl.BlockSpec(memory_space=pltpu.VMEM)
    stats, mean = pl.pallas_call(
        sums_kernel,
        in_specs=[smem(), vmem, vmem, vmem],
        out_shape=[row, jax.ShapeDtypeStruct((1, width), F32)],
        compiler_params=params(),
    )(ques_span, ques_hidden, vis_proj, vis_resid)
    stats_all = [stats] + exchange(stats, "seq", peers)

    scaled, norms = pl.pallas_call(
        norm_kernel,
        out_shape=[jax.ShapeDtypeStruct((tokens, width), F32), row],
        compiler_params=params(),
    )(*own_all, w_value, gain, vis_proj)
    norms_all = [norms] + exchange(norms, "seq", peers)

    grad, logit = pl.pallas_call(
        functools.partial(gate_kernel, features, peers),
        out_shape=[jax.ShapeDtypeStruct((tokens, width), BF16), row],
        compiler_params=params(),
    )(*stats_all, *norms_all, vis_proj, vis_resid, scaled, mean)

    ques_grad = pl.pallas_call(
        ques_kernel,
        in_specs=[smem(), vmem, vmem],
        out_shape=jax.ShapeDtypeStruct(ques_hidden.shape, BF16),
        compiler_params=params(),
    )(ques_span, logit, vis_proj)

    held = None
    for chunk in range(CHUNKS):
        partial = down_chunk(w_down, grad, peers, chunk, CHUNKS)
        sums = [partial[0]] + [
            lax.ppermute(partial[k], "seq", [(i, i ^ k) for i in range(peers)])
            for k in range(1, peers)
        ]
        if capacity % 16 == 0:
            placed = place(owner, sums, slots, capacity, owners_count)
            parts = [placed[0]] + [
                lax.ppermute(placed[k], "frame", [(i, i ^ k) for i in range(owners_count)])
                for k in range(1, owners_count)
            ]
        else:
            (placed,) = place(owner, sums, slots, capacity, 1)
            mine = lax.axis_index("frame")
            order = jnp.arange(owners_count) ^ mine
            split = placed.reshape(owners_count, capacity, -1)[order]
            split = lax.all_to_all(split, "frame", split_axis=0, concat_axis=0, tiled=True)
            parts = [split[order].reshape(slots, -1)]
        held = final(pre_owned, parts, held, capacity, chunk, CHUNKS)
    return (held, ques_grad)


def solution(mesh):
    in_specs = (
        P("frame", "seq", None),
        P("seq", None),
        P("seq"),
        P("frame", None),
        P("frame", None, None),
        P("frame", None),
        P("frame", None, "seq"),
        P("frame", None, "seq"),
        P("frame", None, "seq"),
        P(None, "seq"),
        P("frame", "seq", None),
    )
    out_specs = (P("frame", "seq", None), P("frame", None, "seq"))
    run = functools.partial(body, mesh.shape["seq"], mesh.shape["frame"])
    return jax.shard_map(run, mesh=mesh, in_specs=in_specs, out_specs=out_specs, check_vma=False)
```

```python
import functools
import math

import jax
import jax.numpy as jnp
from jax import lax
from jax.experimental import pallas as pl
from jax.experimental.pallas import tpu as pltpu
from jax.sharding import PartitionSpec as P

EPSILON = 1e-06
F32 = jnp.float32
BF16 = jnp.bfloat16
LANES = 128
VMEM_BYTES = 40 * 1024 * 1024
HBM = pl.BlockSpec(memory_space=pltpu.HBM)
VMEM = pl.BlockSpec(memory_space=pltpu.VMEM)
ANY = pl.BlockSpec(memory_space=pl.ANY)


def call(kernel, out_shape, in_specs, scratch=(), aliases=None, out_specs=None):
    return pl.pallas_call(
        kernel,
        out_shape=out_shape,
        in_specs=in_specs,
        out_specs=jax.tree.map(lambda _: VMEM, out_shape) if out_specs is None else out_specs,
        scratch_shapes=list(scratch),
        input_output_aliases=aliases or {},
        compiler_params=pltpu.CompilerParams(vmem_limit_bytes=VMEM_BYTES),
        cost_estimate=pl.CostEstimate(flops=1024, bytes_accessed=1024, transcendentals=0),
    )


def shape(dims, dtype):
    return jax.ShapeDtypeStruct(dims, dtype)


def swap(value, axis, count, step):
    return lax.ppermute(value, axis, [(i, i ^ step) for i in range(count)])


def to_column(row):
    return jnp.transpose(jnp.broadcast_to(row, (LANES, row.shape[1])), (1, 0))


def pick_kernel(pieces, pos_hbm, rows_hbm, own_ref, pos, rows, sems):
    tokens, shard_len = pos.shape[1], rows.shape[0]
    size = shard_len // pieces
    head = pltpu.make_async_copy(pos_hbm, pos, sems.at[pieces])
    head.start()
    copies = []
    for piece in range(pieces):
        cut = pl.ds(piece * size, size)
        copies.append(
            pltpu.make_async_copy(rows_hbm.at[0, cut], rows.at[cut], sems.at[piece])
        )
        copies[-1].start()
    offset = lax.axis_index("seq") * shard_len
    head.wait()
    column = to_column(pos[...] - offset)
    lanes = lax.broadcasted_iota(jnp.int32, (tokens, LANES), 1)
    total = None
    for piece in range(pieces):
        select = jnp.concatenate(
            [
                jnp.where(column == lanes + at, 1.0, 0.0).astype(BF16)
                for at in range(piece * size, (piece + 1) * size, LANES)
            ],
            axis=1,
        )
        copies[piece].wait()
        part = jnp.dot(
            select, rows[piece * size : (piece + 1) * size, :], preferred_element_type=F32
        )
        total = part if total is None else total + part
    own_ref[...] = total.astype(BF16)


def load_kernel(
    span_hbm, hidden_hbm, gain_hbm, proj_hbm, resid_hbm, weight_hbm,
    stats_ref, projt_ref, residt_ref, gaint_ref, meant_ref, weight_ref,
    span, hidden, gain, proj, resid, sems,
):
    copies = [
        pltpu.make_async_copy(source, target, sems.at[index])
        for index, (source, target) in enumerate(
            [
                (span_hbm, span),
                (hidden_hbm.at[0], hidden),
                (gain_hbm, gain),
                (proj_hbm.at[0], proj),
                (resid_hbm.at[0], resid),
                (weight_hbm, weight_ref),
            ]
        )
    ]
    for copy in copies:
        copy.start()
    for copy in copies[:5]:
        copy.wait()
    start, count = span[0, 0], span[0, 1]
    tokens, width = proj.shape
    places = lax.broadcasted_iota(jnp.int32, (hidden.shape[0], 1), 0)
    mask = ((places >= start) & (places < start + count)).astype(F32)
    query = square = cross = jnp.zeros((LANES, tokens), F32)
    for at in range(0, width, LANES):
        cut = slice(at, at + LANES)
        mean = jnp.sum(hidden[:, cut].astype(F32) * mask, axis=0, keepdims=True)
        meant = to_column(mean / count.astype(F32))
        projt = jnp.transpose(proj[:, cut].astype(F32), (1, 0))
        residt = jnp.transpose(resid[:, cut].astype(F32), (1, 0))
        meant_ref[cut, :] = meant
        projt_ref[cut, :] = projt
        residt_ref[cut, :] = residt
        gaint_ref[cut, :] = to_column(gain[:, cut])
        query = query + projt * meant
        square = square + projt * projt
        cross = cross + projt * residt
    stats_ref[...] = jnp.zeros(stats_ref.shape, F32)
    for row, value in enumerate((query, square, cross)):
        stats_ref[row : row + 1, :] = jnp.sum(value, axis=0, keepdims=True)
    copies[5].wait()


def norm_kernel(peers, *refs):
    own_refs = refs[:peers]
    stats_ref, weight_ref, gaint_ref, projt_ref, scaledt_ref, sums_ref, pickedt = refs[peers:]
    key_width = own_refs[0].shape[1]
    for at in range(0, key_width, LANES):
        cut = slice(at, at + LANES)
        picked = own_refs[0][:, cut].astype(F32)
        for ref in own_refs[1:]:
            picked = picked + ref[:, cut].astype(F32)
        pickedt[cut, :] = jnp.transpose(picked, (1, 0)).astype(BF16)
    width, tokens = projt_ref.shape
    total = jnp.zeros((LANES, tokens), F32)
    for at in range(0, width, 256):
        cut = slice(at, at + 256)
        normed = jnp.dot(weight_ref[cut, :], pickedt[...], preferred_element_type=F32)
        scaled = normed * gaint_ref[cut, :]
        scaledt_ref[cut, :] = scaled
        terms = scaled * projt_ref[cut, :]
        total = total + terms[:LANES] + terms[LANES:]
    sums_ref[...] = stats_ref[...]
    sums_ref[3:4, :] = jnp.sum(total, axis=0, keepdims=True)


def start_weights(weight_hbm, weights, sems, peers, base, rows):
    quarter = weight_hbm.shape[0] // peers
    block = min(rows, 256)
    copies = []
    for peer in range(peers):
        first = (lax.axis_index("seq") ^ peer) * quarter + base
        for at in range(0, rows, block):
            index = len(copies)
            copies.append(
                pltpu.make_async_copy(
                    weight_hbm.at[pl.ds(pl.multiple_of(first + at, block), block)],
                    weights.at[pl.ds(peer * rows + at, block)],
                    sems.at[index],
                )
            )
            copies[-1].start()
    return copies


def multiply(weights, copies, gradt_ref, out_refs):
    rows = out_refs[0].shape[0]
    block = min(rows, 256)
    inner = rows // block
    for index, copy in enumerate(copies):
        peer, part = index // inner, index % inner
        copy.wait()
        value = jnp.dot(
            weights[index * block : (index + 1) * block, :],
            gradt_ref[...],
            preferred_element_type=F32,
        )
        out_refs[peer][part * block : (part + 1) * block, :] = value.astype(BF16)


def gate_kernel(features, peers, base, rows, *refs):
    sums_refs = refs[:peers]
    projt_ref, residt_ref, scaledt_ref, meant_ref, weight_hbm = refs[peers : peers + 5]
    gradt_ref, logit_ref = refs[peers + 5 : peers + 7]
    out_refs = refs[peers + 7 : -2]
    weights, sems = refs[-2:]
    copies = start_weights(weight_hbm, weights, sems, peers, base, rows)
    sums = sums_refs[0][...]
    for ref in sums_refs[1:]:
        sums = sums + ref[...]
    sum_query, sum_square, sum_resid, sum_norm = (sums[i : i + 1] for i in range(4))
    gate_scale = 4.0 / math.sqrt(features)
    gate = jax.nn.sigmoid(gate_scale * sum_query)
    inv_rms = lax.rsqrt(gate * gate * sum_square / features + EPSILON)
    coef = gate * inv_rms * inv_rms * inv_rms * (gate * sum_norm) / features
    gate_grad = sum_resid + inv_rms * sum_norm - coef * sum_square
    logit = gate_grad * gate * (1.0 - gate) * gate_scale
    logit_ref[...] = jnp.broadcast_to(logit, logit_ref.shape)
    for at in range(0, projt_ref.shape[0], LANES):
        cut = slice(at, at + LANES)
        grad = residt_ref[cut, :] + inv_rms * scaledt_ref[cut, :] - coef * projt_ref[cut, :]
        gradt_ref[cut, :] = (gate * grad + logit * meant_ref[cut, :]).astype(BF16)
    multiply(weights, copies, gradt_ref, out_refs)


def down_kernel(peers, base, rows, after, *refs):
    weight_hbm, gradt_ref = refs[:2]
    out_refs = refs[2 + after : -2]
    weights, sems = refs[-2:]
    copies = start_weights(weight_hbm, weights, sems, peers, base, rows)
    multiply(weights, copies, gradt_ref, out_refs)


def ques_kernel(span_hbm, logit_ref, proj_hbm, after_ref, out_ref, span, proj, sems):
    del after_ref
    head = pltpu.make_async_copy(span_hbm, span, sems.at[0])
    load = pltpu.make_async_copy(proj_hbm.at[0], proj, sems.at[1])
    head.start()
    load.start()
    head.wait()
    start, count = span[0, 0], span[0, 1]
    length, width = out_ref.shape[1], out_ref.shape[2]
    places = lax.broadcasted_iota(jnp.int32, (length, LANES), 0)
    mask = ((places >= start) & (places < start + count)).astype(F32)
    column = to_column(logit_ref[0:1, :])
    load.wait()
    for at in range(0, width, LANES):
        cut = slice(at, at + LANES)
        total = jnp.sum(column * proj[:, cut].astype(F32), axis=0, keepdims=True)
        out_ref[0, :, cut] = (mask * total / count.astype(F32)).astype(BF16)


def place_kernel(capacity, owners_count, halves, mine, *refs):
    owner_hbm = refs[0]
    part_refs = refs[1 : 1 + mine]
    out_refs = refs[-2 - halves : -2]
    owner_ref, sem = refs[-2:]
    head = pltpu.make_async_copy(owner_hbm, owner_ref, sem.at[0])
    head.start()
    head.wait()
    tokens = owner_ref.shape[1]
    owner = owner_ref[...]
    column = to_column(owner)
    above = lax.broadcasted_iota(jnp.int32, (tokens, tokens), 0)
    below = lax.broadcasted_iota(jnp.int32, (tokens, tokens), 1)
    earlier = jnp.where((column == owner) & (above < below), 1.0, 0.0)
    rank = jnp.sum(earlier, axis=0, keepdims=True).astype(jnp.int32)
    away = owner ^ lax.axis_index("frame")
    if halves == 2:
        away = (away & 1) * (owners_count // 2) + (away >> 1)
    target = away * capacity + rank
    slots = owners_count * capacity
    places = lax.broadcasted_iota(jnp.int32, (slots, tokens), 0)
    placing = jnp.where(places == target, 1.0, 0.0).astype(BF16)
    total = part_refs[0][...].astype(F32)
    for ref in part_refs[1:]:
        total = total + ref[...].astype(F32)
    placed = lax.dot_general(
        placing, total.astype(BF16), (((1,), (1,)), ((), ())), preferred_element_type=F32
    ).astype(BF16)
    size = slots // halves
    for index, ref in enumerate(out_refs):
        ref[...] = placed[index * size : (index + 1) * size, :]


def group_kernel(capacity, same_ref, other_ref, *out_refs):
    for index, ref in enumerate(out_refs):
        cut = slice(index * capacity, (index + 1) * capacity)
        ref[:capacity, :] = same_ref[cut, :]
        ref[capacity:, :] = other_ref[cut, :]


def slope(pre_act):
    normal_cdf = 0.5 * (1.0 + lax.erf(pre_act * 0.7071067811865476))
    density = jnp.exp(-0.5 * pre_act * pre_act) * 0.3989422804014327
    return normal_cdf + pre_act * density


def final_kernel(capacity, base, count, *refs):
    part_refs = refs[:count]
    pre_hbm = refs[count]
    out_hbm, pre, out, sems = refs[-4:]
    rows, slots = pre.shape
    cut = pl.ds(base, rows)
    load = pltpu.make_async_copy(pre_hbm.at[0, cut], pre, sems.at[0])
    load.start()
    joined = jnp.concatenate([ref[...] for ref in part_refs], axis=0)
    source = lax.broadcasted_iota(jnp.int32, (slots, slots), 0)
    goal = lax.broadcasted_iota(jnp.int32, (slots, slots), 1)
    moved = (goal ^ (lax.axis_index("frame") * capacity)) == source
    hidden = lax.dot_general(
        joined,
        jnp.where(moved, 1.0, 0.0).astype(BF16),
        (((0,), (0,)), ((), ())),
        preferred_element_type=F32,
    )
    load.wait()
    out[...] = (hidden * slope(pre[...].astype(F32))).astype(BF16)
    store = pltpu.make_async_copy(out, out_hbm.at[0, cut], sems.at[1])
    store.start()
    store.wait()


def chunk_rows(quarter):
    if quarter % 2048 == 0:
        return [quarter // 4, 3 * quarter // 8, 3 * quarter // 8]
    return [quarter // 2] * 2


def body(
    peers,
    owners_count,
    value_grad,
    w_value,
    norm_gain,
    vis_pos,
    frame_owner,
    ques_span,
    vis_proj,
    vis_resid,
    ques_hidden,
    w_down,
    pre_owned,
):
    _, tokens, width = vis_proj.shape
    shard_len, key_width = value_grad.shape[1:]
    length = ques_hidden.shape[1]
    features = peers * width
    slots = pre_owned.shape[2]
    capacity = slots // owners_count
    gain = norm_gain.reshape(1, width)
    owner = frame_owner.reshape(1, tokens)
    row = shape((8, tokens), F32)
    tall = shape((width, tokens), F32)
    dma = pltpu.SemaphoreType.DMA

    pieces = max(1, shard_len // 256)
    own = call(
        functools.partial(pick_kernel, pieces),
        shape((tokens, key_width), BF16),
        [HBM, HBM],
        [
            pltpu.VMEM((1, tokens), jnp.int32),
            pltpu.VMEM((shard_len, key_width), BF16),
            dma((pieces + 1,)),
        ],
    )(vis_pos, value_grad)
    own_all = [own] + [swap(own, "seq", peers, k) for k in range(1, peers)]

    stats, projt, residt, gaint, meant, weight = call(
        load_kernel,
        [row, tall, tall, tall, tall, shape(w_value.shape, BF16)],
        [HBM] * 6,
        [
            pltpu.SMEM((1, 2), jnp.int32),
            pltpu.VMEM((length, width), BF16),
            pltpu.VMEM((1, width), F32),
            pltpu.VMEM((tokens, width), BF16),
            pltpu.VMEM((tokens, width), BF16),
            dma((6,)),
        ],
    )(ques_span, ques_hidden, gain, vis_proj, vis_resid, w_value)

    scaledt, sums = call(
        functools.partial(norm_kernel, peers),
        [tall, row],
        [VMEM] * (peers + 4),
        [pltpu.VMEM((key_width, tokens), BF16)],
    )(*own_all, stats, weight, gaint, projt)
    sums_all = [sums] + [swap(sums, "seq", peers, k) for k in range(1, peers)]

    chunks = chunk_rows(w_down.shape[0] // peers)

    def weights_scratch(rows):
        copies = peers * (rows // min(rows, 256))
        return [pltpu.VMEM((peers * rows, width), BF16), dma((copies,))]

    def first_chunk():
        rows = chunks[0]
        gradt, logit, *partial = call(
            functools.partial(gate_kernel, features, peers, 0, rows),
            [shape((width, tokens), BF16), row] + [shape((rows, tokens), BF16)] * peers,
            [VMEM] * (peers + 4) + [HBM],
            weights_scratch(rows),
        )(*sums_all, projt, residt, scaledt, meant, w_down)
        return gradt, logit, partial

    def next_chunk(base, rows, after):
        return call(
            functools.partial(down_kernel, peers, base, rows, len(after)),
            [shape((rows, tokens), BF16)] * peers,
            [HBM, VMEM] + [ANY] * len(after),
            weights_scratch(rows),
        )(w_down, gradt, *after)

    def reduce(partial):
        return [partial[0]] + [swap(partial[k], "seq", peers, k) for k in range(1, peers)]

    paired = capacity % 16 == 0 and owners_count % 2 == 0
    halves = 2 if paired else 1

    def route(parts, after):
        rows = parts[0].shape[0]
        placed = call(
            functools.partial(place_kernel, capacity, owners_count, halves, len(parts)),
            [shape((slots // halves, rows), BF16)] * halves,
            [HBM] + [VMEM] * len(parts) + [ANY] * len(after),
            [pltpu.VMEM((1, tokens), jnp.int32), dma((1,))],
        )(owner, *parts, *after)
        if not paired:
            order = jnp.arange(owners_count) ^ lax.axis_index("frame")
            split = placed[0].reshape(owners_count, capacity, rows)[order]
            split = lax.all_to_all(split, "frame", split_axis=0, concat_axis=0, tiled=True)
            return [split[order].reshape(slots, rows)]
        same, other = placed
        other = swap(other, "frame", owners_count, 1)
        pairs = owners_count // 2
        grouped = call(
            functools.partial(group_kernel, capacity),
            [shape((2 * capacity, rows), BF16)] * pairs,
            [VMEM, VMEM],
        )(same, other)
        return [grouped[0]] + [
            swap(grouped[k], "frame", owners_count, 2 * k) for k in range(1, pairs)
        ]

    def finish(parts, base, rows, held):
        return call(
            functools.partial(final_kernel, capacity, base, len(parts)),
            shape(pre_owned.shape, BF16),
            [VMEM] * len(parts) + [HBM] + [HBM] * len(held),
            [
                pltpu.VMEM((rows, slots), BF16),
                pltpu.VMEM((rows, slots), BF16),
                dma((2,)),
            ],
            {len(parts) + 1: 0} if held else None,
            HBM,
        )(*parts, pre_owned, *held)

    bases = [sum(chunks[:i]) for i in range(len(chunks))]
    gradt, logit, partial = first_chunk()
    waiting = [reduce(partial), reduce(next_chunk(bases[1], chunks[1], []))]
    routed = []
    for index in range(len(chunks)):
        after = []
        if index == len(chunks) - 1:
            ques_grad = call(
                ques_kernel,
                shape(ques_hidden.shape, BF16),
                [HBM, VMEM, HBM, ANY],
                [
                    pltpu.SMEM((1, 2), jnp.int32),
                    pltpu.VMEM((tokens, width), BF16),
                    dma((2,)),
                ],
            )(ques_span, logit, vis_proj, routed[-1][0])
            after = [ques_grad]
        routed.append(route(waiting[index], after))
        if index + 2 < len(chunks):
            ahead = index + 2
            waiting.append(reduce(next_chunk(bases[ahead], chunks[ahead], [routed[-1][0]])))
    held = []
    for index in range(len(chunks)):
        held = [finish(routed[index], bases[index], chunks[index], held)]
    return (held[0], ques_grad)


def solution(mesh):
    in_specs = (
        P("frame", "seq", None),
        P("seq", None),
        P("seq"),
        P("frame", None),
        P("frame", None, None),
        P("frame", None),
        P("frame", None, "seq"),
        P("frame", None, "seq"),
        P("frame", None, "seq"),
        P(None, "seq"),
        P("frame", "seq", None),
    )
    out_specs = (P("frame", "seq", None), P("frame", None, "seq"))
    run = functools.partial(body, mesh.shape["seq"], mesh.shape["frame"])
    return jax.shard_map(run, mesh=mesh, in_specs=in_specs, out_specs=out_specs, check_vma=False)
```

```python
import functools
import math

import jax
import jax.numpy as jnp
from jax import lax
from jax.experimental import pallas as pl
from jax.experimental.pallas import tpu as pltpu
from jax.sharding import PartitionSpec as P

EPSILON = 1e-06
F32 = jnp.float32
BF16 = jnp.bfloat16
LANES = 128
MIB = 1024 * 1024
GRANT, LOAD_GRANT, PICK_GRANT = 40, 40, 63
HBM = pl.BlockSpec(memory_space=pltpu.HBM)
VMEM = pl.BlockSpec(memory_space=pltpu.VMEM)
ANY = pl.BlockSpec(memory_space=pl.ANY)


def call(kernel, out_shape, in_specs, scratch=(), aliases=None, out_specs=None, grant=GRANT):
    return pl.pallas_call(
        kernel,
        out_shape=out_shape,
        in_specs=in_specs,
        out_specs=jax.tree.map(lambda _: VMEM, out_shape) if out_specs is None else out_specs,
        scratch_shapes=list(scratch),
        input_output_aliases=aliases or {},
        compiler_params=pltpu.CompilerParams(vmem_limit_bytes=grant * MIB),
        cost_estimate=pl.CostEstimate(flops=1024, bytes_accessed=1024, transcendentals=0),
    )


class Chain:
    def __init__(self):
        self.last = []

    def call(self, kernel, out_shape, in_specs, scratch=(), aliases=None, out_specs=None):
        given, made, linked = len(in_specs), len(out_shape), len(self.last)

        def run(*refs):
            outs = refs[given + linked :]
            outs[made][...] = jnp.zeros(outs[made].shape, F32)
            kernel(*refs[:given], *outs[:made], *outs[made + 1 :])

        out_specs = [VMEM] * made if out_specs is None else out_specs
        run_call = call(
            run,
            [*out_shape, shape((8, LANES), F32)],
            [*in_specs, *[VMEM] * linked],
            scratch,
            aliases,
            [*out_specs, VMEM],
        )

        def apply(*args):
            *results, token = run_call(*args, *self.last)
            self.last = [token]
            return results

        return apply


def shape(dims, dtype):
    return jax.ShapeDtypeStruct(dims, dtype)


def swap(value, axis, count, step):
    return lax.ppermute(value, axis, [(i, i ^ step) for i in range(count)])


def to_column(row):
    return jnp.transpose(jnp.broadcast_to(row, (LANES, row.shape[1])), (1, 0))


def pick_kernel(pieces, pos_hbm, rows_hbm, own_ref, pos, rows, sems):
    tokens, shard_len = pos.shape[1], rows.shape[0]
    size = shard_len // pieces
    head = pltpu.make_async_copy(pos_hbm, pos, sems.at[pieces])
    head.start()
    copies = []
    for piece in range(pieces):
        cut = pl.ds(piece * size, size)
        copies.append(
            pltpu.make_async_copy(rows_hbm.at[0, cut], rows.at[cut], sems.at[piece])
        )
        copies[-1].start()
    offset = lax.axis_index("seq") * shard_len
    head.wait()
    column = to_column(pos[...] - offset)
    lanes = lax.broadcasted_iota(jnp.int32, (tokens, LANES), 1)
    total = None
    for piece in range(pieces):
        select = jnp.concatenate(
            [
                jnp.where(column == lanes + at, 1.0, 0.0).astype(BF16)
                for at in range(piece * size, (piece + 1) * size, LANES)
            ],
            axis=1,
        )
        copies[piece].wait()
        part = jnp.dot(
            select, rows[piece * size : (piece + 1) * size, :], preferred_element_type=F32
        )
        total = part if total is None else total + part
    own_ref[...] = total.astype(BF16)


def load_kernel(
    span_hbm, hidden_hbm, gain_hbm, proj_hbm, resid_hbm, weight_hbm,
    stats_ref, projt_ref, residt_ref, gaint_ref, meant_ref, weight_ref,
    span, hidden, gain, proj, resid, sems,
):
    copies = [
        pltpu.make_async_copy(source, target, sems.at[index])
        for index, (source, target) in enumerate(
            [
                (span_hbm, span),
                (hidden_hbm.at[0], hidden),
                (gain_hbm, gain),
                (proj_hbm.at[0], proj),
                (resid_hbm.at[0], resid),
                (weight_hbm, weight_ref),
            ]
        )
    ]
    for copy in copies:
        copy.start()
    for copy in copies[:5]:
        copy.wait()
    start, count = span[0, 0], span[0, 1]
    tokens, width = proj.shape
    places = lax.broadcasted_iota(jnp.int32, (hidden.shape[0], 1), 0)
    mask = ((places >= start) & (places < start + count)).astype(F32)
    query = square = cross = jnp.zeros((LANES, tokens), F32)
    for at in range(0, width, LANES):
        cut = slice(at, at + LANES)
        mean = jnp.sum(hidden[:, cut].astype(F32) * mask, axis=0, keepdims=True)
        meant = to_column(mean / count.astype(F32))
        projt = jnp.transpose(proj[:, cut].astype(F32), (1, 0))
        residt = jnp.transpose(resid[:, cut].astype(F32), (1, 0))
        meant_ref[cut, :] = meant
        projt_ref[cut, :] = projt
        residt_ref[cut, :] = residt
        gaint_ref[cut, :] = to_column(gain[:, cut])
        query = query + projt * meant
        square = square + projt * projt
        cross = cross + projt * residt
    stats_ref[...] = jnp.zeros(stats_ref.shape, F32)
    for row, value in enumerate((query, square, cross)):
        stats_ref[row : row + 1, :] = jnp.sum(value, axis=0, keepdims=True)
    copies[5].wait()


def norm_kernel(peers, *refs):
    own_refs = refs[:peers]
    stats_ref, weight_ref, gaint_ref, projt_ref, scaledt_ref, sums_ref, pickedt = refs[peers:]
    key_width = own_refs[0].shape[1]
    for at in range(0, key_width, LANES):
        cut = slice(at, at + LANES)
        picked = own_refs[0][:, cut].astype(F32)
        for ref in own_refs[1:]:
            picked = picked + ref[:, cut].astype(F32)
        pickedt[cut, :] = jnp.transpose(picked, (1, 0)).astype(BF16)
    width, tokens = projt_ref.shape
    total = jnp.zeros((LANES, tokens), F32)
    for at in range(0, width, 256):
        cut = slice(at, at + 256)
        normed = jnp.dot(weight_ref[cut, :], pickedt[...], preferred_element_type=F32)
        scaled = normed * gaint_ref[cut, :]
        scaledt_ref[cut, :] = scaled
        terms = scaled * projt_ref[cut, :]
        total = total + terms[:LANES] + terms[LANES:]
    sums_ref[...] = stats_ref[...]
    sums_ref[3:4, :] = jnp.sum(total, axis=0, keepdims=True)


def start_weights(weight_hbm, weights, sems, peers, base, rows):
    quarter = weight_hbm.shape[0] // peers
    block = min(rows, 256)
    copies = []
    for peer in range(peers):
        first = (lax.axis_index("seq") ^ peer) * quarter + base
        for at in range(0, rows, block):
            index = len(copies)
            copies.append(
                pltpu.make_async_copy(
                    weight_hbm.at[pl.ds(pl.multiple_of(first + at, block), block)],
                    weights.at[pl.ds(peer * rows + at, block)],
                    sems.at[index],
                )
            )
            copies[-1].start()
    return copies


def multiply(weights, copies, gradt_ref, out_refs):
    rows = out_refs[0].shape[0]
    inner = len(copies) // len(out_refs)
    for peer, ref in enumerate(out_refs):
        for copy in copies[peer * inner : (peer + 1) * inner]:
            copy.wait()
        value = jnp.dot(
            weights[peer * rows : (peer + 1) * rows, :],
            gradt_ref[...],
            preferred_element_type=F32,
        )
        ref[...] = value.astype(BF16)


def gate_kernel(features, peers, base, rows, *refs):
    sums_refs = refs[:peers]
    projt_ref, residt_ref, scaledt_ref, meant_ref, weight_hbm = refs[peers : peers + 5]
    gradt_ref, logit_ref = refs[peers + 5 : peers + 7]
    out_refs = refs[peers + 7 : -2]
    weights, sems = refs[-2:]
    copies = start_weights(weight_hbm, weights, sems, peers, base, rows)
    sums = sums_refs[0][...]
    for ref in sums_refs[1:]:
        sums = sums + ref[...]
    sum_query, sum_square, sum_resid, sum_norm = (sums[i : i + 1] for i in range(4))
    gate_scale = 4.0 / math.sqrt(features)
    gate = jax.nn.sigmoid(gate_scale * sum_query)
    inv_rms = lax.rsqrt(gate * gate * sum_square / features + EPSILON)
    coef = gate * inv_rms * inv_rms * inv_rms * (gate * sum_norm) / features
    gate_grad = sum_resid + inv_rms * sum_norm - coef * sum_square
    logit = gate_grad * gate * (1.0 - gate) * gate_scale
    logit_ref[...] = jnp.broadcast_to(logit, logit_ref.shape)
    for at in range(0, projt_ref.shape[0], LANES):
        cut = slice(at, at + LANES)
        grad = residt_ref[cut, :] + inv_rms * scaledt_ref[cut, :] - coef * projt_ref[cut, :]
        gradt_ref[cut, :] = (gate * grad + logit * meant_ref[cut, :]).astype(BF16)
    multiply(weights, copies, gradt_ref, out_refs)


def down_kernel(peers, base, rows, *refs):
    weight_hbm, gradt_ref = refs[:2]
    out_refs = refs[2:-2]
    weights, sems = refs[-2:]
    copies = start_weights(weight_hbm, weights, sems, peers, base, rows)
    multiply(weights, copies, gradt_ref, out_refs)


def ques_kernel(span_hbm, logit_ref, proj_hbm, out_ref, span, proj, sems):
    head = pltpu.make_async_copy(span_hbm, span, sems.at[0])
    load = pltpu.make_async_copy(proj_hbm.at[0], proj, sems.at[1])
    head.start()
    load.start()
    head.wait()
    start, count = span[0, 0], span[0, 1]
    length, width = out_ref.shape[1], out_ref.shape[2]
    places = lax.broadcasted_iota(jnp.int32, (length, LANES), 0)
    mask = ((places >= start) & (places < start + count)).astype(F32)
    column = to_column(logit_ref[0:1, :])
    load.wait()
    for at in range(0, width, LANES):
        cut = slice(at, at + LANES)
        total = jnp.sum(column * proj[:, cut].astype(F32), axis=0, keepdims=True)
        out_ref[0, :, cut] = (mask * total / count.astype(F32)).astype(BF16)


def place_kernel(capacity, owners_count, pieces, mine, *refs):
    owner_hbm = refs[0]
    part_refs = refs[1 : 1 + mine]
    out_refs = refs[-2 - pieces : -2]
    owner_ref, sem = refs[-2:]
    head = pltpu.make_async_copy(owner_hbm, owner_ref, sem.at[0])
    head.start()
    head.wait()
    tokens = owner_ref.shape[1]
    owner = owner_ref[...]
    column = to_column(owner)
    above = lax.broadcasted_iota(jnp.int32, (tokens, tokens), 0)
    below = lax.broadcasted_iota(jnp.int32, (tokens, tokens), 1)
    earlier = jnp.where((column == owner) & (above < below), 1.0, 0.0)
    rank = jnp.sum(earlier, axis=0, keepdims=True).astype(jnp.int32)
    away = owner ^ lax.axis_index("frame")
    target = away * capacity + rank
    slots = owners_count * capacity
    places = lax.broadcasted_iota(jnp.int32, (slots, tokens), 0)
    placing = jnp.where(places == target, 1.0, 0.0).astype(BF16)
    total = part_refs[0][...].astype(F32)
    for ref in part_refs[1:]:
        total = total + ref[...].astype(F32)
    placed = lax.dot_general(
        placing, total.astype(BF16), (((1,), (1,)), ((), ())), preferred_element_type=F32
    ).astype(BF16)
    size = slots // pieces
    for index, ref in enumerate(out_refs):
        ref[...] = placed[index * size : (index + 1) * size, :]


def group_kernel(capacity, *refs):
    *part_refs, keep_ref, send_ref = refs
    for index, ref in enumerate(part_refs):
        cut = slice(index * capacity, (index + 1) * capacity)
        keep_ref[cut, :] = ref[:capacity, :]
        send_ref[cut, :] = ref[capacity:, :]


def slope(pre_act):
    normal_cdf = 0.5 * (1.0 + lax.erf(pre_act * 0.7071067811865476))
    density = jnp.exp(-0.5 * pre_act * pre_act) * 0.3989422804014327
    return normal_cdf + pre_act * density


def final_kernel(capacity, base, count, *refs):
    part_refs = refs[:count]
    pre_hbm = refs[count]
    out_hbm, pre, out, sems = refs[-4:]
    rows, slots = pre.shape
    cut = pl.ds(base, rows)
    load = pltpu.make_async_copy(pre_hbm.at[0, cut], pre, sems.at[0])
    load.start()
    joined = jnp.concatenate([ref[...] for ref in part_refs], axis=0)
    source = lax.broadcasted_iota(jnp.int32, (slots, slots), 0)
    goal = lax.broadcasted_iota(jnp.int32, (slots, slots), 1)
    origin = goal ^ (lax.axis_index("frame") * capacity)
    if count == 2:
        away = origin // capacity
        origin += ((away & 1) * (slots // capacity // 2) + (away >> 1) - away) * capacity
    moved = origin == source
    hidden = lax.dot_general(
        joined,
        jnp.where(moved, 1.0, 0.0).astype(BF16),
        (((0,), (0,)), ((), ())),
        preferred_element_type=F32,
    )
    load.wait()
    out[...] = (hidden * slope(pre[...].astype(F32))).astype(BF16)
    store = pltpu.make_async_copy(out, out_hbm.at[0, cut], sems.at[1])
    store.start()
    store.wait()


def chunk_rows(quarter):
    return [quarter // 2] * 2


def body(
    peers,
    owners_count,
    value_grad,
    w_value,
    norm_gain,
    vis_pos,
    frame_owner,
    ques_span,
    vis_proj,
    vis_resid,
    ques_hidden,
    w_down,
    pre_owned,
):
    _, tokens, width = vis_proj.shape
    shard_len, key_width = value_grad.shape[1:]
    length = ques_hidden.shape[1]
    features = peers * width
    slots = pre_owned.shape[2]
    capacity = slots // owners_count
    gain = norm_gain.reshape(1, width)
    owner = frame_owner.reshape(1, tokens)
    row = shape((8, tokens), F32)
    tall = shape((width, tokens), F32)
    dma = pltpu.SemaphoreType.DMA

    pieces = max(1, shard_len // 256)
    own = call(
        functools.partial(pick_kernel, pieces),
        shape((tokens, key_width), BF16),
        [HBM, HBM],
        [
            pltpu.VMEM((1, tokens), jnp.int32),
            pltpu.VMEM((shard_len, key_width), BF16),
            dma((pieces + 1,)),
        ],
        grant=PICK_GRANT,
    )(vis_pos, value_grad)
    own_all = [own] + [swap(own, "seq", peers, k) for k in range(1, peers)]

    stats, projt, residt, gaint, meant, weight = call(
        load_kernel,
        [row, tall, tall, tall, tall, shape(w_value.shape, BF16)],
        [HBM] * 6,
        [
            pltpu.SMEM((1, 2), jnp.int32),
            pltpu.VMEM((length, width), BF16),
            pltpu.VMEM((1, width), F32),
            pltpu.VMEM((tokens, width), BF16),
            pltpu.VMEM((tokens, width), BF16),
            dma((6,)),
        ],
        grant=LOAD_GRANT,
    )(ques_span, ques_hidden, gain, vis_proj, vis_resid, w_value)

    scaledt, sums = call(
        functools.partial(norm_kernel, peers),
        [tall, row],
        [VMEM] * (peers + 4),
        [pltpu.VMEM((key_width, tokens), BF16)],
    )(*own_all, stats, weight, gaint, projt)
    sums_all = [sums] + [swap(sums, "seq", peers, k) for k in range(1, peers)]

    chunks = chunk_rows(w_down.shape[0] // peers)
    bases = [sum(chunks[:i]) for i in range(len(chunks))]
    chain = Chain()

    def weights_scratch(rows):
        copies = peers * (rows // min(rows, 256))
        return [pltpu.VMEM((peers * rows, width), BF16), dma((copies,))]

    def reduce(partial):
        return [partial[0]] + [swap(partial[k], "seq", peers, k) for k in range(1, peers)]

    def down(index):
        rows = chunks[index]
        return chain.call(
            functools.partial(down_kernel, peers, bases[index], rows),
            [shape((rows, tokens), BF16)] * peers,
            [HBM, VMEM],
            weights_scratch(rows),
        )(w_down, gradt)

    paired = capacity % 16 == 0 and owners_count % 2 == 0
    pairs = owners_count // 2
    pieces = pairs if paired else 1

    def place(parts):
        rows = parts[0].shape[0]
        placed = chain.call(
            functools.partial(place_kernel, capacity, owners_count, pieces, len(parts)),
            [shape((slots // pieces, rows), BF16)] * pieces,
            [HBM] + [VMEM] * len(parts),
            [pltpu.VMEM((1, tokens), jnp.int32), dma((1,))],
        )(owner, *parts)
        if paired:
            return [placed[0]] + [
                swap(placed[k], "frame", owners_count, 2 * k) for k in range(1, pairs)
            ]
        order = jnp.arange(owners_count) ^ lax.axis_index("frame")
        split = placed[0].reshape(owners_count, capacity, rows)[order]
        split = lax.all_to_all(split, "frame", split_axis=0, concat_axis=0, tiled=True)
        return [split[order].reshape(slots, rows)]

    def group(parts):
        if not paired:
            return parts
        keep, send = chain.call(
            functools.partial(group_kernel, capacity),
            [shape((slots // 2, parts[0].shape[1]), BF16)] * 2,
            [VMEM] * pairs,
        )(*parts)
        return [keep, swap(send, "frame", owners_count, 1)]

    def finish(parts, index, held):
        rows = chunks[index]
        return chain.call(
            functools.partial(final_kernel, capacity, bases[index], len(parts)),
            [shape(pre_owned.shape, BF16)],
            [VMEM] * len(parts) + [HBM] + [HBM] * len(held),
            [
                pltpu.VMEM((rows, slots), BF16),
                pltpu.VMEM((rows, slots), BF16),
                dma((2,)),
            ],
            {len(parts) + 1: 0} if held else None,
            [HBM],
        )(*parts, pre_owned, *held)

    gradt, logit, *partial = chain.call(
        functools.partial(gate_kernel, features, peers, 0, chunks[0]),
        [shape((width, tokens), BF16), row] + [shape((chunks[0], tokens), BF16)] * peers,
        [VMEM] * (peers + 4) + [HBM],
        weights_scratch(chunks[0]),
    )(*sums_all, projt, residt, scaledt, meant, w_down)
    waiting = [reduce(partial), reduce(down(1))]
    placed = place(waiting[0])
    (ques_grad,) = chain.call(
        ques_kernel,
        [shape(ques_hidden.shape, BF16)],
        [HBM, VMEM, HBM],
        [pltpu.SMEM((1, 2), jnp.int32), pltpu.VMEM((tokens, width), BF16), dma((2,))],
    )(ques_span, logit, vis_proj)
    held = []
    for index in range(len(chunks)):
        parts = group(placed)
        if index + 1 < len(chunks):
            placed = place(waiting[index + 1])
            if index + 2 < len(chunks):
                waiting.append(reduce(down(index + 2)))
        held = finish(parts, index, held)
    return (held[0], ques_grad)


def solution(mesh):
    in_specs = (
        P("frame", "seq", None),
        P("seq", None),
        P("seq"),
        P("frame", None),
        P("frame", None, None),
        P("frame", None),
        P("frame", None, "seq"),
        P("frame", None, "seq"),
        P("frame", None, "seq"),
        P(None, "seq"),
        P("frame", "seq", None),
    )
    out_specs = (P("frame", "seq", None), P("frame", None, "seq"))
    run = functools.partial(body, mesh.shape["seq"], mesh.shape["frame"])
    return jax.shard_map(run, mesh=mesh, in_specs=in_specs, out_specs=out_specs, check_vma=False)
```

```python
import functools
import math

import jax
import jax.numpy as jnp
from jax import lax
from jax.experimental import pallas as pl
from jax.experimental.pallas import tpu as pltpu
from jax.sharding import PartitionSpec as P

EPSILON = 1e-06
F32 = jnp.float32
BF16 = jnp.bfloat16
LANES = 128
MIB = 1024 * 1024
GRANT, LOAD_GRANT, PICK_GRANT = 40, 40, 63
HBM = pl.BlockSpec(memory_space=pltpu.HBM)
VMEM = pl.BlockSpec(memory_space=pltpu.VMEM)
ANY = pl.BlockSpec(memory_space=pl.ANY)


def call(
    kernel, out_shape, in_specs, scratch=(), aliases=None, out_specs=None, grant=GRANT, cost=1024
):
    return pl.pallas_call(
        kernel,
        out_shape=out_shape,
        in_specs=in_specs,
        out_specs=jax.tree.map(lambda _: VMEM, out_shape) if out_specs is None else out_specs,
        scratch_shapes=list(scratch),
        input_output_aliases=aliases or {},
        compiler_params=pltpu.CompilerParams(vmem_limit_bytes=grant * MIB),
        cost_estimate=pl.CostEstimate(flops=256 * cost, bytes_accessed=cost, transcendentals=0),
    )


class Chain:
    def __init__(self):
        self.last = []

    def call(
        self, kernel, out_shape, in_specs, scratch=(), aliases=None, out_specs=None, cost=1024
    ):
        given, made, linked = len(in_specs), len(out_shape), len(self.last)

        def run(*refs):
            outs = refs[given + linked :]
            outs[made][...] = jnp.zeros(outs[made].shape, F32)
            kernel(*refs[:given], *outs[:made], *outs[made + 1 :])

        out_specs = [VMEM] * made if out_specs is None else out_specs
        run_call = call(
            run,
            [*out_shape, shape((8, LANES), F32)],
            [*in_specs, *[VMEM] * linked],
            scratch,
            aliases,
            [*out_specs, VMEM],
            cost=cost,
        )

        def apply(*args):
            *results, token = run_call(*args, *self.last)
            self.last = [token]
            return results

        return apply


def shape(dims, dtype):
    return jax.ShapeDtypeStruct(dims, dtype)


def swap(value, axis, count, step):
    return lax.ppermute(value, axis, [(i, i ^ step) for i in range(count)])


def to_column(row):
    return jnp.transpose(jnp.broadcast_to(row, (LANES, row.shape[1])), (1, 0))


def pick_kernel(pieces, pos_hbm, rows_hbm, own_ref, pos, rows, sems):
    tokens, shard_len = pos.shape[1], rows.shape[0]
    size = shard_len // pieces
    head = pltpu.make_async_copy(pos_hbm, pos, sems.at[pieces])
    head.start()
    copies = []
    for piece in range(pieces):
        cut = pl.ds(piece * size, size)
        copies.append(
            pltpu.make_async_copy(rows_hbm.at[0, cut], rows.at[cut], sems.at[piece])
        )
        copies[-1].start()
    offset = lax.axis_index("seq") * shard_len
    head.wait()
    column = to_column(pos[...] - offset)
    lanes = lax.broadcasted_iota(jnp.int32, (tokens, LANES), 1)
    total = None
    for piece in range(pieces):
        select = jnp.concatenate(
            [
                jnp.where(column == lanes + at, 1.0, 0.0).astype(BF16)
                for at in range(piece * size, (piece + 1) * size, LANES)
            ],
            axis=1,
        )
        copies[piece].wait()
        part = jnp.dot(
            select, rows[piece * size : (piece + 1) * size, :], preferred_element_type=F32
        )
        total = part if total is None else total + part
    own_ref[...] = total.astype(BF16)


def load_kernel(
    span_hbm, hidden_hbm, gain_hbm, proj_hbm, resid_hbm, weight_hbm,
    stats_ref, projt_ref, residt_ref, gaint_ref, meant_ref, weight_ref,
    span, hidden, gain, proj, resid, sems,
):
    copies = [
        pltpu.make_async_copy(source, target, sems.at[index])
        for index, (source, target) in enumerate(
            [
                (span_hbm, span),
                (hidden_hbm.at[0], hidden),
                (gain_hbm, gain),
                (proj_hbm.at[0], proj),
                (resid_hbm.at[0], resid),
                (weight_hbm, weight_ref),
            ]
        )
    ]
    for copy in copies:
        copy.start()
    for copy in copies[:5]:
        copy.wait()
    start, count = span[0, 0], span[0, 1]
    tokens, width = proj.shape
    places = lax.broadcasted_iota(jnp.int32, (hidden.shape[0], 1), 0)
    mask = ((places >= start) & (places < start + count)).astype(F32)
    query = square = cross = jnp.zeros((LANES, tokens), F32)
    for at in range(0, width, LANES):
        cut = slice(at, at + LANES)
        mean = jnp.sum(hidden[:, cut].astype(F32) * mask, axis=0, keepdims=True)
        meant = to_column(mean / count.astype(F32))
        projt = jnp.transpose(proj[:, cut].astype(F32), (1, 0))
        residt = jnp.transpose(resid[:, cut].astype(F32), (1, 0))
        meant_ref[cut, :] = meant
        projt_ref[cut, :] = projt
        residt_ref[cut, :] = residt
        gaint_ref[cut, :] = to_column(gain[:, cut])
        query = query + projt * meant
        square = square + projt * projt
        cross = cross + projt * residt
    stats_ref[...] = jnp.zeros(stats_ref.shape, F32)
    for row, value in enumerate((query, square, cross)):
        stats_ref[row : row + 1, :] = jnp.sum(value, axis=0, keepdims=True)
    copies[5].wait()


def norm_kernel(peers, *refs):
    own_refs = refs[:peers]
    stats_ref, weight_ref, gaint_ref, projt_ref, scaledt_ref, sums_ref, pickedt = refs[peers:]
    key_width = own_refs[0].shape[1]
    for at in range(0, key_width, LANES):
        cut = slice(at, at + LANES)
        picked = own_refs[0][:, cut].astype(F32)
        for ref in own_refs[1:]:
            picked = picked + ref[:, cut].astype(F32)
        pickedt[cut, :] = jnp.transpose(picked, (1, 0)).astype(BF16)
    width, tokens = projt_ref.shape
    total = jnp.zeros((LANES, tokens), F32)
    for at in range(0, width, 256):
        cut = slice(at, at + 256)
        normed = jnp.dot(weight_ref[cut, :], pickedt[...], preferred_element_type=F32)
        scaled = normed * gaint_ref[cut, :]
        scaledt_ref[cut, :] = scaled
        terms = scaled * projt_ref[cut, :]
        total = total + terms[:LANES] + terms[LANES:]
    sums_ref[...] = stats_ref[...]
    sums_ref[3:4, :] = jnp.sum(total, axis=0, keepdims=True)


def start_weights(weight_hbm, weights, sems, peers, share, base, rows):
    quarter = weight_hbm.shape[0] // peers
    block = min(rows, 256)
    part = lax.rem(lax.axis_index("frame"), share) * (quarter // share)
    copies = []
    for peer in range(peers):
        first = (lax.axis_index("seq") ^ peer) * quarter + part + base
        for at in range(0, rows, block):
            index = len(copies)
            copies.append(
                pltpu.make_async_copy(
                    weight_hbm.at[pl.ds(pl.multiple_of(first + at, block), block)],
                    weights.at[pl.ds(peer * rows + at, block)],
                    sems.at[index],
                )
            )
            copies[-1].start()
    return copies


def preload_kernel(peers, share, rows, weight_hbm, after_ref, weights_ref, sems):
    del after_ref
    for copy in start_weights(weight_hbm, weights_ref, sems, peers, share, 0, rows):
        copy.wait()


def gate_kernel(features, peers, *refs):
    sums_refs = refs[:peers]
    projt_ref, residt_ref, scaledt_ref, meant_ref, owner_ref, after_ref = refs[peers : peers + 6]
    del after_ref
    gradt_ref, logit_ref = refs[peers + 6 :]
    sums = sums_refs[0][...]
    for ref in sums_refs[1:]:
        sums = sums + ref[...]
    sum_query, sum_square, sum_resid, sum_norm = (sums[i : i + 1] for i in range(4))
    gate_scale = 4.0 / math.sqrt(features)
    gate = jax.nn.sigmoid(gate_scale * sum_query)
    inv_rms = lax.rsqrt(gate * gate * sum_square / features + EPSILON)
    coef = gate * inv_rms * inv_rms * inv_rms * (gate * sum_norm) / features
    gate_grad = sum_resid + inv_rms * sum_norm - coef * sum_square
    logit = gate_grad * gate * (1.0 - gate) * gate_scale
    logit_ref[...] = jnp.broadcast_to(logit, logit_ref.shape)
    width = projt_ref.shape[0]
    for at in range(0, width, LANES):
        cut = slice(at, at + LANES)
        grad = residt_ref[cut, :] + inv_rms * scaledt_ref[cut, :] - coef * projt_ref[cut, :]
        gradt_ref[cut, :] = (gate * grad + logit * meant_ref[cut, :]).astype(BF16)
    tail = gradt_ref.shape[0] - width
    owner = owner_ref[...].astype(F32)
    gradt_ref[width:, :] = jnp.broadcast_to(owner, (tail, owner.shape[1])).astype(BF16)


def down_kernel(peers, share, base, rows, held, *refs):
    weight_ref = refs[0]
    gradt_refs = refs[1 : 1 + share]
    out_refs = refs[1 + share : 1 + share + peers]
    scratch = list(refs[1 + share + peers :])
    joined = scratch.pop(0)
    copies = None
    if held:
        weights = weight_ref
    else:
        weights, sems = scratch
        copies = start_weights(weight_ref, weights, sems, peers, share, base, rows)
    width, tokens = joined.shape[0], gradt_refs[0].shape[1]
    for index, ref in enumerate(gradt_refs):
        joined[:, index * tokens : (index + 1) * tokens] = ref[:width, :]
    block = min(rows, 256)
    inner = rows // block
    for index in range(peers * inner):
        peer, part = index // inner, index % inner
        if copies is not None:
            copies[index].wait()
        value = jnp.dot(
            weights[index * block : (index + 1) * block, :],
            joined[...],
            preferred_element_type=F32,
        )
        out_refs[peer][part * block : (part + 1) * block, :] = value.astype(BF16)


def ques_kernel(span_hbm, logit_ref, proj_hbm, out_ref, span, proj, sems):
    head = pltpu.make_async_copy(span_hbm, span, sems.at[0])
    load = pltpu.make_async_copy(proj_hbm.at[0], proj, sems.at[1])
    head.start()
    load.start()
    head.wait()
    start, count = span[0, 0], span[0, 1]
    length, width = out_ref.shape[1], out_ref.shape[2]
    places = lax.broadcasted_iota(jnp.int32, (length, LANES), 0)
    mask = ((places >= start) & (places < start + count)).astype(F32)
    column = to_column(logit_ref[0:1, :])
    load.wait()
    for at in range(0, width, LANES):
        cut = slice(at, at + LANES)
        total = jnp.sum(column * proj[:, cut].astype(F32), axis=0, keepdims=True)
        out_ref[0, :, cut] = (mask * total / count.astype(F32)).astype(BF16)


def targets(owner, capacity, share, source):
    tokens = owner.shape[1]
    above = lax.broadcasted_iota(jnp.int32, (tokens, tokens), 0)
    below = lax.broadcasted_iota(jnp.int32, (tokens, tokens), 1)
    earlier = jnp.where((to_column(owner) == owner) & (above < below), 1.0, 0.0)
    rank = jnp.sum(earlier, axis=0, keepdims=True).astype(jnp.int32)
    away = owner ^ lax.axis_index("frame")
    return (away * share + source) * capacity + rank


def place_kernel(capacity, share, pieces, mine, *refs):
    gradt_refs = refs[:share]
    part_refs = refs[share : share + mine]
    out_refs = refs[-pieces:]
    target = jnp.concatenate(
        [
            targets(ref[-16:-15, :].astype(F32).astype(jnp.int32), capacity, share, source)
            for source, ref in enumerate(gradt_refs)
        ],
        axis=1,
    )
    size = out_refs[0].shape[0]
    places = lax.broadcasted_iota(jnp.int32, (size * pieces, target.shape[1]), 0)
    placing = jnp.where(places == target, 1.0, 0.0).astype(BF16)
    total = part_refs[0][...].astype(F32)
    for ref in part_refs[1:]:
        total = total + ref[...].astype(F32)
    placed = lax.dot_general(
        placing, total.astype(BF16), (((1,), (1,)), ((), ())), preferred_element_type=F32
    ).astype(BF16)
    for index, ref in enumerate(out_refs):
        ref[...] = placed[index * size : (index + 1) * size, :]


def group_kernel(*refs):
    *part_refs, keep_ref, send_ref = refs
    size = part_refs[0].shape[0] // 2
    for index, ref in enumerate(part_refs):
        cut = slice(index * size, (index + 1) * size)
        keep_ref[cut, :] = ref[:size, :]
        send_ref[cut, :] = ref[size:, :]


def slope(pre_act):
    normal_cdf = 0.5 * (1.0 + lax.erf(pre_act * 0.7071067811865476))
    density = jnp.exp(-0.5 * pre_act * pre_act) * 0.3989422804014327
    return normal_cdf + pre_act * density


def final_kernel(capacity, share, turn, base, *refs):
    part_ref, pre_hbm = refs[:2]
    out_hbm, pre, out, sems = refs[-4:]
    rows, slots = pre.shape
    part = lax.rem(lax.axis_index("frame") + turn, share) * (pre_hbm.shape[1] // share)
    cut = pl.ds(pl.multiple_of(part + base, rows), rows)
    load = pltpu.make_async_copy(pre_hbm.at[0, cut], pre, sems.at[0])
    load.start()
    source = lax.broadcasted_iota(jnp.int32, (slots, slots), 0)
    goal = lax.broadcasted_iota(jnp.int32, (slots, slots), 1)
    moved = (goal ^ ((lax.axis_index("frame") ^ turn) * capacity)) == source
    hidden = lax.dot_general(
        part_ref[...],
        jnp.where(moved, 1.0, 0.0).astype(BF16),
        (((0,), (0,)), ((), ())),
        preferred_element_type=F32,
    )
    load.wait()
    out[...] = (hidden * slope(pre[...].astype(F32))).astype(BF16)
    store = pltpu.make_async_copy(out, out_hbm.at[0, cut], sems.at[1])
    store.start()
    store.wait()


def chunk_rows(quarter):
    return [quarter // 2] * 2


def body(
    peers,
    owners_count,
    value_grad,
    w_value,
    norm_gain,
    vis_pos,
    frame_owner,
    ques_span,
    vis_proj,
    vis_resid,
    ques_hidden,
    w_down,
    pre_owned,
):
    _, tokens, width = vis_proj.shape
    shard_len, key_width = value_grad.shape[1:]
    length = ques_hidden.shape[1]
    features = peers * width
    slots = pre_owned.shape[2]
    capacity = slots // owners_count
    gain = norm_gain.reshape(1, width)
    owner = frame_owner.reshape(1, tokens)
    row = shape((8, tokens), F32)
    tall = shape((width, tokens), F32)
    dma = pltpu.SemaphoreType.DMA

    pieces = max(1, shard_len // 256)
    own = call(
        functools.partial(pick_kernel, pieces),
        shape((tokens, key_width), BF16),
        [HBM, HBM],
        [
            pltpu.VMEM((1, tokens), jnp.int32),
            pltpu.VMEM((shard_len, key_width), BF16),
            dma((pieces + 1,)),
        ],
        grant=PICK_GRANT,
    )(vis_pos, value_grad)
    own_all = [own] + [swap(own, "seq", peers, k) for k in range(1, peers)]

    stats, projt, residt, gaint, meant, weight = call(
        load_kernel,
        [row, tall, tall, tall, tall, shape(w_value.shape, BF16)],
        [HBM] * 6,
        [
            pltpu.SMEM((1, 2), jnp.int32),
            pltpu.VMEM((length, width), BF16),
            pltpu.VMEM((1, width), F32),
            pltpu.VMEM((tokens, width), BF16),
            pltpu.VMEM((tokens, width), BF16),
            dma((6,)),
        ],
        grant=LOAD_GRANT,
    )(ques_span, ques_hidden, gain, vis_proj, vis_resid, w_value)

    scaledt, sums = call(
        functools.partial(norm_kernel, peers),
        [tall, row],
        [VMEM] * (peers + 4),
        [pltpu.VMEM((key_width, tokens), BF16)],
    )(*own_all, stats, weight, gaint, projt)
    sums_all = [sums] + [swap(sums, "seq", peers, k) for k in range(1, peers)]

    paired = capacity % 16 == 0 and owners_count % 2 == 0
    share = 2 if paired else 1
    pieces = owners_count // 2 if paired else 1
    chunks = chunk_rows(w_down.shape[0] // peers // share)
    bases = [sum(chunks[:i]) for i in range(len(chunks))]
    chain = Chain()

    def sems(rows):
        return dma((peers * (rows // min(rows, 256)),))

    preloaded = call(
        functools.partial(preload_kernel, peers, share, chunks[0]),
        shape((peers * chunks[0], width), BF16),
        [HBM, VMEM],
        [sems(chunks[0])],
    )(w_down, sums)

    gradt, logit = chain.call(
        functools.partial(gate_kernel, features, peers),
        [shape((width + 16, tokens), BF16), row],
        [VMEM] * (peers + 5) + [ANY],
    )(*sums_all, projt, residt, scaledt, meant, owner, preloaded)
    gradts = [gradt] + [swap(gradt, "frame", owners_count, k) for k in range(1, share)]

    def down(index):
        rows = chunks[index]
        weights = [pltpu.VMEM((peers * rows, width), BF16), sems(rows)]
        partial = chain.call(
            functools.partial(down_kernel, peers, share, bases[index], rows, index == 0),
            [shape((rows, share * tokens), BF16)] * peers,
            [VMEM if index == 0 else HBM] + [VMEM] * share,
            [pltpu.VMEM((width, share * tokens), BF16)] + (weights if index else []),
            cost=2 * peers * rows * width,
        )(w_down if index else preloaded, *gradts)
        return [partial[0]] + [swap(partial[k], "seq", peers, k) for k in range(1, peers)]

    def place(parts):
        rows = parts[0].shape[0]
        placed = chain.call(
            functools.partial(place_kernel, capacity, share, pieces, len(parts)),
            [shape((slots * share // pieces, rows), BF16)] * pieces,
            [VMEM] * (share + len(parts)),
        )(*gradts, *parts)
        if paired:
            return [placed[0]] + [
                swap(placed[k], "frame", owners_count, 2 * k) for k in range(1, pieces)
            ]
        order = jnp.arange(owners_count) ^ lax.axis_index("frame")
        split = placed[0].reshape(owners_count, capacity, rows)[order]
        split = lax.all_to_all(split, "frame", split_axis=0, concat_axis=0, tiled=True)
        return [split[order].reshape(slots, rows)]

    def group(parts):
        if not paired:
            return parts
        keep, send = chain.call(
            group_kernel,
            [shape((slots, parts[0].shape[1]), BF16)] * 2,
            [VMEM] * pieces,
        )(*parts)
        return [keep, swap(send, "frame", owners_count, 1)]

    def finish(parts, index, held):
        rows = chunks[index]
        for turn, part in enumerate(parts):
            held = chain.call(
                functools.partial(final_kernel, capacity, share, turn, bases[index]),
                [shape(pre_owned.shape, BF16)],
                [VMEM, HBM] + [HBM] * len(held),
                [pltpu.VMEM((rows, slots), BF16), pltpu.VMEM((rows, slots), BF16), dma((2,))],
                {2: 0} if held else None,
                [HBM],
            )(part, pre_owned, *held)
        return held

    waiting = [down(0), down(1)]
    placed = place(waiting[0])
    (ques_grad,) = chain.call(
        ques_kernel,
        [shape(ques_hidden.shape, BF16)],
        [HBM, VMEM, HBM],
        [pltpu.SMEM((1, 2), jnp.int32), pltpu.VMEM((tokens, width), BF16), dma((2,))],
    )(ques_span, logit, vis_proj)
    held = []
    for index in range(len(chunks)):
        parts = group(placed)
        if index + 1 < len(chunks):
            placed = place(waiting[index + 1])
            if index + 2 < len(chunks):
                waiting.append(down(index + 2))
        held = finish(parts, index, held)
    return (held[0], ques_grad)


def solution(mesh):
    in_specs = (
        P("frame", "seq", None),
        P("seq", None),
        P("seq"),
        P("frame", None),
        P("frame", None, None),
        P("frame", None),
        P("frame", None, "seq"),
        P("frame", None, "seq"),
        P("frame", None, "seq"),
        P(None, "seq"),
        P("frame", "seq", None),
    )
    out_specs = (P("frame", "seq", None), P("frame", None, "seq"))
    run = functools.partial(body, mesh.shape["seq"], mesh.shape["frame"])
    return jax.shard_map(run, mesh=mesh, in_specs=in_specs, out_specs=out_specs, check_vma=False)
```

```python
import functools
import math

import jax
import jax.numpy as jnp
from jax import lax
from jax.experimental import pallas as pl
from jax.experimental.pallas import tpu as pltpu
from jax.sharding import PartitionSpec as P

EPSILON = 1e-06
F32 = jnp.float32
BF16 = jnp.bfloat16
LANES = 128
AHEAD = 3
MIB = 1024 * 1024
GRANT, LOAD_GRANT, PICK_GRANT = 40, 46, 54
HBM = pl.BlockSpec(memory_space=pltpu.HBM)
VMEM = pl.BlockSpec(memory_space=pltpu.VMEM)
ANY = pl.BlockSpec(memory_space=pl.ANY)


def call(
    kernel, out_shape, in_specs, scratch=(), aliases=None, out_specs=None, grant=GRANT, cost=1024
):
    return pl.pallas_call(
        kernel,
        out_shape=out_shape,
        in_specs=in_specs,
        out_specs=jax.tree.map(lambda _: VMEM, out_shape) if out_specs is None else out_specs,
        scratch_shapes=list(scratch),
        input_output_aliases=aliases or {},
        compiler_params=pltpu.CompilerParams(vmem_limit_bytes=grant * MIB),
        cost_estimate=pl.CostEstimate(flops=256 * cost, bytes_accessed=cost, transcendentals=0),
    )


class Chain:
    def __init__(self):
        self.last = []

    def call(
        self, kernel, out_shape, in_specs, scratch=(), aliases=None, out_specs=None, cost=1024
    ):
        given, made, linked = len(in_specs), len(out_shape), len(self.last)

        def run(*refs):
            outs = refs[given + linked :]
            outs[made][...] = jnp.zeros(outs[made].shape, F32)
            kernel(*refs[:given], *outs[:made], *outs[made + 1 :])

        out_specs = [VMEM] * made if out_specs is None else out_specs
        run_call = call(
            run,
            [*out_shape, shape((8, LANES), F32)],
            [*in_specs, *[VMEM] * linked],
            scratch,
            aliases,
            [*out_specs, VMEM],
            cost=cost,
        )

        def apply(*args):
            *results, token = run_call(*args, *self.last)
            self.last = [token]
            return results

        return apply


def shape(dims, dtype):
    return jax.ShapeDtypeStruct(dims, dtype)


def swap(value, axis, count, step):
    return lax.ppermute(value, axis, [(i, i ^ step) for i in range(count)])


def far_first(count):
    return [0, *reversed(range(1, count))]


def swaps(values, axis, count, stride=1):
    return [
        swap(value, axis, count, step * stride) if step else value
        for value, step in zip(values, far_first(len(values)))
    ]


def to_column(row):
    return jnp.transpose(jnp.broadcast_to(row, (LANES, row.shape[1])), (1, 0))


def pick_kernel(pieces, pos_hbm, rows_hbm, own_ref, pos, rows, sems):
    tokens, shard_len = pos.shape[1], rows.shape[0]
    size = shard_len // pieces
    head = pltpu.make_async_copy(pos_hbm, pos, sems.at[pieces])
    head.start()
    copies = []
    for piece in range(pieces):
        cut = pl.ds(piece * size, size)
        copies.append(
            pltpu.make_async_copy(rows_hbm.at[0, cut], rows.at[cut], sems.at[piece])
        )
        copies[-1].start()
    offset = lax.axis_index("seq") * shard_len
    head.wait()
    column = to_column(pos[...] - offset)
    lanes = lax.broadcasted_iota(jnp.int32, (tokens, LANES), 1)
    total = None
    for piece in range(pieces):
        select = jnp.concatenate(
            [
                jnp.where(column == lanes + at, 1.0, 0.0).astype(BF16)
                for at in range(piece * size, (piece + 1) * size, LANES)
            ],
            axis=1,
        )
        copies[piece].wait()
        part = jnp.dot(
            select, rows[piece * size : (piece + 1) * size, :], preferred_element_type=F32
        )
        total = part if total is None else total + part
    own_ref[...] = total.astype(BF16)


def load_kernel(
    span_hbm, hidden_hbm, gain_hbm, proj_hbm, resid_hbm, weight_hbm,
    stats_ref, projt_ref, residt_ref, gaint_ref, meant_ref, weight_ref,
    span, hidden, gain, proj, resid, sems,
):
    copies = [
        pltpu.make_async_copy(source, target, sems.at[index])
        for index, (source, target) in enumerate(
            [
                (span_hbm, span),
                (hidden_hbm.at[0], hidden),
                (gain_hbm, gain),
                (proj_hbm.at[0], proj),
                (resid_hbm.at[0], resid),
                (weight_hbm, weight_ref),
            ]
        )
    ]
    for copy in copies:
        copy.start()
    for copy in copies[:5]:
        copy.wait()
    start, count = span[0, 0], span[0, 1]
    tokens, width = proj.shape
    places = lax.broadcasted_iota(jnp.int32, (hidden.shape[0], 1), 0)
    mask = ((places >= start) & (places < start + count)).astype(F32)
    query = square = cross = jnp.zeros((LANES, tokens), F32)
    for at in range(0, width, LANES):
        cut = slice(at, at + LANES)
        mean = jnp.sum(hidden[:, cut].astype(F32) * mask, axis=0, keepdims=True)
        meant = to_column(mean / count.astype(F32))
        projt = jnp.transpose(proj[:, cut].astype(F32), (1, 0))
        residt = jnp.transpose(resid[:, cut].astype(F32), (1, 0))
        meant_ref[cut, :] = meant
        projt_ref[cut, :] = projt
        residt_ref[cut, :] = residt
        gaint_ref[cut, :] = to_column(gain[:, cut])
        query = query + projt * meant
        square = square + projt * projt
        cross = cross + projt * residt
    stats_ref[...] = jnp.zeros(stats_ref.shape, F32)
    for row, value in enumerate((query, square, cross)):
        stats_ref[row : row + 1, :] = jnp.sum(value, axis=0, keepdims=True)
    copies[5].wait()


def norm_kernel(peers, *refs):
    own_refs = refs[:peers]
    stats_ref, weight_ref, gaint_ref, projt_ref, scaledt_ref, sums_ref, pickedt = refs[peers:]
    key_width = own_refs[0].shape[1]
    for at in range(0, key_width, LANES):
        cut = slice(at, at + LANES)
        picked = own_refs[0][:, cut].astype(F32)
        for ref in own_refs[1:]:
            picked = picked + ref[:, cut].astype(F32)
        pickedt[cut, :] = jnp.transpose(picked, (1, 0)).astype(BF16)
    width, tokens = projt_ref.shape
    total = jnp.zeros((LANES, tokens), F32)
    for at in range(0, width, 256):
        cut = slice(at, at + 256)
        normed = jnp.dot(weight_ref[cut, :], pickedt[...], preferred_element_type=F32)
        scaled = normed * gaint_ref[cut, :]
        scaledt_ref[cut, :] = scaled
        terms = scaled * projt_ref[cut, :]
        total = total + terms[:LANES] + terms[LANES:]
    sums_ref[...] = stats_ref[...]
    sums_ref[3:4, :] = jnp.sum(total, axis=0, keepdims=True)


def weight_copies(weight_hbm, weights, sems, peers, share, base, rows):
    quarter = weight_hbm.shape[0] // peers
    block = min(rows, 256)
    part = lax.rem(lax.axis_index("frame"), share) * (quarter // share)
    copies = []
    for peer, step in enumerate(far_first(peers)):
        first = (lax.axis_index("seq") ^ step) * quarter + part + base
        for at in range(0, rows, block):
            index = len(copies)
            copies.append(
                pltpu.make_async_copy(
                    weight_hbm.at[pl.ds(pl.multiple_of(first + at, block), block)],
                    weights.at[pl.ds(peer * rows + at, block)],
                    sems.at[index],
                )
            )
    return copies


def preload_kernel(peers, share, rows, weight_hbm, after_ref, weights_ref, sems):
    del after_ref
    copies = weight_copies(weight_hbm, weights_ref, sems, peers, share, 0, rows)
    for copy in copies:
        copy.start()
    for copy in copies:
        copy.wait()


def gate_kernel(features, peers, *refs):
    sums_refs = refs[:peers]
    projt_ref, residt_ref, scaledt_ref, meant_ref, owner_ref, after_ref = refs[peers : peers + 6]
    del after_ref
    gradt_ref, logit_ref = refs[peers + 6 :]
    sums = sums_refs[0][...]
    for ref in sums_refs[1:]:
        sums = sums + ref[...]
    sum_query, sum_square, sum_resid, sum_norm = (sums[i : i + 1] for i in range(4))
    gate_scale = 4.0 / math.sqrt(features)
    gate = jax.nn.sigmoid(gate_scale * sum_query)
    inv_rms = lax.rsqrt(gate * gate * sum_square / features + EPSILON)
    coef = gate * inv_rms * inv_rms * inv_rms * (gate * sum_norm) / features
    gate_grad = sum_resid + inv_rms * sum_norm - coef * sum_square
    logit = gate_grad * gate * (1.0 - gate) * gate_scale
    logit_ref[...] = jnp.broadcast_to(logit, logit_ref.shape)
    width = projt_ref.shape[0]
    for at in range(0, width, LANES):
        cut = slice(at, at + LANES)
        grad = residt_ref[cut, :] + inv_rms * scaledt_ref[cut, :] - coef * projt_ref[cut, :]
        gradt_ref[cut, :] = (gate * grad + logit * meant_ref[cut, :]).astype(BF16)
    tail = gradt_ref.shape[0] - width
    owner = owner_ref[...].astype(F32)
    gradt_ref[width:, :] = jnp.broadcast_to(owner, (tail, owner.shape[1])).astype(BF16)


def down_kernel(peers, share, base, rows, held, *refs):
    weight_ref = refs[0]
    gradt_refs = refs[1 : 1 + share]
    out_refs = refs[1 + share : 1 + share + peers]
    scratch = list(refs[1 + share + peers :])
    joined = scratch.pop(0)
    copies = []
    if held:
        weights = weight_ref
    else:
        weights, sems = scratch
        copies = weight_copies(weight_ref, weights, sems, peers, share, base, rows)
    for copy in copies[:AHEAD]:
        copy.start()
    width, tokens = joined.shape[0], gradt_refs[0].shape[1]
    for index, ref in enumerate(gradt_refs):
        joined[:, index * tokens : (index + 1) * tokens] = ref[:width, :]
    block = min(rows, 256)
    inner = rows // block
    for index in range(peers * inner):
        peer, part = index // inner, index % inner
        if copies:
            copies[index].wait()
        if index + AHEAD < len(copies):
            copies[index + AHEAD].start()
        value = jnp.dot(
            weights[index * block : (index + 1) * block, :],
            joined[...],
            preferred_element_type=F32,
        )
        out_refs[peer][part * block : (part + 1) * block, :] = value.astype(BF16)


def ques_kernel(span_hbm, logit_ref, proj_hbm, out_ref, span, proj, sems):
    head = pltpu.make_async_copy(span_hbm, span, sems.at[0])
    load = pltpu.make_async_copy(proj_hbm.at[0], proj, sems.at[1])
    head.start()
    load.start()
    head.wait()
    start, count = span[0, 0], span[0, 1]
    length, width = out_ref.shape[1], out_ref.shape[2]
    places = lax.broadcasted_iota(jnp.int32, (length, LANES), 0)
    mask = ((places >= start) & (places < start + count)).astype(F32)
    column = to_column(logit_ref[0:1, :])
    load.wait()
    for at in range(0, width, LANES):
        cut = slice(at, at + LANES)
        total = jnp.sum(column * proj[:, cut].astype(F32), axis=0, keepdims=True)
        out_ref[0, :, cut] = (mask * total / count.astype(F32)).astype(BF16)


def targets(owner, capacity, share, source):
    tokens = owner.shape[1]
    above = lax.broadcasted_iota(jnp.int32, (tokens, tokens), 0)
    below = lax.broadcasted_iota(jnp.int32, (tokens, tokens), 1)
    earlier = jnp.where((to_column(owner) == owner) & (above < below), 1.0, 0.0)
    rank = jnp.sum(earlier, axis=0, keepdims=True).astype(jnp.int32)
    away = owner ^ lax.axis_index("frame")
    return (away * share + source) * capacity + rank


def place_kernel(capacity, share, pieces, mine, *refs):
    gradt_refs = refs[:share]
    part_refs = refs[share : share + mine]
    out_refs = refs[-pieces:]
    target = jnp.concatenate(
        [
            targets(ref[-16:-15, :].astype(F32).astype(jnp.int32), capacity, share, source)
            for source, ref in enumerate(gradt_refs)
        ],
        axis=1,
    )
    size = out_refs[0].shape[0]
    places = lax.broadcasted_iota(jnp.int32, (size * pieces, target.shape[1]), 0)
    placing = jnp.where(places == target, 1.0, 0.0).astype(BF16)
    total = part_refs[0][...].astype(F32)
    for ref in part_refs[1:]:
        total = total + ref[...].astype(F32)
    placed = lax.dot_general(
        placing, total.astype(BF16), (((1,), (1,)), ((), ())), preferred_element_type=F32
    ).astype(BF16)
    for ref, step in zip(out_refs, far_first(pieces)):
        ref[...] = placed[step * size : (step + 1) * size, :]


def group_kernel(*refs):
    *part_refs, keep_ref, send_ref = refs
    size = part_refs[0].shape[0] // 2
    for ref, step in zip(part_refs, far_first(len(part_refs))):
        cut = slice(step * size, (step + 1) * size)
        keep_ref[cut, :] = ref[:size, :]
        send_ref[cut, :] = ref[size:, :]


def slope(pre_act):
    normal_cdf = 0.5 * (1.0 + lax.erf(pre_act * 0.7071067811865476))
    density = jnp.exp(-0.5 * pre_act * pre_act) * 0.3989422804014327
    return normal_cdf + pre_act * density


def slope_kernel(pieces, pre_hbm, slope_ref, pre, sems):
    rows = pre.shape[0] // pieces
    copies = []
    for piece in range(pieces):
        cut = pl.ds(piece * rows, rows)
        copies.append(pltpu.make_async_copy(pre_hbm.at[0, cut], pre.at[cut], sems.at[piece]))
        copies[-1].start()
    for piece, copy in enumerate(copies):
        copy.wait()
        cut = slice(piece * rows, (piece + 1) * rows)
        slope_ref[cut, :] = slope(pre[cut, :].astype(F32))


def final_kernel(capacity, share, turn, base, *refs):
    part_ref, slope_ref = refs[:2]
    out_hbm, out, sem = refs[-3:]
    rows, slots = out.shape
    part = lax.rem(lax.axis_index("frame") + turn, share) * (slope_ref.shape[0] // share)
    cut = pl.ds(pl.multiple_of(part + base, rows), rows)
    source = lax.broadcasted_iota(jnp.int32, (slots, slots), 0)
    goal = lax.broadcasted_iota(jnp.int32, (slots, slots), 1)
    moved = (goal ^ ((lax.axis_index("frame") ^ turn) * capacity)) == source
    hidden = lax.dot_general(
        part_ref[...],
        jnp.where(moved, 1.0, 0.0).astype(BF16),
        (((0,), (0,)), ((), ())),
        preferred_element_type=F32,
    )
    out[...] = (hidden * slope_ref[cut, :]).astype(BF16)
    store = pltpu.make_async_copy(out, out_hbm.at[0, cut], sem.at[0])
    store.start()
    store.wait()


def chunk_rows(quarter):
    return [quarter // 2] * 2


def body(
    peers,
    owners_count,
    value_grad,
    w_value,
    norm_gain,
    vis_pos,
    frame_owner,
    ques_span,
    vis_proj,
    vis_resid,
    ques_hidden,
    w_down,
    pre_owned,
):
    _, tokens, width = vis_proj.shape
    shard_len, key_width = value_grad.shape[1:]
    length = ques_hidden.shape[1]
    features = peers * width
    slots = pre_owned.shape[2]
    capacity = slots // owners_count
    gain = norm_gain.reshape(1, width)
    owner = frame_owner.reshape(1, tokens)
    row = shape((8, tokens), F32)
    tall = shape((width, tokens), F32)
    dma = pltpu.SemaphoreType.DMA

    pieces = max(1, shard_len // 256)
    own = call(
        functools.partial(pick_kernel, pieces),
        shape((tokens, key_width), BF16),
        [HBM, HBM],
        [
            pltpu.VMEM((1, tokens), jnp.int32),
            pltpu.VMEM((shard_len, key_width), BF16),
            dma((pieces + 1,)),
        ],
        grant=PICK_GRANT,
    )(vis_pos, value_grad)
    own_all = [own] + [swap(own, "seq", peers, k) for k in range(1, peers)]

    stats, projt, residt, gaint, meant, weight = call(
        load_kernel,
        [row, tall, tall, tall, tall, shape(w_value.shape, BF16)],
        [HBM] * 6,
        [
            pltpu.SMEM((1, 2), jnp.int32),
            pltpu.VMEM((length, width), BF16),
            pltpu.VMEM((1, width), F32),
            pltpu.VMEM((tokens, width), BF16),
            pltpu.VMEM((tokens, width), BF16),
            dma((6,)),
        ],
        grant=LOAD_GRANT,
    )(ques_span, ques_hidden, gain, vis_proj, vis_resid, w_value)

    scaledt, sums = call(
        functools.partial(norm_kernel, peers),
        [tall, row],
        [VMEM] * (peers + 4),
        [pltpu.VMEM((key_width, tokens), BF16)],
    )(*own_all, stats, weight, gaint, projt)
    sums_all = [sums] + [swap(sums, "seq", peers, k) for k in range(1, peers)]

    paired = capacity % 16 == 0 and owners_count % 2 == 0
    share = 2 if paired else 1
    pieces = owners_count // 2 if paired else 1
    chunks = chunk_rows(w_down.shape[0] // peers // share)
    bases = [sum(chunks[:i]) for i in range(len(chunks))]
    chain = Chain()

    def sems(rows):
        return dma((peers * (rows // min(rows, 256)),))

    preloaded = call(
        functools.partial(preload_kernel, peers, share, chunks[0]),
        shape((peers * chunks[0], width), BF16),
        [HBM, VMEM],
        [sems(chunks[0])],
    )(w_down, sums)

    gradt, logit = chain.call(
        functools.partial(gate_kernel, features, peers),
        [shape((width + 16, tokens), BF16), row],
        [VMEM] * (peers + 5) + [ANY],
    )(*sums_all, projt, residt, scaledt, meant, owner, preloaded)
    gradts = [gradt] + [swap(gradt, "frame", owners_count, k) for k in range(1, share)]

    def down(index):
        rows = chunks[index]
        weights = [pltpu.VMEM((peers * rows, width), BF16), sems(rows)]
        partial = chain.call(
            functools.partial(down_kernel, peers, share, bases[index], rows, index == 0),
            [shape((rows, share * tokens), BF16)] * peers,
            [VMEM if index == 0 else HBM] + [VMEM] * share,
            [pltpu.VMEM((width, share * tokens), BF16)] + (weights if index else []),
            cost=2 * peers * rows * width,
        )(w_down if index else preloaded, *gradts)
        return swaps(partial, "seq", peers)

    def place(parts, after=()):
        rows = parts[0].shape[0]
        placed = chain.call(
            functools.partial(place_kernel, capacity, share, pieces, len(parts)),
            [shape((slots * share // pieces, rows), BF16)] * pieces,
            [VMEM] * (share + len(parts)) + [ANY] * len(after),
        )(*gradts, *parts, *after)
        if paired:
            return swaps(placed, "frame", owners_count, 2)
        order = jnp.arange(owners_count) ^ lax.axis_index("frame")
        split = placed[0].reshape(owners_count, capacity, rows)[order]
        split = lax.all_to_all(split, "frame", split_axis=0, concat_axis=0, tiled=True)
        return [split[order].reshape(slots, rows)]

    def group(parts):
        if not paired:
            return parts
        keep, send = chain.call(
            group_kernel,
            [shape((slots, parts[0].shape[1]), BF16)] * 2,
            [VMEM] * pieces,
        )(*parts)
        return [keep, swap(send, "frame", owners_count, 1)]

    def finish(parts, index, held):
        rows = chunks[index]
        for turn, part in enumerate(parts):
            held = chain.call(
                functools.partial(final_kernel, capacity, share, turn, bases[index]),
                [shape(pre_owned.shape, BF16)],
                [VMEM, VMEM] + [HBM] * len(held),
                [pltpu.VMEM((rows, slots), BF16), dma((1,))],
                {2: 0} if held else None,
                [HBM],
            )(part, slopes, *held)
        return held

    waiting = [down(0), down(1)]
    (slopes,) = chain.call(
        functools.partial(slope_kernel, 4),
        [shape(pre_owned.shape[1:], F32)],
        [HBM],
        [pltpu.VMEM(pre_owned.shape[1:], BF16), dma((4,))],
    )(pre_owned)
    placed = place(waiting[0], waiting[1][-1:])
    (ques_grad,) = chain.call(
        ques_kernel,
        [shape(ques_hidden.shape, BF16)],
        [HBM, VMEM, HBM],
        [pltpu.SMEM((1, 2), jnp.int32), pltpu.VMEM((tokens, width), BF16), dma((2,))],
        cost=400000000,
    )(ques_span, logit, vis_proj)
    held = []
    for index in range(len(chunks)):
        parts = group(placed)
        if index + 1 < len(chunks):
            placed = place(waiting[index + 1])
            if index + 2 < len(chunks):
                waiting.append(down(index + 2))
        held = finish(parts, index, held)
    return (held[0], ques_grad)


def solution(mesh):
    in_specs = (
        P("frame", "seq", None),
        P("seq", None),
        P("seq"),
        P("frame", None),
        P("frame", None, None),
        P("frame", None),
        P("frame", None, "seq"),
        P("frame", None, "seq"),
        P("frame", None, "seq"),
        P(None, "seq"),
        P("frame", "seq", None),
    )
    out_specs = (P("frame", "seq", None), P("frame", None, "seq"))
    run = functools.partial(body, mesh.shape["seq"], mesh.shape["frame"])
    return jax.shard_map(run, mesh=mesh, in_specs=in_specs, out_specs=out_specs, check_vma=False)
```

```python
import functools
import math

import jax
import jax.numpy as jnp
from jax import lax
from jax.experimental import pallas as pl
from jax.experimental.pallas import tpu as pltpu
from jax.sharding import PartitionSpec as P

EPSILON = 1e-06
F32 = jnp.float32
BF16 = jnp.bfloat16
LANES = 128
AHEAD = 6
MIB = 1024 * 1024
GRANT, LOAD_GRANT, PICK_GRANT = 40, 46, 54
HBM = pl.BlockSpec(memory_space=pltpu.HBM)
VMEM = pl.BlockSpec(memory_space=pltpu.VMEM)
ANY = pl.BlockSpec(memory_space=pl.ANY)


def call(
    kernel, out_shape, in_specs, scratch=(), aliases=None, out_specs=None, grant=GRANT, cost=1024
):
    return pl.pallas_call(
        kernel,
        out_shape=out_shape,
        in_specs=in_specs,
        out_specs=jax.tree.map(lambda _: VMEM, out_shape) if out_specs is None else out_specs,
        scratch_shapes=list(scratch),
        input_output_aliases=aliases or {},
        compiler_params=pltpu.CompilerParams(vmem_limit_bytes=grant * MIB),
        cost_estimate=pl.CostEstimate(flops=256 * cost, bytes_accessed=cost, transcendentals=0),
    )


class Chain:
    def __init__(self):
        self.last = []

    def call(
        self, kernel, out_shape, in_specs, scratch=(), aliases=None, out_specs=None, cost=1024
    ):
        given, made, linked = len(in_specs), len(out_shape), len(self.last)

        def run(*refs):
            outs = refs[given + linked :]
            outs[made][...] = jnp.zeros(outs[made].shape, F32)
            kernel(*refs[:given], *outs[:made], *outs[made + 1 :])

        out_specs = [VMEM] * made if out_specs is None else out_specs
        run_call = call(
            run,
            [*out_shape, shape((8, LANES), F32)],
            [*in_specs, *[VMEM] * linked],
            scratch,
            aliases,
            [*out_specs, VMEM],
            cost=cost,
        )

        def apply(*args):
            *results, token = run_call(*args, *self.last)
            self.last = [token]
            return results

        return apply


def shape(dims, dtype):
    return jax.ShapeDtypeStruct(dims, dtype)


def swap(value, axis, count, step):
    return lax.ppermute(value, axis, [(i, i ^ step) for i in range(count)])


def far_first(count):
    return [0, *reversed(range(1, count))]


def swaps(values, axis, count, stride=1):
    return [
        swap(value, axis, count, step * stride) if step else value
        for value, step in zip(values, far_first(len(values)))
    ]


def to_column(row):
    return jnp.transpose(jnp.broadcast_to(row, (LANES, row.shape[1])), (1, 0))


def pick_kernel(pieces, pos_hbm, rows_hbm, own_ref, pos, rows, sems):
    tokens, shard_len = pos.shape[1], rows.shape[0]
    size = shard_len // pieces
    head = pltpu.make_async_copy(pos_hbm, pos, sems.at[pieces])
    head.start()
    copies = []
    for piece in range(pieces):
        cut = pl.ds(piece * size, size)
        copies.append(
            pltpu.make_async_copy(rows_hbm.at[0, cut], rows.at[cut], sems.at[piece])
        )
        copies[-1].start()
    offset = lax.axis_index("seq") * shard_len
    head.wait()
    column = to_column(pos[...] - offset)
    lanes = lax.broadcasted_iota(jnp.int32, (tokens, LANES), 1)
    total = None
    for piece in range(pieces):
        select = jnp.concatenate(
            [
                jnp.where(column == lanes + at, 1.0, 0.0).astype(BF16)
                for at in range(piece * size, (piece + 1) * size, LANES)
            ],
            axis=1,
        )
        copies[piece].wait()
        part = jnp.dot(
            select, rows[piece * size : (piece + 1) * size, :], preferred_element_type=F32
        )
        total = part if total is None else total + part
    own_ref[...] = total.astype(BF16)


def load_kernel(
    span_hbm, hidden_hbm, gain_hbm, proj_hbm, resid_hbm, weight_hbm,
    stats_ref, projt_ref, residt_ref, gaint_ref, meant_ref, weight_ref,
    span, hidden, gain, proj, resid, sems,
):
    copies = [
        pltpu.make_async_copy(source, target, sems.at[index])
        for index, (source, target) in enumerate(
            [
                (span_hbm, span),
                (hidden_hbm.at[0], hidden),
                (gain_hbm, gain),
                (proj_hbm.at[0], proj),
                (resid_hbm.at[0], resid),
                (weight_hbm, weight_ref),
            ]
        )
    ]
    for copy in copies:
        copy.start()
    for copy in copies[:5]:
        copy.wait()
    start, count = span[0, 0], span[0, 1]
    tokens, width = proj.shape
    places = lax.broadcasted_iota(jnp.int32, (hidden.shape[0], 1), 0)
    mask = ((places >= start) & (places < start + count)).astype(F32)
    query = square = cross = jnp.zeros((LANES, tokens), F32)
    for at in range(0, width, LANES):
        cut = slice(at, at + LANES)
        mean = jnp.sum(hidden[:, cut].astype(F32) * mask, axis=0, keepdims=True)
        meant = to_column(mean / count.astype(F32))
        projt = jnp.transpose(proj[:, cut].astype(F32), (1, 0))
        residt = jnp.transpose(resid[:, cut].astype(F32), (1, 0))
        meant_ref[cut, :] = meant
        projt_ref[cut, :] = projt
        residt_ref[cut, :] = residt
        gaint_ref[cut, :] = to_column(gain[:, cut])
        query = query + projt * meant
        square = square + projt * projt
        cross = cross + projt * residt
    stats_ref[...] = jnp.zeros(stats_ref.shape, F32)
    for row, value in enumerate((query, square, cross)):
        stats_ref[row : row + 1, :] = jnp.sum(value, axis=0, keepdims=True)
    copies[5].wait()


def norm_kernel(peers, *refs):
    own_refs = refs[:peers]
    stats_ref, weight_ref, gaint_ref, projt_ref, scaledt_ref, sums_ref, pickedt = refs[peers:]
    key_width = own_refs[0].shape[1]
    for at in range(0, key_width, LANES):
        cut = slice(at, at + LANES)
        picked = own_refs[0][:, cut].astype(F32)
        for ref in own_refs[1:]:
            picked = picked + ref[:, cut].astype(F32)
        pickedt[cut, :] = jnp.transpose(picked, (1, 0)).astype(BF16)
    width, tokens = projt_ref.shape
    total = jnp.zeros((LANES, tokens), F32)
    for at in range(0, width, 256):
        cut = slice(at, at + 256)
        normed = jnp.dot(weight_ref[cut, :], pickedt[...], preferred_element_type=F32)
        scaled = normed * gaint_ref[cut, :]
        scaledt_ref[cut, :] = scaled
        terms = scaled * projt_ref[cut, :]
        total = total + terms[:LANES] + terms[LANES:]
    sums_ref[...] = stats_ref[...]
    sums_ref[3:4, :] = jnp.sum(total, axis=0, keepdims=True)


def weight_copies(weight_hbm, weights, sems, steps, peers, share, base, rows):
    quarter = weight_hbm.shape[0] // peers
    block = min(rows, 256)
    part = lax.rem(lax.axis_index("frame"), share) * (quarter // share)
    copies = []
    for peer, step in enumerate(steps):
        first = (lax.axis_index("seq") ^ step) * quarter + part + base
        for at in range(0, rows, block):
            index = len(copies)
            copies.append(
                pltpu.make_async_copy(
                    weight_hbm.at[pl.ds(pl.multiple_of(first + at, block), block)],
                    weights.at[pl.ds(peer * rows + at, block)],
                    sems.at[index],
                )
            )
    return copies


def preload_kernel(steps, peers, share, rows, weight_hbm, after_ref, weights_ref, sems):
    del after_ref
    copies = weight_copies(weight_hbm, weights_ref, sems, steps, peers, share, 0, rows)
    for copy in copies:
        copy.start()
    for copy in copies:
        copy.wait()


def gate_kernel(features, peers, *refs):
    sums_refs = refs[:peers]
    projt_ref, residt_ref, scaledt_ref, meant_ref, owner_ref, after_ref = refs[peers : peers + 6]
    del after_ref
    gradt_ref, logit_ref = refs[peers + 6 :]
    sums = sums_refs[0][...]
    for ref in sums_refs[1:]:
        sums = sums + ref[...]
    sum_query, sum_square, sum_resid, sum_norm = (sums[i : i + 1] for i in range(4))
    gate_scale = 4.0 / math.sqrt(features)
    gate = jax.nn.sigmoid(gate_scale * sum_query)
    inv_rms = lax.rsqrt(gate * gate * sum_square / features + EPSILON)
    coef = gate * inv_rms * inv_rms * inv_rms * (gate * sum_norm) / features
    gate_grad = sum_resid + inv_rms * sum_norm - coef * sum_square
    logit = gate_grad * gate * (1.0 - gate) * gate_scale
    logit_ref[...] = jnp.broadcast_to(logit, logit_ref.shape)
    width = projt_ref.shape[0]
    for at in range(0, width, LANES):
        cut = slice(at, at + LANES)
        grad = residt_ref[cut, :] + inv_rms * scaledt_ref[cut, :] - coef * projt_ref[cut, :]
        gradt_ref[cut, :] = (gate * grad + logit * meant_ref[cut, :]).astype(BF16)
    tail = gradt_ref.shape[0] - width
    owner = owner_ref[...].astype(F32)
    gradt_ref[width:, :] = jnp.broadcast_to(owner, (tail, owner.shape[1])).astype(BF16)


def down_kernel(peers, share, base, rows, held, *refs):
    weight_refs = refs[: max(held, 1)]
    gradt_refs = refs[len(weight_refs) : len(weight_refs) + share]
    scratch = list(refs[len(weight_refs) + share :])
    out_refs = [scratch.pop(0) for _ in range(peers)]
    joined = scratch.pop(0)
    copies = []
    if held:
        weights = weight_refs
    else:
        weights, sems = scratch[:1], scratch[1]
        copies = weight_copies(
            weight_refs[0], weights[0], sems, far_first(peers), peers, share, base, rows
        )
    for copy in copies[:AHEAD]:
        copy.start()
    width, tokens = joined.shape[0], gradt_refs[0].shape[1]
    for index, ref in enumerate(gradt_refs):
        joined[:, index * tokens : (index + 1) * tokens] = ref[:width, :]
    block = min(rows, 256)
    inner = rows // block
    each = peers * inner // len(weights)
    for index in range(peers * inner):
        peer, part = index // inner, index % inner
        if copies:
            copies[index].wait()
        if index + AHEAD < len(copies):
            copies[index + AHEAD].start()
        place = index % each
        value = jnp.dot(
            weights[index // each][place * block : (place + 1) * block, :],
            joined[...],
            preferred_element_type=F32,
        )
        out_refs[peer][part * block : (part + 1) * block, :] = value.astype(BF16)


def ques_kernel(span_hbm, logit_ref, proj_hbm, out_ref, span, proj, sems):
    head = pltpu.make_async_copy(span_hbm, span, sems.at[0])
    load = pltpu.make_async_copy(proj_hbm.at[0], proj, sems.at[1])
    head.start()
    load.start()
    head.wait()
    start, count = span[0, 0], span[0, 1]
    length, width = out_ref.shape[1], out_ref.shape[2]
    places = lax.broadcasted_iota(jnp.int32, (length, LANES), 0)
    mask = ((places >= start) & (places < start + count)).astype(F32)
    column = to_column(logit_ref[0:1, :])
    load.wait()
    for at in range(0, width, LANES):
        cut = slice(at, at + LANES)
        total = jnp.sum(column * proj[:, cut].astype(F32), axis=0, keepdims=True)
        out_ref[0, :, cut] = (mask * total / count.astype(F32)).astype(BF16)


def targets(owner, capacity, share, source):
    tokens = owner.shape[1]
    above = lax.broadcasted_iota(jnp.int32, (tokens, tokens), 0)
    below = lax.broadcasted_iota(jnp.int32, (tokens, tokens), 1)
    earlier = jnp.where((to_column(owner) == owner) & (above < below), 1.0, 0.0)
    rank = jnp.sum(earlier, axis=0, keepdims=True).astype(jnp.int32)
    away = owner ^ lax.axis_index("frame")
    return (away * share + source) * capacity + rank


def place_kernel(capacity, share, pieces, mine, *refs):
    gradt_refs = refs[:share]
    part_refs = refs[share : share + mine]
    out_refs = refs[-pieces:]
    target = jnp.concatenate(
        [
            targets(ref[-16:-15, :].astype(F32).astype(jnp.int32), capacity, share, source)
            for source, ref in enumerate(gradt_refs)
        ],
        axis=1,
    )
    size = out_refs[0].shape[0]
    places = lax.broadcasted_iota(jnp.int32, (size * pieces, target.shape[1]), 0)
    placing = jnp.where(places == target, 1.0, 0.0).astype(BF16)
    total = part_refs[0][...].astype(F32)
    for ref in part_refs[1:]:
        total = total + ref[...].astype(F32)
    placed = lax.dot_general(
        placing, total.astype(BF16), (((1,), (1,)), ((), ())), preferred_element_type=F32
    ).astype(BF16)
    for ref, step in zip(out_refs, far_first(pieces)):
        ref[...] = placed[step * size : (step + 1) * size, :]


def group_kernel(*refs):
    *part_refs, keep_ref, send_ref = refs
    size = part_refs[0].shape[0] // 2
    for ref, step in zip(part_refs, far_first(len(part_refs))):
        cut = slice(step * size, (step + 1) * size)
        keep_ref[cut, :] = ref[:size, :]
        send_ref[cut, :] = ref[size:, :]


def slope(pre_act):
    normal_cdf = 0.5 * (1.0 + lax.erf(pre_act * 0.7071067811865476))
    density = jnp.exp(-0.5 * pre_act * pre_act) * 0.3989422804014327
    return normal_cdf + pre_act * density


def slope_kernel(pieces, pre_hbm, slope_ref, pre, sems):
    rows = pre.shape[0] // pieces
    copies = []
    for piece in range(pieces):
        cut = pl.ds(piece * rows, rows)
        copies.append(pltpu.make_async_copy(pre_hbm.at[0, cut], pre.at[cut], sems.at[piece]))
        copies[-1].start()
    for piece, copy in enumerate(copies):
        copy.wait()
        cut = slice(piece * rows, (piece + 1) * rows)
        slope_ref[cut, :] = slope(pre[cut, :].astype(F32))


def final_kernel(capacity, share, turn, base, *refs):
    part_ref, slope_ref = refs[:2]
    out_hbm, out, sem = refs[-3:]
    rows, slots = out.shape
    part = lax.rem(lax.axis_index("frame") + turn, share) * (slope_ref.shape[0] // share)
    cut = pl.ds(pl.multiple_of(part + base, rows), rows)
    source = lax.broadcasted_iota(jnp.int32, (slots, slots), 0)
    goal = lax.broadcasted_iota(jnp.int32, (slots, slots), 1)
    moved = (goal ^ ((lax.axis_index("frame") ^ turn) * capacity)) == source
    hidden = lax.dot_general(
        part_ref[...],
        jnp.where(moved, 1.0, 0.0).astype(BF16),
        (((0,), (0,)), ((), ())),
        preferred_element_type=F32,
    )
    out[...] = (hidden * slope_ref[cut, :]).astype(BF16)
    store = pltpu.make_async_copy(out, out_hbm.at[0, cut], sem.at[0])
    store.start()
    store.wait()


def chunk_rows(quarter):
    return [quarter // 2] * 2


def body(
    peers,
    owners_count,
    value_grad,
    w_value,
    norm_gain,
    vis_pos,
    frame_owner,
    ques_span,
    vis_proj,
    vis_resid,
    ques_hidden,
    w_down,
    pre_owned,
):
    _, tokens, width = vis_proj.shape
    shard_len, key_width = value_grad.shape[1:]
    length = ques_hidden.shape[1]
    features = peers * width
    slots = pre_owned.shape[2]
    capacity = slots // owners_count
    gain = norm_gain.reshape(1, width)
    owner = frame_owner.reshape(1, tokens)
    row = shape((8, tokens), F32)
    tall = shape((width, tokens), F32)
    dma = pltpu.SemaphoreType.DMA

    pieces = max(1, shard_len // 256)
    own = call(
        functools.partial(pick_kernel, pieces),
        shape((tokens, key_width), BF16),
        [HBM, HBM],
        [
            pltpu.VMEM((1, tokens), jnp.int32),
            pltpu.VMEM((shard_len, key_width), BF16),
            dma((pieces + 1,)),
        ],
        grant=PICK_GRANT,
    )(vis_pos, value_grad)
    own_all = [own] + [swap(own, "seq", peers, k) for k in range(1, peers)]

    stats, projt, residt, gaint, meant, weight = call(
        load_kernel,
        [row, tall, tall, tall, tall, shape(w_value.shape, BF16)],
        [HBM] * 6,
        [
            pltpu.SMEM((1, 2), jnp.int32),
            pltpu.VMEM((length, width), BF16),
            pltpu.VMEM((1, width), F32),
            pltpu.VMEM((tokens, width), BF16),
            pltpu.VMEM((tokens, width), BF16),
            dma((6,)),
        ],
        grant=LOAD_GRANT,
    )(ques_span, ques_hidden, gain, vis_proj, vis_resid, w_value)

    scaledt, sums = call(
        functools.partial(norm_kernel, peers),
        [tall, row],
        [VMEM] * (peers + 4),
        [pltpu.VMEM((key_width, tokens), BF16)],
    )(*own_all, stats, weight, gaint, projt)
    sums_all = [sums] + [swap(sums, "seq", peers, k) for k in range(1, peers)]

    paired = capacity % 16 == 0 and owners_count % 2 == 0
    share = 2 if paired else 1
    pieces = owners_count // 2 if paired else 1
    chunks = chunk_rows(w_down.shape[0] // peers // share)
    bases = [sum(chunks[:i]) for i in range(len(chunks))]
    chain = Chain()

    def sems(rows, count=peers):
        return dma((count * (rows // min(rows, 256)),))

    def preload(caller, steps, after):
        (weights,) = caller(
            functools.partial(preload_kernel, steps, peers, share, chunks[0]),
            [shape((len(steps) * chunks[0], width), BF16)],
            [HBM, VMEM],
            [sems(chunks[0], len(steps))],
        )(w_down, after)
        return weights

    steps = far_first(peers)
    preloaded = [preload(call, steps[: peers // 2], sums)]
    gradt, logit = chain.call(
        functools.partial(gate_kernel, features, peers),
        [shape((width + 16, tokens), BF16), row],
        [VMEM] * (peers + 5) + [ANY],
    )(*sums_all, projt, residt, scaledt, meant, owner, preloaded[0])
    preloaded.append(preload(chain.call, steps[peers // 2 :], logit))
    gradts = [gradt] + [swap(gradt, "frame", owners_count, k) for k in range(1, share)]

    def down(index):
        rows = chunks[index]
        weights = [pltpu.VMEM((peers * rows, width), BF16), sems(rows)]
        partial = chain.call(
            functools.partial(
                down_kernel, peers, share, bases[index], rows, 0 if index else len(preloaded)
            ),
            [shape((rows, share * tokens), BF16)] * peers,
            ([HBM] if index else [VMEM] * len(preloaded)) + [VMEM] * share,
            [pltpu.VMEM((width, share * tokens), BF16)] + (weights if index else []),
            cost=2 * peers * rows * width,
        )(*([w_down] if index else preloaded), *gradts)
        return swaps(partial, "seq", peers)

    def place(parts):
        rows = parts[0].shape[0]
        placed = chain.call(
            functools.partial(place_kernel, capacity, share, pieces, len(parts)),
            [shape((slots * share // pieces, rows), BF16)] * pieces,
            [VMEM] * (share + len(parts)),
        )(*gradts, *parts)
        if paired:
            return swaps(placed, "frame", owners_count, 2)
        order = jnp.arange(owners_count) ^ lax.axis_index("frame")
        split = placed[0].reshape(owners_count, capacity, rows)[order]
        split = lax.all_to_all(split, "frame", split_axis=0, concat_axis=0, tiled=True)
        return [split[order].reshape(slots, rows)]

    def group(parts):
        if not paired:
            return parts
        keep, send = chain.call(
            group_kernel,
            [shape((slots, parts[0].shape[1]), BF16)] * 2,
            [VMEM] * pieces,
        )(*parts)
        return [keep, swap(send, "frame", owners_count, 1)]

    def finish(parts, index, turn, held):
        rows = chunks[index]
        return chain.call(
            functools.partial(final_kernel, capacity, share, turn, bases[index]),
            [shape(pre_owned.shape, BF16)],
            [VMEM, VMEM] + [HBM] * len(held),
            [pltpu.VMEM((rows, slots), BF16), dma((1,))],
            {2: 0} if held else None,
            [HBM],
        )(parts[turn], slopes, *held)

    waiting = [down(0), down(1)]
    (slopes,) = chain.call(
        functools.partial(slope_kernel, 4),
        [shape(pre_owned.shape[1:], F32)],
        [HBM],
        [pltpu.VMEM(pre_owned.shape[1:], BF16), dma((4,))],
    )(pre_owned)
    (ques_grad,) = chain.call(
        ques_kernel,
        [shape(ques_hidden.shape, BF16)],
        [HBM, VMEM, HBM],
        [pltpu.SMEM((1, 2), jnp.int32), pltpu.VMEM((tokens, width), BF16), dma((2,))],
        cost=400000000,
    )(ques_span, logit, vis_proj)
    placed = [place(parts) for parts in waiting]
    first = group(placed[0])
    held = finish(first, 0, 0, [])
    second = group(placed[1])
    for turn in range(1, share):
        held = finish(first, 0, turn, held)
    for turn in range(share):
        held = finish(second, 1, turn, held)
    return (held[0], ques_grad)


def solution(mesh):
    in_specs = (
        P("frame", "seq", None),
        P("seq", None),
        P("seq"),
        P("frame", None),
        P("frame", None, None),
        P("frame", None),
        P("frame", None, "seq"),
        P("frame", None, "seq"),
        P("frame", None, "seq"),
        P(None, "seq"),
        P("frame", "seq", None),
    )
    out_specs = (P("frame", "seq", None), P("frame", None, "seq"))
    run = functools.partial(body, mesh.shape["seq"], mesh.shape["frame"])
    return jax.shard_map(run, mesh=mesh, in_specs=in_specs, out_specs=out_specs, check_vma=False)
```

```python
import functools
import math

import jax
import jax.numpy as jnp
from jax import lax
from jax.experimental import pallas as pl
from jax.experimental.pallas import tpu as pltpu
from jax.sharding import PartitionSpec as P

EPSILON = 1e-06
F32 = jnp.float32
BF16 = jnp.bfloat16
LANES = 128
AHEAD = 4
MIB = 1024 * 1024
GRANT, LOAD_GRANT, PICK_GRANT = 40, 46, 54
HBM = pl.BlockSpec(memory_space=pltpu.HBM)
VMEM = pl.BlockSpec(memory_space=pltpu.VMEM)
ANY = pl.BlockSpec(memory_space=pl.ANY)


def call(
    kernel, out_shape, in_specs, scratch=(), aliases=None, out_specs=None, grant=GRANT, cost=1024
):
    return pl.pallas_call(
        kernel,
        out_shape=out_shape,
        in_specs=in_specs,
        out_specs=jax.tree.map(lambda _: VMEM, out_shape) if out_specs is None else out_specs,
        scratch_shapes=list(scratch),
        input_output_aliases=aliases or {},
        compiler_params=pltpu.CompilerParams(vmem_limit_bytes=grant * MIB),
        cost_estimate=pl.CostEstimate(flops=256 * cost, bytes_accessed=cost, transcendentals=0),
    )


class Chain:
    def __init__(self):
        self.last = []

    def call(
        self, kernel, out_shape, in_specs, scratch=(), aliases=None, out_specs=None, cost=1024
    ):
        given, made, linked = len(in_specs), len(out_shape), len(self.last)

        def run(*refs):
            outs = refs[given + linked :]
            outs[made][...] = jnp.zeros(outs[made].shape, F32)
            kernel(*refs[:given], *outs[:made], *outs[made + 1 :])

        out_specs = [VMEM] * made if out_specs is None else out_specs
        run_call = call(
            run,
            [*out_shape, shape((8, LANES), F32)],
            [*in_specs, *[VMEM] * linked],
            scratch,
            aliases,
            [*out_specs, VMEM],
            cost=cost,
        )

        def apply(*args):
            *results, token = run_call(*args, *self.last)
            self.last = [token]
            return results

        return apply


def shape(dims, dtype):
    return jax.ShapeDtypeStruct(dims, dtype)


def swap(value, axis, count, step):
    return lax.ppermute(value, axis, [(i, i ^ step) for i in range(count)])


def far_first(count):
    return [0, *reversed(range(1, count))]


def swaps(values, axis, count, stride=1):
    return [
        swap(value, axis, count, step * stride) if step else value
        for value, step in zip(values, far_first(len(values)))
    ]


def to_column(row):
    return jnp.transpose(jnp.broadcast_to(row, (LANES, row.shape[1])), (1, 0))


def pick_kernel(pieces, pos_hbm, rows_hbm, own_ref, pos, rows, sems):
    tokens, shard_len = pos.shape[1], rows.shape[0]
    size = shard_len // pieces
    head = pltpu.make_async_copy(pos_hbm, pos, sems.at[pieces])
    head.start()
    copies = []
    for piece in range(pieces):
        cut = pl.ds(piece * size, size)
        copies.append(
            pltpu.make_async_copy(rows_hbm.at[0, cut], rows.at[cut], sems.at[piece])
        )
        copies[-1].start()
    offset = lax.axis_index("seq") * shard_len
    head.wait()
    column = to_column(pos[...] - offset)
    lanes = lax.broadcasted_iota(jnp.int32, (tokens, LANES), 1)
    total = None
    for piece in range(pieces):
        select = jnp.concatenate(
            [
                jnp.where(column == lanes + at, 1.0, 0.0).astype(BF16)
                for at in range(piece * size, (piece + 1) * size, LANES)
            ],
            axis=1,
        )
        copies[piece].wait()
        part = jnp.dot(
            select, rows[piece * size : (piece + 1) * size, :], preferred_element_type=F32
        )
        total = part if total is None else total + part
    own_ref[...] = total.astype(BF16)


def load_kernel(
    span_hbm, hidden_hbm, gain_hbm, proj_hbm, resid_hbm, weight_hbm,
    stats_ref, projt_ref, residt_ref, gaint_ref, meant_ref, weight_ref,
    span, hidden, gain, proj, resid, sems,
):
    copies = [
        pltpu.make_async_copy(source, target, sems.at[index])
        for index, (source, target) in enumerate(
            [
                (span_hbm, span),
                (hidden_hbm.at[0], hidden),
                (gain_hbm, gain),
                (proj_hbm.at[0], proj),
                (resid_hbm.at[0], resid),
                (weight_hbm, weight_ref),
            ]
        )
    ]
    for copy in copies:
        copy.start()
    for copy in copies[:5]:
        copy.wait()
    start, count = span[0, 0], span[0, 1]
    tokens, width = proj.shape
    places = lax.broadcasted_iota(jnp.int32, (hidden.shape[0], 1), 0)
    mask = ((places >= start) & (places < start + count)).astype(F32)
    query = square = cross = jnp.zeros((LANES, tokens), F32)
    for at in range(0, width, LANES):
        cut = slice(at, at + LANES)
        mean = jnp.sum(hidden[:, cut].astype(F32) * mask, axis=0, keepdims=True)
        meant = to_column(mean / count.astype(F32))
        projt = jnp.transpose(proj[:, cut].astype(F32), (1, 0))
        residt = jnp.transpose(resid[:, cut].astype(F32), (1, 0))
        meant_ref[cut, :] = meant
        projt_ref[cut, :] = projt
        residt_ref[cut, :] = residt
        gaint_ref[cut, :] = to_column(gain[:, cut])
        query = query + projt * meant
        square = square + projt * projt
        cross = cross + projt * residt
    stats_ref[...] = jnp.zeros(stats_ref.shape, F32)
    for row, value in enumerate((query, square, cross)):
        stats_ref[row : row + 1, :] = jnp.sum(value, axis=0, keepdims=True)
    copies[5].wait()


def norm_kernel(peers, *refs):
    own_refs = refs[:peers]
    stats_ref, weight_ref, gaint_ref, projt_ref, scaledt_ref, sums_ref, pickedt = refs[peers:]
    key_width = own_refs[0].shape[1]
    for at in range(0, key_width, LANES):
        cut = slice(at, at + LANES)
        picked = own_refs[0][:, cut].astype(F32)
        for ref in own_refs[1:]:
            picked = picked + ref[:, cut].astype(F32)
        pickedt[cut, :] = jnp.transpose(picked, (1, 0)).astype(BF16)
    width, tokens = projt_ref.shape
    total = jnp.zeros((LANES, tokens), F32)
    for at in range(0, width, 256):
        cut = slice(at, at + 256)
        normed = jnp.dot(weight_ref[cut, :], pickedt[...], preferred_element_type=F32)
        scaled = normed * gaint_ref[cut, :]
        scaledt_ref[cut, :] = scaled
        terms = scaled * projt_ref[cut, :]
        total = total + terms[:LANES] + terms[LANES:]
    sums_ref[...] = stats_ref[...]
    sums_ref[3:4, :] = jnp.sum(total, axis=0, keepdims=True)


def weight_copy(weight_hbm, weights, sems, peers, share, base, rows, index, skipped=0):
    quarter = weight_hbm.shape[0] // peers
    block = min(rows, 256)
    inner = rows // block
    step = lax.rem(peers - index // inner, peers)
    first = (lax.axis_index("seq") ^ step) * quarter + base + lax.rem(index, inner) * block
    first += lax.rem(lax.axis_index("frame"), share) * (quarter // share)
    place = index - skipped
    return pltpu.make_async_copy(
        weight_hbm.at[pl.ds(pl.multiple_of(first, block), block)],
        weights.at[pl.ds(pl.multiple_of(place * block, block), block)],
        sems.at[place],
    )


def preload_kernel(skipped, count, peers, share, rows, weight_hbm, after_ref, weights_ref, sems):
    del after_ref
    copies = [
        weight_copy(weight_hbm, weights_ref, sems, peers, share, 0, rows, index, skipped)
        for index in range(skipped, skipped + count)
    ]
    for copy in copies:
        copy.start()
    for copy in copies:
        copy.wait()


def gate_kernel(features, peers, *refs):
    sums_refs = refs[:peers]
    projt_ref, residt_ref, scaledt_ref, meant_ref, owner_ref, after_ref = refs[peers : peers + 6]
    del after_ref
    gradt_ref, logit_ref = refs[peers + 6 :]
    sums = sums_refs[0][...]
    for ref in sums_refs[1:]:
        sums = sums + ref[...]
    sum_query, sum_square, sum_resid, sum_norm = (sums[i : i + 1] for i in range(4))
    gate_scale = 4.0 / math.sqrt(features)
    gate = jax.nn.sigmoid(gate_scale * sum_query)
    inv_rms = lax.rsqrt(gate * gate * sum_square / features + EPSILON)
    coef = gate * inv_rms * inv_rms * inv_rms * (gate * sum_norm) / features
    gate_grad = sum_resid + inv_rms * sum_norm - coef * sum_square
    logit = gate_grad * gate * (1.0 - gate) * gate_scale
    logit_ref[...] = jnp.broadcast_to(logit, logit_ref.shape)
    width = projt_ref.shape[0]
    for at in range(0, width, LANES):
        cut = slice(at, at + LANES)
        grad = residt_ref[cut, :] + inv_rms * scaledt_ref[cut, :] - coef * projt_ref[cut, :]
        gradt_ref[cut, :] = (gate * grad + logit * meant_ref[cut, :]).astype(BF16)
    tail = gradt_ref.shape[0] - width
    owner = owner_ref[...].astype(F32)
    gradt_ref[width:, :] = jnp.broadcast_to(owner, (tail, owner.shape[1])).astype(BF16)


def down_kernel(peers, share, base, rows, held, *refs):
    weight_refs = refs[: max(held, 1)]
    gradt_refs = refs[len(weight_refs) : len(weight_refs) + share]
    scratch = list(refs[len(weight_refs) + share :])
    out_refs = [scratch.pop(0) for _ in range(peers)]
    joined = scratch.pop(0)
    block = min(rows, 256)
    inner = rows // block
    total = peers * inner

    def copy(index):
        return weight_copy(weight_refs[0], *scratch, peers, share, base, rows, index)

    if not held:
        for index in range(min(AHEAD, total)):
            copy(index).start()
    width, tokens = joined.shape[0], gradt_refs[0].shape[1]
    for index, ref in enumerate(gradt_refs):
        joined[:, index * tokens : (index + 1) * tokens] = ref[:width, :]
    each = total // len(weight_refs)
    for peer, ref in enumerate(out_refs):
        if held:
            weights = weight_refs[peer * inner // each]
            for part in range(inner):
                at = (peer * inner + part) % each * block
                value = jnp.dot(
                    weights[at : at + block, :], joined[...], preferred_element_type=F32
                )
                ref[part * block : (part + 1) * block, :] = value.astype(BF16)
            continue

        def step(part, carry, peer=peer, ref=ref):
            index = peer * inner + part
            copy(index).wait()

            @pl.when(index + AHEAD < total)
            def _():
                copy(index + AHEAD).start()

            at = pl.multiple_of(index * block, block)
            value = jnp.dot(
                scratch[0][pl.ds(at, block), :], joined[...], preferred_element_type=F32
            )
            ref[pl.ds(pl.multiple_of(part * block, block), block), :] = value.astype(BF16)
            return carry

        lax.fori_loop(0, inner, step, 0)


def ques_kernel(span_hbm, logit_ref, proj_hbm, out_ref, span, proj, sems):
    head = pltpu.make_async_copy(span_hbm, span, sems.at[0])
    load = pltpu.make_async_copy(proj_hbm.at[0], proj, sems.at[1])
    head.start()
    load.start()
    head.wait()
    start, count = span[0, 0], span[0, 1]
    length, width = out_ref.shape[1], out_ref.shape[2]
    places = lax.broadcasted_iota(jnp.int32, (length, LANES), 0)
    mask = ((places >= start) & (places < start + count)).astype(F32)
    column = to_column(logit_ref[0:1, :])
    load.wait()
    for at in range(0, width, LANES):
        cut = slice(at, at + LANES)
        total = jnp.sum(column * proj[:, cut].astype(F32), axis=0, keepdims=True)
        out_ref[0, :, cut] = (mask * total / count.astype(F32)).astype(BF16)


def targets(owner, capacity, share, source):
    tokens = owner.shape[1]
    above = lax.broadcasted_iota(jnp.int32, (tokens, tokens), 0)
    below = lax.broadcasted_iota(jnp.int32, (tokens, tokens), 1)
    earlier = jnp.where((to_column(owner) == owner) & (above < below), 1.0, 0.0)
    rank = jnp.sum(earlier, axis=0, keepdims=True).astype(jnp.int32)
    away = owner ^ lax.axis_index("frame")
    return (away * share + source) * capacity + rank


def place_kernel(capacity, share, pieces, mine, *refs):
    gradt_refs = refs[:share]
    part_refs = refs[share : share + mine]
    out_refs = refs[-pieces:]
    target = jnp.concatenate(
        [
            targets(ref[-16:-15, :].astype(F32).astype(jnp.int32), capacity, share, source)
            for source, ref in enumerate(gradt_refs)
        ],
        axis=1,
    )
    size = out_refs[0].shape[0]
    places = lax.broadcasted_iota(jnp.int32, (size * pieces, target.shape[1]), 0)
    placing = jnp.where(places == target, 1.0, 0.0).astype(BF16)
    total = part_refs[0][...].astype(F32)
    for ref in part_refs[1:]:
        total = total + ref[...].astype(F32)
    placed = lax.dot_general(
        placing, total.astype(BF16), (((1,), (1,)), ((), ())), preferred_element_type=F32
    ).astype(BF16)
    for ref, step in zip(out_refs, far_first(pieces)):
        ref[...] = placed[step * size : (step + 1) * size, :]


def group_kernel(*refs):
    *part_refs, keep_ref, send_ref = refs
    size = part_refs[0].shape[0] // 2
    for ref, step in zip(part_refs, far_first(len(part_refs))):
        cut = slice(step * size, (step + 1) * size)
        keep_ref[cut, :] = ref[:size, :]
        send_ref[cut, :] = ref[size:, :]


def slope(pre_act):
    normal_cdf = 0.5 * (1.0 + lax.erf(pre_act * 0.7071067811865476))
    density = jnp.exp(-0.5 * pre_act * pre_act) * 0.3989422804014327
    return normal_cdf + pre_act * density


def slope_kernel(pieces, pre_hbm, slope_ref, pre, sems):
    rows = pre.shape[0] // pieces
    copies = []
    for piece in range(pieces):
        cut = pl.ds(piece * rows, rows)
        copies.append(pltpu.make_async_copy(pre_hbm.at[0, cut], pre.at[cut], sems.at[piece]))
        copies[-1].start()
    for piece, copy in enumerate(copies):
        copy.wait()
        cut = slice(piece * rows, (piece + 1) * rows)
        slope_ref[cut, :] = slope(pre[cut, :].astype(F32))


def final_kernel(capacity, share, turn, base, *refs):
    part_ref, slope_ref = refs[:2]
    out_hbm, out, sem = refs[-3:]
    rows, slots = out.shape
    part = lax.rem(lax.axis_index("frame") + turn, share) * (slope_ref.shape[0] // share)
    cut = pl.ds(pl.multiple_of(part + base, rows), rows)
    source = lax.broadcasted_iota(jnp.int32, (slots, slots), 0)
    goal = lax.broadcasted_iota(jnp.int32, (slots, slots), 1)
    moved = (goal ^ ((lax.axis_index("frame") ^ turn) * capacity)) == source
    hidden = lax.dot_general(
        part_ref[...],
        jnp.where(moved, 1.0, 0.0).astype(BF16),
        (((0,), (0,)), ((), ())),
        preferred_element_type=F32,
    )
    out[...] = (hidden * slope_ref[cut, :]).astype(BF16)
    store = pltpu.make_async_copy(out, out_hbm.at[0, cut], sem.at[0])
    store.start()
    store.wait()


def chunk_rows(quarter):
    return [quarter // 2] * 2


def body(
    peers,
    owners_count,
    value_grad,
    w_value,
    norm_gain,
    vis_pos,
    frame_owner,
    ques_span,
    vis_proj,
    vis_resid,
    ques_hidden,
    w_down,
    pre_owned,
):
    _, tokens, width = vis_proj.shape
    shard_len, key_width = value_grad.shape[1:]
    length = ques_hidden.shape[1]
    features = peers * width
    slots = pre_owned.shape[2]
    capacity = slots // owners_count
    gain = norm_gain.reshape(1, width)
    owner = frame_owner.reshape(1, tokens)
    row = shape((8, tokens), F32)
    tall = shape((width, tokens), F32)
    dma = pltpu.SemaphoreType.DMA

    pieces = max(1, shard_len // 256)
    own = call(
        functools.partial(pick_kernel, pieces),
        shape((tokens, key_width), BF16),
        [HBM, HBM],
        [
            pltpu.VMEM((1, tokens), jnp.int32),
            pltpu.VMEM((shard_len, key_width), BF16),
            dma((pieces + 1,)),
        ],
        grant=PICK_GRANT,
    )(vis_pos, value_grad)
    own_all = [own] + [swap(own, "seq", peers, k) for k in range(1, peers)]

    stats, projt, residt, gaint, meant, weight = call(
        load_kernel,
        [row, tall, tall, tall, tall, shape(w_value.shape, BF16)],
        [HBM] * 6,
        [
            pltpu.SMEM((1, 2), jnp.int32),
            pltpu.VMEM((length, width), BF16),
            pltpu.VMEM((1, width), F32),
            pltpu.VMEM((tokens, width), BF16),
            pltpu.VMEM((tokens, width), BF16),
            dma((6,)),
        ],
        grant=LOAD_GRANT,
    )(ques_span, ques_hidden, gain, vis_proj, vis_resid, w_value)

    scaledt, sums = call(
        functools.partial(norm_kernel, peers),
        [tall, row],
        [VMEM] * (peers + 4),
        [pltpu.VMEM((key_width, tokens), BF16)],
    )(*own_all, stats, weight, gaint, projt)
    sums_all = [sums] + [swap(sums, "seq", peers, k) for k in range(1, peers)]

    paired = capacity % 16 == 0 and owners_count % 2 == 0
    share = 2 if paired else 1
    pieces = owners_count // 2 if paired else 1
    chunks = chunk_rows(w_down.shape[0] // peers // share)
    bases = [sum(chunks[:i]) for i in range(len(chunks))]
    chain = Chain()

    def sems(rows, count=peers):
        return dma((count * (rows // min(rows, 256)),))

    def preload(caller, half, after):
        count = peers // 2 * (chunks[0] // min(chunks[0], 256))
        (weights,) = caller(
            functools.partial(preload_kernel, half * count, count, peers, share, chunks[0]),
            [shape((peers // 2 * chunks[0], width), BF16)],
            [HBM, VMEM],
            [sems(chunks[0], peers // 2)],
        )(w_down, after)
        return weights

    preloaded = [preload(call, 0, sums)]
    gradt, logit = chain.call(
        functools.partial(gate_kernel, features, peers),
        [shape((width + 16, tokens), BF16), row],
        [VMEM] * (peers + 5) + [ANY],
    )(*sums_all, projt, residt, scaledt, meant, owner, preloaded[0])
    preloaded.append(preload(chain.call, 1, logit))
    gradts = [gradt] + [swap(gradt, "frame", owners_count, k) for k in range(1, share)]

    def down(index):
        rows = chunks[index]
        weights = [pltpu.VMEM((peers * rows, width), BF16), sems(rows)]
        partial = chain.call(
            functools.partial(
                down_kernel, peers, share, bases[index], rows, 0 if index else len(preloaded)
            ),
            [shape((rows, share * tokens), BF16)] * peers,
            ([HBM] if index else [VMEM] * len(preloaded)) + [VMEM] * share,
            [pltpu.VMEM((width, share * tokens), BF16)] + (weights if index else []),
            cost=2 * peers * rows * width,
        )(*([w_down] if index else preloaded), *gradts)
        return swaps(partial, "seq", peers)

    def place(parts):
        rows = parts[0].shape[0]
        placed = chain.call(
            functools.partial(place_kernel, capacity, share, pieces, len(parts)),
            [shape((slots * share // pieces, rows), BF16)] * pieces,
            [VMEM] * (share + len(parts)),
        )(*gradts, *parts)
        if paired:
            return swaps(placed, "frame", owners_count, 2)
        order = jnp.arange(owners_count) ^ lax.axis_index("frame")
        split = placed[0].reshape(owners_count, capacity, rows)[order]
        split = lax.all_to_all(split, "frame", split_axis=0, concat_axis=0, tiled=True)
        return [split[order].reshape(slots, rows)]

    def group(parts):
        if not paired:
            return parts
        keep, send = chain.call(
            group_kernel,
            [shape((slots, parts[0].shape[1]), BF16)] * 2,
            [VMEM] * pieces,
        )(*parts)
        return [keep, swap(send, "frame", owners_count, 1)]

    def finish(parts, index, turn, held):
        rows = chunks[index]
        return chain.call(
            functools.partial(final_kernel, capacity, share, turn, bases[index]),
            [shape(pre_owned.shape, BF16)],
            [VMEM, VMEM] + [HBM] * len(held),
            [pltpu.VMEM((rows, slots), BF16), dma((1,))],
            {2: 0} if held else None,
            [HBM],
        )(parts[turn], slopes, *held)

    waiting = [down(0), down(1)]
    (slopes,) = chain.call(
        functools.partial(slope_kernel, 4),
        [shape(pre_owned.shape[1:], F32)],
        [HBM],
        [pltpu.VMEM(pre_owned.shape[1:], BF16), dma((4,))],
    )(pre_owned)
    (ques_grad,) = chain.call(
        ques_kernel,
        [shape(ques_hidden.shape, BF16)],
        [HBM, VMEM, HBM],
        [pltpu.SMEM((1, 2), jnp.int32), pltpu.VMEM((tokens, width), BF16), dma((2,))],
        cost=400000000,
    )(ques_span, logit, vis_proj)
    placed = [place(parts) for parts in waiting]
    first = group(placed[0])
    held = finish(first, 0, 0, [])
    second = group(placed[1])
    for turn in range(1, share):
        held = finish(first, 0, turn, held)
    for turn in range(share):
        held = finish(second, 1, turn, held)
    return (held[0], ques_grad)


def solution(mesh):
    in_specs = (
        P("frame", "seq", None),
        P("seq", None),
        P("seq"),
        P("frame", None),
        P("frame", None, None),
        P("frame", None),
        P("frame", None, "seq"),
        P("frame", None, "seq"),
        P("frame", None, "seq"),
        P(None, "seq"),
        P("frame", "seq", None),
    )
    out_specs = (P("frame", "seq", None), P("frame", None, "seq"))
    run = functools.partial(body, mesh.shape["seq"], mesh.shape["frame"])
    return jax.shard_map(run, mesh=mesh, in_specs=in_specs, out_specs=out_specs, check_vma=False)
```

```python
import functools
import math

import jax
import jax.numpy as jnp
from jax import lax
from jax.experimental import pallas as pl
from jax.experimental.pallas import tpu as pltpu
from jax.sharding import PartitionSpec as P

EPSILON = 1e-06
F32 = jnp.float32
BF16 = jnp.bfloat16
LANES = 128
AHEAD = 4
MIB = 1024 * 1024
GRANT, LOAD_GRANT, PICK_GRANT = 40, 46, 53
HBM = pl.BlockSpec(memory_space=pltpu.HBM)
VMEM = pl.BlockSpec(memory_space=pltpu.VMEM)
ANY = pl.BlockSpec(memory_space=pl.ANY)


def call(
    kernel, out_shape, in_specs, scratch=(), aliases=None, out_specs=None, grant=GRANT, cost=1024
):
    return pl.pallas_call(
        kernel,
        out_shape=out_shape,
        in_specs=in_specs,
        out_specs=jax.tree.map(lambda _: VMEM, out_shape) if out_specs is None else out_specs,
        scratch_shapes=list(scratch),
        input_output_aliases=aliases or {},
        compiler_params=pltpu.CompilerParams(vmem_limit_bytes=grant * MIB),
        cost_estimate=pl.CostEstimate(flops=256 * cost, bytes_accessed=cost, transcendentals=0),
    )


class Chain:
    def __init__(self):
        self.last = []

    def call(
        self, kernel, out_shape, in_specs, scratch=(), aliases=None, out_specs=None, cost=1024
    ):
        given, made, linked = len(in_specs), len(out_shape), len(self.last)

        def run(*refs):
            outs = refs[given + linked :]
            outs[made][...] = jnp.zeros(outs[made].shape, F32)
            kernel(*refs[:given], *outs[:made], *outs[made + 1 :])

        out_specs = [VMEM] * made if out_specs is None else out_specs
        run_call = call(
            run,
            [*out_shape, shape((8, LANES), F32)],
            [*in_specs, *[VMEM] * linked],
            scratch,
            aliases,
            [*out_specs, VMEM],
            cost=cost,
        )

        def apply(*args):
            *results, token = run_call(*args, *self.last)
            self.last = [token]
            return results

        return apply


def shape(dims, dtype):
    return jax.ShapeDtypeStruct(dims, dtype)


def swap(value, axis, count, step):
    return lax.ppermute(value, axis, [(i, i ^ step) for i in range(count)])


def far_first(count):
    return [0, *reversed(range(1, count))]


def swaps(values, axis, count, stride=1):
    return [
        swap(value, axis, count, step * stride) if step else value
        for value, step in zip(values, far_first(len(values)))
    ]


def to_column(row):
    return jnp.transpose(jnp.broadcast_to(row, (LANES, row.shape[1])), (1, 0))


def pick_kernel(pieces, pos_hbm, rows_hbm, own_ref, pos, rows, sems):
    tokens, shard_len = pos.shape[1], rows.shape[0]
    size = shard_len // pieces
    head = pltpu.make_async_copy(pos_hbm, pos, sems.at[pieces])
    head.start()
    copies = []
    for piece in range(pieces):
        cut = pl.ds(piece * size, size)
        copies.append(
            pltpu.make_async_copy(rows_hbm.at[0, cut], rows.at[cut], sems.at[piece])
        )
        copies[-1].start()
    offset = lax.axis_index("seq") * shard_len
    head.wait()
    column = to_column(pos[...] - offset)
    lanes = lax.broadcasted_iota(jnp.int32, (tokens, LANES), 1)
    total = None
    for piece in range(pieces):
        select = jnp.concatenate(
            [
                jnp.where(column == lanes + at, 1.0, 0.0).astype(BF16)
                for at in range(piece * size, (piece + 1) * size, LANES)
            ],
            axis=1,
        )
        copies[piece].wait()
        part = jnp.dot(
            select, rows[piece * size : (piece + 1) * size, :], preferred_element_type=F32
        )
        total = part if total is None else total + part
    own_ref[...] = total.astype(BF16)


def load_kernel(
    span_hbm, hidden_ref, gain_ref, proj_ref, resid_ref, weight_hbm,
    stats_ref, projt_ref, residt_ref, gaint_ref, meant_ref, weight_ref,
    span, sems,
):
    load = pltpu.make_async_copy(weight_hbm, weight_ref, sems.at[0])
    head = pltpu.make_async_copy(span_hbm, span, sems.at[1])
    head.start()
    load.start()
    tokens, width = proj_ref.shape[1:]
    for at in range(0, width, LANES):
        cut = slice(at, at + LANES)
        gaint_ref[cut, :] = to_column(gain_ref[:, cut])
        projt_ref[cut, :] = jnp.transpose(proj_ref[0, :, cut].astype(F32), (1, 0))
        residt_ref[cut, :] = jnp.transpose(resid_ref[0, :, cut].astype(F32), (1, 0))
    head.wait()
    start, count = span[0, 0], span[0, 1]
    places = lax.broadcasted_iota(jnp.int32, (hidden_ref.shape[1], 1), 0)
    mask = ((places >= start) & (places < start + count)).astype(F32)
    query = square = cross = jnp.zeros((LANES, tokens), F32)
    for at in range(0, width, LANES):
        cut = slice(at, at + LANES)
        mean = jnp.sum(hidden_ref[0, :, cut].astype(F32) * mask, axis=0, keepdims=True)
        meant = to_column(mean / count.astype(F32))
        meant_ref[cut, :] = meant
        projt = projt_ref[cut, :]
        residt = residt_ref[cut, :]
        query = query + projt * meant
        square = square + projt * projt
        cross = cross + projt * residt
    stats_ref[...] = jnp.zeros(stats_ref.shape, F32)
    for row, value in enumerate((query, square, cross)):
        stats_ref[row : row + 1, :] = jnp.sum(value, axis=0, keepdims=True)
    load.wait()


def norm_kernel(peers, *refs):
    own_refs = refs[:peers]
    stats_ref, weight_ref, gaint_ref, projt_ref, scaledt_ref, sums_ref, pickedt = refs[peers:]
    key_width = own_refs[0].shape[1]
    for at in range(0, key_width, LANES):
        cut = slice(at, at + LANES)
        picked = own_refs[0][:, cut].astype(F32)
        for ref in own_refs[1:]:
            picked = picked + ref[:, cut].astype(F32)
        pickedt[cut, :] = jnp.transpose(picked, (1, 0)).astype(BF16)
    width, tokens = projt_ref.shape
    total = jnp.zeros((LANES, tokens), F32)
    for at in range(0, width, 256):
        cut = slice(at, at + 256)
        normed = jnp.dot(weight_ref[cut, :], pickedt[...], preferred_element_type=F32)
        scaled = normed * gaint_ref[cut, :]
        scaledt_ref[cut, :] = scaled
        terms = scaled * projt_ref[cut, :]
        total = total + terms[:LANES] + terms[LANES:]
    sums_ref[...] = stats_ref[...]
    sums_ref[3:4, :] = jnp.sum(total, axis=0, keepdims=True)


def weight_copy(weight_hbm, weights, sems, peers, share, base, rows, index, skipped=0):
    quarter = weight_hbm.shape[0] // peers
    block = min(rows, 256)
    inner = rows // block
    step = lax.rem(peers - index // inner, peers)
    first = (lax.axis_index("seq") ^ step) * quarter + base + lax.rem(index, inner) * block
    first += lax.rem(lax.axis_index("frame"), share) * (quarter // share)
    place = index - skipped
    return pltpu.make_async_copy(
        weight_hbm.at[pl.ds(pl.multiple_of(first, block), block)],
        weights.at[pl.ds(pl.multiple_of(place * block, block), block)],
        sems.at[place],
    )


def preload_kernel(skipped, count, peers, share, rows, weight_hbm, after_ref, weights_ref, sems):
    del after_ref
    copies = [
        weight_copy(weight_hbm, weights_ref, sems, peers, share, 0, rows, index, skipped)
        for index in range(skipped, skipped + count)
    ]
    for copy in copies:
        copy.start()
    for copy in copies:
        copy.wait()


def gate_kernel(features, peers, *refs):
    sums_refs = refs[:peers]
    projt_ref, residt_ref, scaledt_ref, meant_ref, owner_ref, after_ref = refs[peers : peers + 6]
    del after_ref
    gradt_ref, logit_ref = refs[peers + 6 :]
    sums = sums_refs[0][...]
    for ref in sums_refs[1:]:
        sums = sums + ref[...]
    sum_query, sum_square, sum_resid, sum_norm = (sums[i : i + 1] for i in range(4))
    gate_scale = 4.0 / math.sqrt(features)
    gate = jax.nn.sigmoid(gate_scale * sum_query)
    inv_rms = lax.rsqrt(gate * gate * sum_square / features + EPSILON)
    coef = gate * inv_rms * inv_rms * inv_rms * (gate * sum_norm) / features
    gate_grad = sum_resid + inv_rms * sum_norm - coef * sum_square
    logit = gate_grad * gate * (1.0 - gate) * gate_scale
    logit_ref[...] = jnp.broadcast_to(logit, logit_ref.shape)
    width = projt_ref.shape[0]
    for at in range(0, width, LANES):
        cut = slice(at, at + LANES)
        grad = residt_ref[cut, :] + inv_rms * scaledt_ref[cut, :] - coef * projt_ref[cut, :]
        gradt_ref[cut, :] = (gate * grad + logit * meant_ref[cut, :]).astype(BF16)
    tail = gradt_ref.shape[0] - width
    owner = owner_ref[...].astype(F32)
    gradt_ref[width:, :] = jnp.broadcast_to(owner, (tail, owner.shape[1])).astype(BF16)


def down_kernel(peers, share, base, rows, held, *refs):
    weight_refs = refs[: max(held, 1)]
    gradt_refs = refs[len(weight_refs) : len(weight_refs) + share]
    scratch = list(refs[len(weight_refs) + share :])
    out_refs = [scratch.pop(0) for _ in range(peers)]
    joined = scratch.pop(0)
    block = min(rows, 256)
    inner = rows // block
    total = peers * inner

    def copy(index):
        return weight_copy(weight_refs[0], *scratch, peers, share, base, rows, index)

    if not held:
        for index in range(min(AHEAD, total)):
            copy(index).start()
    width, tokens = joined.shape[0], gradt_refs[0].shape[1]
    for index, ref in enumerate(gradt_refs):
        joined[:, index * tokens : (index + 1) * tokens] = ref[:width, :]
    each = total // len(weight_refs)
    for peer, ref in enumerate(out_refs):
        if held:
            weights = weight_refs[peer * inner // each]
            for part in range(inner):
                at = (peer * inner + part) % each * block
                value = jnp.dot(
                    weights[at : at + block, :], joined[...], preferred_element_type=F32
                )
                ref[part * block : (part + 1) * block, :] = value.astype(BF16)
            continue

        def step(part, carry, peer=peer, ref=ref):
            index = peer * inner + part
            copy(index).wait()

            @pl.when(index + AHEAD < total)
            def _():
                copy(index + AHEAD).start()

            at = pl.multiple_of(index * block, block)
            value = jnp.dot(
                scratch[0][pl.ds(at, block), :], joined[...], preferred_element_type=F32
            )
            ref[pl.ds(pl.multiple_of(part * block, block), block), :] = value.astype(BF16)
            return carry

        lax.fori_loop(0, inner, step, 0)


def ques_kernel(span_hbm, logit_ref, proj_hbm, out_ref, span, proj, sems):
    head = pltpu.make_async_copy(span_hbm, span, sems.at[0])
    load = pltpu.make_async_copy(proj_hbm.at[0], proj, sems.at[1])
    head.start()
    load.start()
    head.wait()
    start, count = span[0, 0], span[0, 1]
    length, width = out_ref.shape[1], out_ref.shape[2]
    places = lax.broadcasted_iota(jnp.int32, (length, LANES), 0)
    mask = ((places >= start) & (places < start + count)).astype(F32)
    column = to_column(logit_ref[0:1, :])
    load.wait()
    for at in range(0, width, LANES):
        cut = slice(at, at + LANES)
        total = jnp.sum(column * proj[:, cut].astype(F32), axis=0, keepdims=True)
        out_ref[0, :, cut] = (mask * total / count.astype(F32)).astype(BF16)


def targets(owner, capacity, share, source):
    tokens = owner.shape[1]
    above = lax.broadcasted_iota(jnp.int32, (tokens, tokens), 0)
    below = lax.broadcasted_iota(jnp.int32, (tokens, tokens), 1)
    earlier = jnp.where((to_column(owner) == owner) & (above < below), 1.0, 0.0)
    rank = jnp.sum(earlier, axis=0, keepdims=True).astype(jnp.int32)
    away = owner ^ lax.axis_index("frame")
    return (away * share + source) * capacity + rank


def place_kernel(capacity, share, pieces, mine, *refs):
    gradt_refs = refs[:share]
    part_refs = refs[share : share + mine]
    out_refs = refs[-pieces:]
    target = jnp.concatenate(
        [
            targets(ref[-16:-15, :].astype(F32).astype(jnp.int32), capacity, share, source)
            for source, ref in enumerate(gradt_refs)
        ],
        axis=1,
    )
    size = out_refs[0].shape[0]
    places = lax.broadcasted_iota(jnp.int32, (size * pieces, target.shape[1]), 0)
    placing = jnp.where(places == target, 1.0, 0.0).astype(BF16)
    total = part_refs[0][...].astype(F32)
    for ref in part_refs[1:]:
        total = total + ref[...].astype(F32)
    placed = lax.dot_general(
        placing, total.astype(BF16), (((1,), (1,)), ((), ())), preferred_element_type=F32
    ).astype(BF16)
    for ref, step in zip(out_refs, far_first(pieces)):
        ref[...] = placed[step * size : (step + 1) * size, :]


def group_kernel(*refs):
    *part_refs, keep_ref, send_ref = refs
    size = part_refs[0].shape[0] // 2
    for ref, step in zip(part_refs, far_first(len(part_refs))):
        cut = slice(step * size, (step + 1) * size)
        keep_ref[cut, :] = ref[:size, :]
        send_ref[cut, :] = ref[size:, :]


def slope(pre_act):
    normal_cdf = 0.5 * (1.0 + lax.erf(pre_act * 0.7071067811865476))
    density = jnp.exp(-0.5 * pre_act * pre_act) * 0.3989422804014327
    return normal_cdf + pre_act * density


def slope_kernel(pieces, pre_hbm, slope_ref, pre, sems):
    rows = pre.shape[0] // pieces
    copies = []
    for piece in range(pieces):
        cut = pl.ds(piece * rows, rows)
        copies.append(pltpu.make_async_copy(pre_hbm.at[0, cut], pre.at[cut], sems.at[piece]))
        copies[-1].start()
    for piece, copy in enumerate(copies):
        copy.wait()
        cut = slice(piece * rows, (piece + 1) * rows)
        slope_ref[cut, :] = slope(pre[cut, :].astype(F32))


def final_kernel(capacity, share, turn, base, *refs):
    part_ref, slope_ref = refs[:2]
    out_hbm, out, sem = refs[-3:]
    rows, slots = out.shape
    part = lax.rem(lax.axis_index("frame") + turn, share) * (slope_ref.shape[0] // share)
    cut = pl.ds(pl.multiple_of(part + base, rows), rows)
    source = lax.broadcasted_iota(jnp.int32, (slots, slots), 0)
    goal = lax.broadcasted_iota(jnp.int32, (slots, slots), 1)
    moved = (goal ^ ((lax.axis_index("frame") ^ turn) * capacity)) == source
    hidden = lax.dot_general(
        part_ref[...],
        jnp.where(moved, 1.0, 0.0).astype(BF16),
        (((0,), (0,)), ((), ())),
        preferred_element_type=F32,
    )
    out[...] = (hidden * slope_ref[cut, :]).astype(BF16)
    store = pltpu.make_async_copy(out, out_hbm.at[0, cut], sem.at[0])
    store.start()
    store.wait()


def chunk_rows(quarter):
    return [quarter // 2] * 2


def body(
    peers,
    owners_count,
    value_grad,
    w_value,
    norm_gain,
    vis_pos,
    frame_owner,
    ques_span,
    vis_proj,
    vis_resid,
    ques_hidden,
    w_down,
    pre_owned,
):
    _, tokens, width = vis_proj.shape
    shard_len, key_width = value_grad.shape[1:]
    length = ques_hidden.shape[1]
    features = peers * width
    slots = pre_owned.shape[2]
    capacity = slots // owners_count
    gain = norm_gain.reshape(1, width)
    owner = frame_owner.reshape(1, tokens)
    row = shape((8, tokens), F32)
    tall = shape((width, tokens), F32)
    dma = pltpu.SemaphoreType.DMA

    pieces = max(1, shard_len // 256)
    own = call(
        functools.partial(pick_kernel, pieces),
        shape((tokens, key_width), BF16),
        [HBM, HBM],
        [
            pltpu.VMEM((1, tokens), jnp.int32),
            pltpu.VMEM((shard_len, key_width), BF16),
            dma((pieces + 1,)),
        ],
        grant=PICK_GRANT,
    )(vis_pos, value_grad)
    own_all = [own] + [swap(own, "seq", peers, k) for k in range(1, peers)]

    stats, projt, residt, gaint, meant, weight = call(
        load_kernel,
        [row, tall, tall, tall, tall, shape(w_value.shape, BF16)],
        [HBM, VMEM, VMEM, VMEM, VMEM, HBM],
        [pltpu.SMEM((1, 2), jnp.int32), dma((2,))],
        grant=LOAD_GRANT,
    )(ques_span, ques_hidden, gain, vis_proj, vis_resid, w_value)

    scaledt, sums = call(
        functools.partial(norm_kernel, peers),
        [tall, row],
        [VMEM] * (peers + 4),
        [pltpu.VMEM((key_width, tokens), BF16)],
    )(*own_all, stats, weight, gaint, projt)
    sums_all = [sums] + [swap(sums, "seq", peers, k) for k in range(1, peers)]

    paired = capacity % 16 == 0 and owners_count % 2 == 0
    share = 2 if paired else 1
    pieces = owners_count // 2 if paired else 1
    chunks = chunk_rows(w_down.shape[0] // peers // share)
    bases = [sum(chunks[:i]) for i in range(len(chunks))]
    chain = Chain()

    def sems(rows, count=peers):
        return dma((count * (rows // min(rows, 256)),))

    def preload(caller, half, after):
        count = peers // 2 * (chunks[0] // min(chunks[0], 256))
        (weights,) = caller(
            functools.partial(preload_kernel, half * count, count, peers, share, chunks[0]),
            [shape((peers // 2 * chunks[0], width), BF16)],
            [HBM, VMEM],
            [sems(chunks[0], peers // 2)],
        )(w_down, after)
        return weights

    preloaded = [preload(call, 0, sums)]
    gradt, logit = chain.call(
        functools.partial(gate_kernel, features, peers),
        [shape((width + 16, tokens), BF16), row],
        [VMEM] * (peers + 5) + [ANY],
    )(*sums_all, projt, residt, scaledt, meant, owner, preloaded[0])
    preloaded.append(preload(chain.call, 1, logit))
    gradts = [gradt] + [swap(gradt, "frame", owners_count, k) for k in range(1, share)]

    def down(index):
        rows = chunks[index]
        weights = [pltpu.VMEM((peers * rows, width), BF16), sems(rows)]
        partial = chain.call(
            functools.partial(
                down_kernel, peers, share, bases[index], rows, 0 if index else len(preloaded)
            ),
            [shape((rows, share * tokens), BF16)] * peers,
            ([HBM] if index else [VMEM] * len(preloaded)) + [VMEM] * share,
            [pltpu.VMEM((width, share * tokens), BF16)] + (weights if index else []),
            cost=2 * peers * rows * width,
        )(*([w_down] if index else preloaded), *gradts)
        return swaps(partial, "seq", peers)

    def place(parts):
        rows = parts[0].shape[0]
        placed = chain.call(
            functools.partial(place_kernel, capacity, share, pieces, len(parts)),
            [shape((slots * share // pieces, rows), BF16)] * pieces,
            [VMEM] * (share + len(parts)),
        )(*gradts, *parts)
        if paired:
            return swaps(placed, "frame", owners_count, 2)
        order = jnp.arange(owners_count) ^ lax.axis_index("frame")
        split = placed[0].reshape(owners_count, capacity, rows)[order]
        split = lax.all_to_all(split, "frame", split_axis=0, concat_axis=0, tiled=True)
        return [split[order].reshape(slots, rows)]

    def group(parts):
        if not paired:
            return parts
        keep, send = chain.call(
            group_kernel,
            [shape((slots, parts[0].shape[1]), BF16)] * 2,
            [VMEM] * pieces,
        )(*parts)
        return [keep, swap(send, "frame", owners_count, 1)]

    def finish(parts, index, turn, held):
        rows = chunks[index]
        return chain.call(
            functools.partial(final_kernel, capacity, share, turn, bases[index]),
            [shape(pre_owned.shape, BF16)],
            [VMEM, VMEM] + [HBM] * len(held),
            [pltpu.VMEM((rows, slots), BF16), dma((1,))],
            {2: 0} if held else None,
            [HBM],
        )(parts[turn], slopes, *held)

    waiting = [down(0), down(1)]
    (slopes,) = chain.call(
        functools.partial(slope_kernel, 4),
        [shape(pre_owned.shape[1:], F32)],
        [HBM],
        [pltpu.VMEM(pre_owned.shape[1:], BF16), dma((4,))],
    )(pre_owned)
    (ques_grad,) = chain.call(
        ques_kernel,
        [shape(ques_hidden.shape, BF16)],
        [HBM, VMEM, HBM],
        [pltpu.SMEM((1, 2), jnp.int32), pltpu.VMEM((tokens, width), BF16), dma((2,))],
        cost=400000000,
    )(ques_span, logit, vis_proj)
    placed = [place(parts) for parts in waiting]
    first = group(placed[0])
    held = finish(first, 0, 0, [])
    second = group(placed[1])
    for turn in range(1, share):
        held = finish(first, 0, turn, held)
    for turn in range(share):
        held = finish(second, 1, turn, held)
    return (held[0], ques_grad)


def solution(mesh):
    in_specs = (
        P("frame", "seq", None),
        P("seq", None),
        P("seq"),
        P("frame", None),
        P("frame", None, None),
        P("frame", None),
        P("frame", None, "seq"),
        P("frame", None, "seq"),
        P("frame", None, "seq"),
        P(None, "seq"),
        P("frame", "seq", None),
    )
    out_specs = (P("frame", "seq", None), P("frame", None, "seq"))
    run = functools.partial(body, mesh.shape["seq"], mesh.shape["frame"])
    return jax.shard_map(run, mesh=mesh, in_specs=in_specs, out_specs=out_specs, check_vma=False)
```

```python
import functools
import math

import jax
import jax.numpy as jnp
from jax import lax
from jax.experimental import pallas as pl
from jax.experimental.pallas import tpu as pltpu
from jax.sharding import PartitionSpec as P

EPSILON = 1e-06
F32 = jnp.float32
BF16 = jnp.bfloat16
LANES = 128
AHEAD = 4
MIB = 1024 * 1024
GRANT, LOAD_GRANT, PICK_GRANT = 40, 46, 53
HBM = pl.BlockSpec(memory_space=pltpu.HBM)
VMEM = pl.BlockSpec(memory_space=pltpu.VMEM)
ANY = pl.BlockSpec(memory_space=pl.ANY)


def call(
    kernel, out_shape, in_specs, scratch=(), aliases=None, out_specs=None, grant=GRANT, cost=1024
):
    return pl.pallas_call(
        kernel,
        out_shape=out_shape,
        in_specs=in_specs,
        out_specs=jax.tree.map(lambda _: VMEM, out_shape) if out_specs is None else out_specs,
        scratch_shapes=list(scratch),
        input_output_aliases=aliases or {},
        compiler_params=pltpu.CompilerParams(vmem_limit_bytes=grant * MIB),
        cost_estimate=pl.CostEstimate(flops=256 * cost, bytes_accessed=cost, transcendentals=0),
    )


class Chain:
    def __init__(self):
        self.last = []

    def call(
        self,
        kernel,
        out_shape,
        in_specs,
        scratch=(),
        aliases=None,
        out_specs=None,
        cost=1024,
        final=False,
    ):
        given, made, linked = len(in_specs), len(out_shape), len(self.last)
        marks = [] if final else [shape((8, LANES), F32)]

        def run(*refs):
            outs = refs[given + linked :]
            for mark in outs[made : made + len(marks)]:
                mark[...] = jnp.zeros(mark.shape, F32)
            kernel(*refs[:given], *outs[:made], *outs[made + len(marks) :])

        out_specs = [VMEM] * made if out_specs is None else out_specs
        run_call = call(
            run,
            [*out_shape, *marks],
            [*in_specs, *[VMEM] * linked],
            scratch,
            aliases,
            [*out_specs, *[VMEM] * len(marks)],
            cost=cost,
        )

        def apply(*args):
            results = run_call(*args, *self.last)
            self.last = list(results[made:])
            return list(results[:made])

        return apply


def shape(dims, dtype):
    return jax.ShapeDtypeStruct(dims, dtype)


def swap(value, axis, count, step):
    return lax.ppermute(value, axis, [(i, i ^ step) for i in range(count)])


def far_first(count):
    return [0, *reversed(range(1, count))]


def swaps(values, axis, count, stride=1):
    return [
        swap(value, axis, count, step * stride) if step else value
        for value, step in zip(values, far_first(len(values)))
    ]


def to_column(row):
    return jnp.transpose(jnp.broadcast_to(row, (LANES, row.shape[1])), (1, 0))


def pick_kernel(pieces, pos_hbm, rows_hbm, own_ref, pos, rows, sems):
    tokens, shard_len = pos.shape[1], rows.shape[0]
    size = shard_len // pieces
    head = pltpu.make_async_copy(pos_hbm, pos, sems.at[pieces])
    head.start()
    copies = []
    for piece in range(pieces):
        cut = pl.ds(piece * size, size)
        copies.append(
            pltpu.make_async_copy(rows_hbm.at[0, cut], rows.at[cut], sems.at[piece])
        )
        copies[-1].start()
    offset = lax.axis_index("seq") * shard_len
    head.wait()
    column = to_column(pos[...] - offset)
    lanes = lax.broadcasted_iota(jnp.int32, (tokens, LANES), 1)
    total = None
    for piece in range(pieces):
        select = jnp.concatenate(
            [
                jnp.where(column == lanes + at, 1.0, 0.0).astype(BF16)
                for at in range(piece * size, (piece + 1) * size, LANES)
            ],
            axis=1,
        )
        copies[piece].wait()
        part = jnp.dot(
            select, rows[piece * size : (piece + 1) * size, :], preferred_element_type=F32
        )
        total = part if total is None else total + part
    own_ref[...] = total.astype(BF16)


def load_kernel(
    span_hbm, hidden_ref, gain_ref, proj_ref, resid_ref, weight_hbm,
    stats_ref, projt_ref, residt_ref, gaint_ref, meant_ref, weight_ref,
    span, sems,
):
    load = pltpu.make_async_copy(weight_hbm, weight_ref, sems.at[0])
    head = pltpu.make_async_copy(span_hbm, span, sems.at[1])
    head.start()
    load.start()
    tokens, width = proj_ref.shape[1:]
    for at in range(0, width, LANES):
        cut = slice(at, at + LANES)
        gaint_ref[cut, :] = to_column(gain_ref[:, cut])
        projt_ref[cut, :] = jnp.transpose(proj_ref[0, :, cut], (1, 0)).astype(F32)
        residt_ref[cut, :] = jnp.transpose(resid_ref[0, :, cut], (1, 0)).astype(F32)
    head.wait()
    start, count = span[0, 0], span[0, 1]
    places = lax.broadcasted_iota(jnp.int32, (hidden_ref.shape[1], 1), 0)
    mask = ((places >= start) & (places < start + count)).astype(F32)
    query = square = cross = jnp.zeros((LANES, tokens), F32)
    for at in range(0, width, LANES):
        cut = slice(at, at + LANES)
        mean = jnp.sum(hidden_ref[0, :, cut].astype(F32) * mask, axis=0, keepdims=True)
        meant = to_column(mean / count.astype(F32))
        meant_ref[cut, :] = meant
        projt = projt_ref[cut, :]
        residt = residt_ref[cut, :]
        query = query + projt * meant
        square = square + projt * projt
        cross = cross + projt * residt
    stats_ref[...] = jnp.zeros(stats_ref.shape, F32)
    for row, value in enumerate((query, square, cross)):
        stats_ref[row : row + 1, :] = jnp.sum(value, axis=0, keepdims=True)
    load.wait()


def norm_kernel(peers, *refs):
    own_refs = refs[:peers]
    stats_ref, weight_ref, gaint_ref, projt_ref, scaledt_ref, sums_ref, pickedt = refs[peers:]
    key_width = own_refs[0].shape[1]
    for at in range(0, key_width, LANES):
        cut = slice(at, at + LANES)
        picked = own_refs[0][:, cut].astype(F32)
        for ref in own_refs[1:]:
            picked = picked + ref[:, cut].astype(F32)
        pickedt[cut, :] = jnp.transpose(picked, (1, 0)).astype(BF16)
    width, tokens = projt_ref.shape
    total = jnp.zeros((LANES, tokens), F32)
    for at in range(0, width, 256):
        cut = slice(at, at + 256)
        normed = jnp.dot(weight_ref[cut, :], pickedt[...], preferred_element_type=F32)
        scaled = normed * gaint_ref[cut, :]
        scaledt_ref[cut, :] = scaled
        terms = scaled * projt_ref[cut, :]
        total = total + terms[:LANES] + terms[LANES:]
    sums_ref[...] = stats_ref[...]
    sums_ref[3:4, :] = jnp.sum(total, axis=0, keepdims=True)


def weight_copy(weight_hbm, weights, sems, peers, share, base, rows, index, skipped=0):
    quarter = weight_hbm.shape[0] // peers
    block = min(rows, 256)
    inner = rows // block
    step = lax.rem(peers - index // inner, peers)
    first = (lax.axis_index("seq") ^ step) * quarter + base + lax.rem(index, inner) * block
    first += lax.rem(lax.axis_index("frame"), share) * (quarter // share)
    place = index - skipped
    return pltpu.make_async_copy(
        weight_hbm.at[pl.ds(pl.multiple_of(first, block), block)],
        weights.at[pl.ds(pl.multiple_of(place * block, block), block)],
        sems.at[place],
    )


def preload_kernel(skipped, count, peers, share, rows, weight_hbm, after_ref, weights_ref, sems):
    del after_ref
    copies = [
        weight_copy(weight_hbm, weights_ref, sems, peers, share, 0, rows, index, skipped)
        for index in range(skipped, skipped + count)
    ]
    for copy in copies:
        copy.start()
    for copy in copies:
        copy.wait()


def gate_kernel(features, peers, *refs):
    sums_refs = refs[:peers]
    projt_ref, residt_ref, scaledt_ref, meant_ref, owner_ref, after_ref = refs[peers : peers + 6]
    del after_ref
    gradt_ref, logit_ref = refs[peers + 6 :]
    sums = sums_refs[0][...]
    for ref in sums_refs[1:]:
        sums = sums + ref[...]
    sum_query, sum_square, sum_resid, sum_norm = (sums[i : i + 1] for i in range(4))
    gate_scale = 4.0 / math.sqrt(features)
    gate = jax.nn.sigmoid(gate_scale * sum_query)
    inv_rms = lax.rsqrt(gate * gate * sum_square / features + EPSILON)
    coef = gate * inv_rms * inv_rms * inv_rms * (gate * sum_norm) / features
    gate_grad = sum_resid + inv_rms * sum_norm - coef * sum_square
    logit = gate_grad * gate * (1.0 - gate) * gate_scale
    logit_ref[...] = jnp.broadcast_to(logit, logit_ref.shape)
    width = projt_ref.shape[0]
    for at in range(0, width, LANES):
        cut = slice(at, at + LANES)
        grad = residt_ref[cut, :] + inv_rms * scaledt_ref[cut, :] - coef * projt_ref[cut, :]
        gradt_ref[cut, :] = (gate * grad + logit * meant_ref[cut, :]).astype(BF16)
    tail = gradt_ref.shape[0] - width
    owner = owner_ref[...].astype(F32)
    gradt_ref[width:, :] = jnp.broadcast_to(owner, (tail, owner.shape[1])).astype(BF16)


def down_kernel(peers, share, base, rows, held, *refs):
    weight_refs = refs[: max(held, 1)]
    gradt_refs = refs[len(weight_refs) : len(weight_refs) + share]
    scratch = list(refs[len(weight_refs) + share :])
    out_refs = [scratch.pop(0) for _ in range(peers)]
    joined = scratch.pop(0)
    block = min(rows, 256)
    inner = rows // block
    total = peers * inner

    def copy(index):
        return weight_copy(weight_refs[0], *scratch, peers, share, base, rows, index)

    if not held:
        for index in range(min(AHEAD, total)):
            copy(index).start()
    width, tokens = joined.shape[0], gradt_refs[0].shape[1]
    for index, ref in enumerate(gradt_refs):
        joined[:, index * tokens : (index + 1) * tokens] = ref[:width, :]
    each = total // len(weight_refs)
    for peer, ref in enumerate(out_refs):
        if held:
            weights = weight_refs[peer * inner // each]
            for part in range(inner):
                at = (peer * inner + part) % each * block
                value = jnp.dot(
                    weights[at : at + block, :], joined[...], preferred_element_type=F32
                )
                ref[part * block : (part + 1) * block, :] = value.astype(BF16)
            continue

        def step(part, carry, peer=peer, ref=ref):
            index = peer * inner + part
            copy(index).wait()

            @pl.when(index + AHEAD < total)
            def _():
                copy(index + AHEAD).start()

            at = pl.multiple_of(index * block, block)
            value = jnp.dot(
                scratch[0][pl.ds(at, block), :], joined[...], preferred_element_type=F32
            )
            ref[pl.ds(pl.multiple_of(part * block, block), block), :] = value.astype(BF16)
            return carry

        lax.fori_loop(0, inner, step, 0)


def ques_kernel(span_hbm, logit_ref, proj_hbm, out_ref, span, proj, sems):
    head = pltpu.make_async_copy(span_hbm, span, sems.at[0])
    load = pltpu.make_async_copy(proj_hbm.at[0], proj, sems.at[1])
    head.start()
    load.start()
    head.wait()
    start, count = span[0, 0], span[0, 1]
    length, width = out_ref.shape[1], out_ref.shape[2]
    places = lax.broadcasted_iota(jnp.int32, (length, LANES), 0)
    mask = ((places >= start) & (places < start + count)).astype(F32)
    column = to_column(logit_ref[0:1, :])
    load.wait()
    for at in range(0, width, LANES):
        cut = slice(at, at + LANES)
        total = jnp.sum(column * proj[:, cut].astype(F32), axis=0, keepdims=True)
        out_ref[0, :, cut] = (mask * total / count.astype(F32)).astype(BF16)


def targets(owner, capacity, share, source):
    tokens = owner.shape[1]
    above = lax.broadcasted_iota(jnp.int32, (tokens, tokens), 0)
    below = lax.broadcasted_iota(jnp.int32, (tokens, tokens), 1)
    earlier = jnp.where((to_column(owner) == owner) & (above < below), 1.0, 0.0)
    rank = jnp.sum(earlier, axis=0, keepdims=True).astype(jnp.int32)
    away = owner ^ lax.axis_index("frame")
    return (away * share + source) * capacity + rank


def place_kernel(capacity, share, pieces, mine, *refs):
    gradt_refs = refs[:share]
    part_refs = refs[share : share + mine]
    out_refs = refs[-pieces:]
    target = jnp.concatenate(
        [
            targets(ref[-16:-15, :].astype(F32).astype(jnp.int32), capacity, share, source)
            for source, ref in enumerate(gradt_refs)
        ],
        axis=1,
    )
    size = out_refs[0].shape[0]
    places = lax.broadcasted_iota(jnp.int32, (size * pieces, target.shape[1]), 0)
    placing = jnp.where(places == target, 1.0, 0.0).astype(BF16)
    total = part_refs[0][...].astype(F32)
    for ref in part_refs[1:]:
        total = total + ref[...].astype(F32)
    placed = lax.dot_general(
        placing, total.astype(BF16), (((1,), (1,)), ((), ())), preferred_element_type=F32
    ).astype(BF16)
    for ref, step in zip(out_refs, far_first(pieces)):
        ref[...] = placed[step * size : (step + 1) * size, :]


def group_kernel(*refs):
    *part_refs, keep_ref, send_ref = refs
    size = part_refs[0].shape[0] // 2
    for ref, step in zip(part_refs, far_first(len(part_refs))):
        cut = slice(step * size, (step + 1) * size)
        keep_ref[cut, :] = ref[:size, :]
        send_ref[cut, :] = ref[size:, :]


def slope(pre_act):
    normal_cdf = 0.5 * (1.0 + lax.erf(pre_act * 0.7071067811865476))
    density = jnp.exp(-0.5 * pre_act * pre_act) * 0.3989422804014327
    return normal_cdf + pre_act * density


def slope_kernel(pieces, pre_hbm, slope_ref, pre, sems):
    rows = pre.shape[0] // pieces
    copies = []
    for piece in range(pieces):
        cut = pl.ds(piece * rows, rows)
        copies.append(pltpu.make_async_copy(pre_hbm.at[0, cut], pre.at[cut], sems.at[piece]))
        copies[-1].start()
    for piece, copy in enumerate(copies):
        copy.wait()
        cut = slice(piece * rows, (piece + 1) * rows)
        slope_ref[cut, :] = slope(pre[cut, :].astype(F32))


def final_kernel(capacity, share, turn, base, *refs):
    part_ref, slope_ref = refs[:2]
    out_hbm, out, sem = refs[-3:]
    rows, slots = out.shape
    part = lax.rem(lax.axis_index("frame") + turn, share) * (slope_ref.shape[0] // share)
    cut = pl.ds(pl.multiple_of(part + base, rows), rows)
    source = lax.broadcasted_iota(jnp.int32, (slots, slots), 0)
    goal = lax.broadcasted_iota(jnp.int32, (slots, slots), 1)
    moved = (goal ^ ((lax.axis_index("frame") ^ turn) * capacity)) == source
    hidden = lax.dot_general(
        part_ref[...],
        jnp.where(moved, 1.0, 0.0).astype(BF16),
        (((0,), (0,)), ((), ())),
        preferred_element_type=F32,
    )
    out[...] = (hidden * slope_ref[cut, :]).astype(BF16)
    store = pltpu.make_async_copy(out, out_hbm.at[0, cut], sem.at[0])
    store.start()
    store.wait()


def chunk_rows(quarter):
    return [quarter // 2] * 2


def body(
    peers,
    owners_count,
    value_grad,
    w_value,
    norm_gain,
    vis_pos,
    frame_owner,
    ques_span,
    vis_proj,
    vis_resid,
    ques_hidden,
    w_down,
    pre_owned,
):
    _, tokens, width = vis_proj.shape
    shard_len, key_width = value_grad.shape[1:]
    length = ques_hidden.shape[1]
    features = peers * width
    slots = pre_owned.shape[2]
    capacity = slots // owners_count
    gain = norm_gain.reshape(1, width)
    owner = frame_owner.reshape(1, tokens)
    row = shape((8, tokens), F32)
    tall = shape((width, tokens), F32)
    dma = pltpu.SemaphoreType.DMA

    pieces = max(1, shard_len // 256)
    own = call(
        functools.partial(pick_kernel, pieces),
        shape((tokens, key_width), BF16),
        [HBM, HBM],
        [
            pltpu.VMEM((1, tokens), jnp.int32),
            pltpu.VMEM((shard_len, key_width), BF16),
            dma((pieces + 1,)),
        ],
        grant=PICK_GRANT,
    )(vis_pos, value_grad)
    own_all = [own] + [swap(own, "seq", peers, k) for k in range(1, peers)]

    stats, projt, residt, gaint, meant, weight = call(
        load_kernel,
        [row, tall, tall, tall, tall, shape(w_value.shape, BF16)],
        [HBM, VMEM, VMEM, VMEM, VMEM, HBM],
        [pltpu.SMEM((1, 2), jnp.int32), dma((2,))],
        grant=LOAD_GRANT,
    )(ques_span, ques_hidden, gain, vis_proj, vis_resid, w_value)

    scaledt, sums = call(
        functools.partial(norm_kernel, peers),
        [tall, row],
        [VMEM] * (peers + 4),
        [pltpu.VMEM((key_width, tokens), BF16)],
    )(*own_all, stats, weight, gaint, projt)
    sums_all = [sums] + [swap(sums, "seq", peers, k) for k in range(1, peers)]

    paired = capacity % 16 == 0 and owners_count % 2 == 0
    share = 2 if paired else 1
    pieces = owners_count // 2 if paired else 1
    chunks = chunk_rows(w_down.shape[0] // peers // share)
    bases = [sum(chunks[:i]) for i in range(len(chunks))]
    chain = Chain()

    def sems(rows, count=peers):
        return dma((count * (rows // min(rows, 256)),))

    def preload(caller, half, after):
        count = peers // 2 * (chunks[0] // min(chunks[0], 256))
        (weights,) = caller(
            functools.partial(preload_kernel, half * count, count, peers, share, chunks[0]),
            [shape((peers // 2 * chunks[0], width), BF16)],
            [HBM, VMEM],
            [sems(chunks[0], peers // 2)],
        )(w_down, after)
        return weights

    preloaded = [preload(call, 0, sums)]
    gradt, logit = chain.call(
        functools.partial(gate_kernel, features, peers),
        [shape((width + 16, tokens), BF16), row],
        [VMEM] * (peers + 5) + [ANY],
    )(*sums_all, projt, residt, scaledt, meant, owner, preloaded[0])
    preloaded.append(preload(chain.call, 1, logit))
    gradts = [gradt] + [swap(gradt, "frame", owners_count, k) for k in range(1, share)]

    def down(index):
        rows = chunks[index]
        weights = [pltpu.VMEM((peers * rows, width), BF16), sems(rows)]
        partial = chain.call(
            functools.partial(
                down_kernel, peers, share, bases[index], rows, 0 if index else len(preloaded)
            ),
            [shape((rows, share * tokens), BF16)] * peers,
            ([HBM] if index else [VMEM] * len(preloaded)) + [VMEM] * share,
            [pltpu.VMEM((width, share * tokens), BF16)] + (weights if index else []),
            cost=2 * peers * rows * width,
        )(*([w_down] if index else preloaded), *gradts)
        return swaps(partial, "seq", peers)

    def place(parts):
        rows = parts[0].shape[0]
        placed = chain.call(
            functools.partial(place_kernel, capacity, share, pieces, len(parts)),
            [shape((slots * share // pieces, rows), BF16)] * pieces,
            [VMEM] * (share + len(parts)),
        )(*gradts, *parts)
        if paired:
            return swaps(placed, "frame", owners_count, 2)
        order = jnp.arange(owners_count) ^ lax.axis_index("frame")
        split = placed[0].reshape(owners_count, capacity, rows)[order]
        split = lax.all_to_all(split, "frame", split_axis=0, concat_axis=0, tiled=True)
        return [split[order].reshape(slots, rows)]

    def group(parts):
        if not paired:
            return parts
        keep, send = chain.call(
            group_kernel,
            [shape((slots, parts[0].shape[1]), BF16)] * 2,
            [VMEM] * pieces,
        )(*parts)
        return [keep, swap(send, "frame", owners_count, 1)]

    def finish(parts, index, turn, held):
        rows = chunks[index]
        return chain.call(
            functools.partial(final_kernel, capacity, share, turn, bases[index]),
            [shape(pre_owned.shape, BF16)],
            [VMEM, VMEM] + [HBM] * len(held),
            [pltpu.VMEM((rows, slots), BF16), dma((1,))],
            {2: 0} if held else None,
            [HBM],
            final=index == len(chunks) - 1 and turn == share - 1,
        )(parts[turn], slopes, *held)

    waiting = [down(0), down(1)]
    placed = [place(parts) for parts in waiting]
    first = group(placed[0])
    (slopes,) = chain.call(
        functools.partial(slope_kernel, 4),
        [shape(pre_owned.shape[1:], F32)],
        [HBM],
        [pltpu.VMEM(pre_owned.shape[1:], BF16), dma((4,))],
    )(pre_owned)
    (ques_grad,) = chain.call(
        ques_kernel,
        [shape(ques_hidden.shape, BF16)],
        [HBM, VMEM, HBM],
        [pltpu.SMEM((1, 2), jnp.int32), pltpu.VMEM((tokens, width), BF16), dma((2,))],
    )(ques_span, logit, vis_proj)
    held = finish(first, 0, 0, [])
    second = group(placed[1])
    for turn in range(1, share):
        held = finish(first, 0, turn, held)
    for turn in range(share):
        held = finish(second, 1, turn, held)
    return (held[0], ques_grad)


def solution(mesh):
    in_specs = (
        P("frame", "seq", None),
        P("seq", None),
        P("seq"),
        P("frame", None),
        P("frame", None, None),
        P("frame", None),
        P("frame", None, "seq"),
        P("frame", None, "seq"),
        P("frame", None, "seq"),
        P(None, "seq"),
        P("frame", "seq", None),
    )
    out_specs = (P("frame", "seq", None), P("frame", None, "seq"))
    run = functools.partial(body, mesh.shape["seq"], mesh.shape["frame"])
    return jax.shard_map(run, mesh=mesh, in_specs=in_specs, out_specs=out_specs, check_vma=False)
```

```python
import functools
import math

import jax
import jax.numpy as jnp
from jax import lax
from jax.experimental import pallas as pl
from jax.experimental.pallas import tpu as pltpu
from jax.sharding import PartitionSpec as P

EPSILON = 1e-06
F32 = jnp.float32
BF16 = jnp.bfloat16
LANES = 128
AHEAD = 4
MIB = 1024 * 1024
GRANT, LOAD_GRANT, PICK_GRANT = 40, 46, 53
HBM = pl.BlockSpec(memory_space=pltpu.HBM)
VMEM = pl.BlockSpec(memory_space=pltpu.VMEM)
ANY = pl.BlockSpec(memory_space=pl.ANY)


def call(
    kernel, out_shape, in_specs, scratch=(), aliases=None, out_specs=None, grant=GRANT, cost=1024
):
    return pl.pallas_call(
        kernel,
        out_shape=out_shape,
        in_specs=in_specs,
        out_specs=jax.tree.map(lambda _: VMEM, out_shape) if out_specs is None else out_specs,
        scratch_shapes=list(scratch),
        input_output_aliases=aliases or {},
        compiler_params=pltpu.CompilerParams(vmem_limit_bytes=grant * MIB),
        cost_estimate=pl.CostEstimate(flops=256 * cost, bytes_accessed=cost, transcendentals=0),
    )


class Chain:
    def __init__(self):
        self.last = []

    def call(
        self,
        kernel,
        out_shape,
        in_specs,
        scratch=(),
        aliases=None,
        out_specs=None,
        cost=1024,
        final=False,
    ):
        given, made, linked = len(in_specs), len(out_shape), len(self.last)
        marks = [] if final else [shape((8, LANES), F32)]

        def run(*refs):
            outs = refs[given + linked :]
            for mark in outs[made : made + len(marks)]:
                mark[...] = jnp.zeros(mark.shape, F32)
            kernel(*refs[:given], *outs[:made], *outs[made + len(marks) :])

        out_specs = [VMEM] * made if out_specs is None else out_specs
        run_call = call(
            run,
            [*out_shape, *marks],
            [*in_specs, *[VMEM] * linked],
            scratch,
            aliases,
            [*out_specs, *[VMEM] * len(marks)],
            cost=cost,
        )

        def apply(*args):
            results = run_call(*args, *self.last)
            self.last = list(results[made:])
            return list(results[:made])

        return apply


def shape(dims, dtype):
    return jax.ShapeDtypeStruct(dims, dtype)


def swap(value, axis, count, step):
    return lax.ppermute(value, axis, [(i, i ^ step) for i in range(count)])


def far_first(count):
    return [0, *reversed(range(1, count))]


def swaps(values, axis, count, stride=1):
    return [
        swap(value, axis, count, step * stride) if step else value
        for value, step in zip(values, far_first(len(values)))
    ]


def to_column(row):
    return jnp.transpose(jnp.broadcast_to(row, (LANES, row.shape[1])), (1, 0))


def pick_kernel(pieces, pos_hbm, rows_hbm, own_ref, pos, rows, sems):
    tokens, shard_len = pos.shape[1], rows.shape[0]
    size = shard_len // pieces
    head = pltpu.make_async_copy(pos_hbm, pos, sems.at[pieces])
    head.start()
    copies = []
    for piece in range(pieces):
        cut = pl.ds(piece * size, size)
        copies.append(
            pltpu.make_async_copy(rows_hbm.at[0, cut], rows.at[cut], sems.at[piece])
        )
        copies[-1].start()
    offset = lax.axis_index("seq") * shard_len
    head.wait()
    column = to_column(pos[...] - offset)
    lanes = lax.broadcasted_iota(jnp.int32, (tokens, LANES), 1)
    total = None
    for piece in range(pieces):
        select = jnp.concatenate(
            [
                jnp.where(column == lanes + at, 1.0, 0.0).astype(BF16)
                for at in range(piece * size, (piece + 1) * size, LANES)
            ],
            axis=1,
        )
        copies[piece].wait()
        part = jnp.dot(
            select, rows[piece * size : (piece + 1) * size, :], preferred_element_type=F32
        )
        total = part if total is None else total + part
    own_ref[...] = total.astype(BF16)


def load_kernel(
    span_hbm, hidden_ref, gain_ref, proj_ref, resid_ref, weight_hbm,
    stats_ref, projt_ref, residt_ref, gaint_ref, meant_ref, weight_ref,
    span, sems,
):
    load = pltpu.make_async_copy(weight_hbm, weight_ref, sems.at[0])
    head = pltpu.make_async_copy(span_hbm, span, sems.at[1])
    head.start()
    load.start()
    tokens, width = proj_ref.shape[1:]
    for at in range(0, width, LANES):
        cut = slice(at, at + LANES)
        gaint_ref[cut, :] = to_column(gain_ref[:, cut])
        projt_ref[cut, :] = jnp.transpose(proj_ref[0, :, cut], (1, 0)).astype(F32)
        residt_ref[cut, :] = jnp.transpose(resid_ref[0, :, cut], (1, 0)).astype(F32)
    head.wait()
    start, count = span[0, 0], span[0, 1]
    places = lax.broadcasted_iota(jnp.int32, (hidden_ref.shape[1], 1), 0)
    mask = ((places >= start) & (places < start + count)).astype(F32)
    query = square = cross = jnp.zeros((LANES, tokens), F32)
    for at in range(0, width, LANES):
        cut = slice(at, at + LANES)
        mean = jnp.sum(hidden_ref[0, :, cut].astype(F32) * mask, axis=0, keepdims=True)
        meant = to_column(mean / count.astype(F32))
        meant_ref[cut, :] = meant
        projt = projt_ref[cut, :]
        residt = residt_ref[cut, :]
        query = query + projt * meant
        square = square + projt * projt
        cross = cross + projt * residt
    stats_ref[...] = jnp.zeros(stats_ref.shape, F32)
    for row, value in enumerate((query, square, cross)):
        stats_ref[row : row + 1, :] = jnp.sum(value, axis=0, keepdims=True)
    load.wait()


def norm_kernel(peers, *refs):
    own_refs = refs[:peers]
    stats_ref, weight_ref, gaint_ref, projt_ref, scaledt_ref, sums_ref, pickedt = refs[peers:]
    key_width = own_refs[0].shape[1]
    for at in range(0, key_width, LANES):
        cut = slice(at, at + LANES)
        picked = own_refs[0][:, cut].astype(F32)
        for ref in own_refs[1:]:
            picked = picked + ref[:, cut].astype(F32)
        pickedt[cut, :] = jnp.transpose(picked, (1, 0)).astype(BF16)
    width, tokens = projt_ref.shape
    total = jnp.zeros((LANES, tokens), F32)
    for at in range(0, width, 256):
        cut = slice(at, at + 256)
        normed = jnp.dot(weight_ref[cut, :], pickedt[...], preferred_element_type=F32)
        scaled = normed * gaint_ref[cut, :]
        scaledt_ref[cut, :] = scaled
        terms = scaled * projt_ref[cut, :]
        total = total + terms[:LANES] + terms[LANES:]
    sums_ref[...] = stats_ref[...]
    sums_ref[3:4, :] = jnp.sum(total, axis=0, keepdims=True)


def weight_copy(weight_hbm, weights, sems, peers, share, base, rows, index, skipped=0):
    quarter = weight_hbm.shape[0] // peers
    block = min(rows, 256)
    inner = rows // block
    step = lax.rem(peers - index // inner, peers)
    first = (lax.axis_index("seq") ^ step) * quarter + base + lax.rem(index, inner) * block
    first += lax.rem(lax.axis_index("frame"), share) * (quarter // share)
    place = index - skipped
    return pltpu.make_async_copy(
        weight_hbm.at[pl.ds(pl.multiple_of(first, block), block)],
        weights.at[pl.ds(pl.multiple_of(place * block, block), block)],
        sems.at[place],
    )


def preload_kernel(skipped, count, peers, share, rows, weight_hbm, after_ref, weights_ref, sems):
    del after_ref
    copies = [
        weight_copy(weight_hbm, weights_ref, sems, peers, share, 0, rows, index, skipped)
        for index in range(skipped, skipped + count)
    ]
    for copy in copies:
        copy.start()
    for copy in copies:
        copy.wait()


def gate_kernel(features, peers, *refs):
    sums_refs = refs[:peers]
    projt_ref, residt_ref, scaledt_ref, meant_ref, owner_ref, after_ref = refs[peers : peers + 6]
    del after_ref
    gradt_ref, logit_ref = refs[peers + 6 :]
    sums = sums_refs[0][...]
    for ref in sums_refs[1:]:
        sums = sums + ref[...]
    sum_query, sum_square, sum_resid, sum_norm = (sums[i : i + 1] for i in range(4))
    gate_scale = 4.0 / math.sqrt(features)
    gate = jax.nn.sigmoid(gate_scale * sum_query)
    inv_rms = lax.rsqrt(gate * gate * sum_square / features + EPSILON)
    coef = gate * inv_rms * inv_rms * inv_rms * (gate * sum_norm) / features
    gate_grad = sum_resid + inv_rms * sum_norm - coef * sum_square
    logit = gate_grad * gate * (1.0 - gate) * gate_scale
    logit_ref[...] = jnp.broadcast_to(logit, logit_ref.shape)
    width = projt_ref.shape[0]
    for at in range(0, width, LANES):
        cut = slice(at, at + LANES)
        grad = residt_ref[cut, :] + inv_rms * scaledt_ref[cut, :] - coef * projt_ref[cut, :]
        gradt_ref[cut, :] = (gate * grad + logit * meant_ref[cut, :]).astype(BF16)
    tail = gradt_ref.shape[0] - width
    owner = owner_ref[...].astype(F32)
    gradt_ref[width:, :] = jnp.broadcast_to(owner, (tail, owner.shape[1])).astype(BF16)


def down_kernel(peers, share, base, rows, held, *refs):
    weight_refs = refs[: max(held, 1)]
    gradt_refs = refs[len(weight_refs) : len(weight_refs) + share]
    scratch = list(refs[len(weight_refs) + share :])
    out_refs = [scratch.pop(0) for _ in range(peers)]
    joined = scratch.pop(0)
    block = min(rows, 256)
    inner = rows // block
    total = peers * inner

    def copy(index):
        return weight_copy(weight_refs[0], *scratch, peers, share, base, rows, index)

    if not held:
        for index in range(min(AHEAD, total)):
            copy(index).start()
    width, tokens = joined.shape[0], gradt_refs[0].shape[1]
    for index, ref in enumerate(gradt_refs):
        joined[:, index * tokens : (index + 1) * tokens] = ref[:width, :]
    each = total // len(weight_refs)
    for peer, ref in enumerate(out_refs):
        if held:
            weights = weight_refs[peer * inner // each]
            for part in range(inner):
                at = (peer * inner + part) % each * block
                value = jnp.dot(
                    weights[at : at + block, :], joined[...], preferred_element_type=F32
                )
                ref[part * block : (part + 1) * block, :] = value.astype(BF16)
            continue

        def step(part, carry, peer=peer, ref=ref):
            index = peer * inner + part
            copy(index).wait()

            @pl.when(index + AHEAD < total)
            def _():
                copy(index + AHEAD).start()

            at = pl.multiple_of(index * block, block)
            value = jnp.dot(
                scratch[0][pl.ds(at, block), :], joined[...], preferred_element_type=F32
            )
            ref[pl.ds(pl.multiple_of(part * block, block), block), :] = value.astype(BF16)
            return carry

        lax.fori_loop(0, inner, step, 0)


def ques_kernel(span_hbm, logit_ref, proj_hbm, out_ref, span, proj, sems):
    head = pltpu.make_async_copy(span_hbm, span, sems.at[0])
    load = pltpu.make_async_copy(proj_hbm.at[0], proj, sems.at[1])
    head.start()
    load.start()
    head.wait()
    start, count = span[0, 0], span[0, 1]
    length, width = out_ref.shape[1], out_ref.shape[2]
    places = lax.broadcasted_iota(jnp.int32, (length, LANES), 0)
    mask = ((places >= start) & (places < start + count)).astype(F32)
    column = to_column(logit_ref[0:1, :])
    load.wait()
    for at in range(0, width, LANES):
        cut = slice(at, at + LANES)
        total = jnp.sum(column * proj[:, cut].astype(F32), axis=0, keepdims=True)
        out_ref[0, :, cut] = (mask * total / count.astype(F32)).astype(BF16)


def targets(owner, capacity, share, source):
    tokens = owner.shape[1]
    above = lax.broadcasted_iota(jnp.int32, (tokens, tokens), 0)
    below = lax.broadcasted_iota(jnp.int32, (tokens, tokens), 1)
    earlier = jnp.where((to_column(owner) == owner) & (above < below), 1.0, 0.0)
    rank = jnp.sum(earlier, axis=0, keepdims=True).astype(jnp.int32)
    away = owner ^ lax.axis_index("frame")
    return (away * share + source) * capacity + rank


def place_kernel(capacity, share, pieces, mine, *refs):
    gradt_refs = refs[:share]
    part_refs = refs[share : share + mine]
    out_refs = refs[-pieces:]
    target = jnp.concatenate(
        [
            targets(ref[-16:-15, :].astype(F32).astype(jnp.int32), capacity, share, source)
            for source, ref in enumerate(gradt_refs)
        ],
        axis=1,
    )
    size = out_refs[0].shape[0]
    places = lax.broadcasted_iota(jnp.int32, (size * pieces, target.shape[1]), 0)
    placing = jnp.where(places == target, 1.0, 0.0).astype(BF16)
    total = part_refs[0][...].astype(F32)
    for ref in part_refs[1:]:
        total = total + ref[...].astype(F32)
    placed = lax.dot_general(
        placing, total.astype(BF16), (((1,), (1,)), ((), ())), preferred_element_type=F32
    ).astype(BF16)
    for ref, step in zip(out_refs, far_first(pieces)):
        ref[...] = placed[step * size : (step + 1) * size, :]


def group_kernel(*refs):
    *part_refs, keep_ref, send_ref = refs
    size = part_refs[0].shape[0] // 2
    for ref, step in zip(part_refs, far_first(len(part_refs))):
        cut = slice(step * size, (step + 1) * size)
        keep_ref[cut, :] = ref[:size, :]
        send_ref[cut, :] = ref[size:, :]


def slope(pre_act):
    normal_cdf = 0.5 * (1.0 + lax.erf(pre_act * 0.7071067811865476))
    density = jnp.exp(-0.5 * pre_act * pre_act) * 0.3989422804014327
    return normal_cdf + pre_act * density


def slope_kernel(pieces, pre_hbm, slope_ref, pre, sems):
    rows = pre.shape[0] // pieces
    copies = []
    for piece in range(pieces):
        cut = pl.ds(piece * rows, rows)
        copies.append(pltpu.make_async_copy(pre_hbm.at[0, cut], pre.at[cut], sems.at[piece]))
        copies[-1].start()
    for piece, copy in enumerate(copies):
        copy.wait()
        cut = slice(piece * rows, (piece + 1) * rows)
        slope_ref[cut, :] = slope(pre[cut, :].astype(F32))


def final_kernel(capacity, share, turn, base, *refs):
    part_ref, slope_ref = refs[:2]
    out_hbm, out, sem = refs[-3:]
    rows, slots = out.shape
    part = lax.rem(lax.axis_index("frame") + turn, share) * (slope_ref.shape[0] // share)
    cut = pl.ds(pl.multiple_of(part + base, rows), rows)
    source = lax.broadcasted_iota(jnp.int32, (slots, slots), 0)
    goal = lax.broadcasted_iota(jnp.int32, (slots, slots), 1)
    moved = (goal ^ ((lax.axis_index("frame") ^ turn) * capacity)) == source
    hidden = lax.dot_general(
        part_ref[...],
        jnp.where(moved, 1.0, 0.0).astype(BF16),
        (((0,), (0,)), ((), ())),
        preferred_element_type=F32,
    )
    out[...] = (hidden * slope_ref[cut, :]).astype(BF16)
    store = pltpu.make_async_copy(out, out_hbm.at[0, cut], sem.at[0])
    store.start()
    store.wait()


def chunk_rows(quarter):
    return [quarter // 2] * 2


def body(
    peers,
    owners_count,
    value_grad,
    w_value,
    norm_gain,
    vis_pos,
    frame_owner,
    ques_span,
    vis_proj,
    vis_resid,
    ques_hidden,
    w_down,
    pre_owned,
):
    _, tokens, width = vis_proj.shape
    shard_len, key_width = value_grad.shape[1:]
    length = ques_hidden.shape[1]
    features = peers * width
    slots = pre_owned.shape[2]
    capacity = slots // owners_count
    gain = norm_gain.reshape(1, width)
    owner = frame_owner.reshape(1, tokens)
    row = shape((8, tokens), F32)
    tall = shape((width, tokens), F32)
    dma = pltpu.SemaphoreType.DMA

    pieces = max(1, shard_len // 256)
    own = call(
        functools.partial(pick_kernel, pieces),
        shape((tokens, key_width), BF16),
        [HBM, HBM],
        [
            pltpu.VMEM((1, tokens), jnp.int32),
            pltpu.VMEM((shard_len, key_width), BF16),
            dma((pieces + 1,)),
        ],
        grant=PICK_GRANT,
    )(vis_pos, value_grad)
    own_all = [own] + [swap(own, "seq", peers, k) for k in range(1, peers)]

    stats, projt, residt, gaint, meant, weight = call(
        load_kernel,
        [row, tall, tall, tall, tall, shape(w_value.shape, BF16)],
        [HBM, VMEM, VMEM, VMEM, VMEM, HBM],
        [pltpu.SMEM((1, 2), jnp.int32), dma((2,))],
        grant=LOAD_GRANT,
    )(ques_span, ques_hidden, gain, vis_proj, vis_resid, w_value)

    scaledt, sums = call(
        functools.partial(norm_kernel, peers),
        [tall, row],
        [VMEM] * (peers + 4),
        [pltpu.VMEM((key_width, tokens), BF16)],
    )(*own_all, stats, weight, gaint, projt)
    sums_all = [sums] + [swap(sums, "seq", peers, k) for k in range(1, peers)]

    paired = capacity % 16 == 0 and owners_count % 2 == 0
    share = 2 if paired else 1
    pieces = owners_count // 2 if paired else 1
    chunks = chunk_rows(w_down.shape[0] // peers // share)
    bases = [sum(chunks[:i]) for i in range(len(chunks))]
    chain = Chain()

    def sems(rows, count=peers):
        return dma((count * (rows // min(rows, 256)),))

    def preload(caller, half, after):
        count = peers // 2 * (chunks[0] // min(chunks[0], 256))
        (weights,) = caller(
            functools.partial(preload_kernel, half * count, count, peers, share, chunks[0]),
            [shape((peers // 2 * chunks[0], width), BF16)],
            [HBM, VMEM],
            [sems(chunks[0], peers // 2)],
        )(w_down, after)
        return weights

    preloaded = [preload(call, 0, sums)]
    gradt, logit = chain.call(
        functools.partial(gate_kernel, features, peers),
        [shape((width + 16, tokens), BF16), row],
        [VMEM] * (peers + 5) + [ANY],
    )(*sums_all, projt, residt, scaledt, meant, owner, preloaded[0])
    preloaded.append(preload(chain.call, 1, logit))
    gradts = [gradt] + [swap(gradt, "frame", owners_count, k) for k in range(1, share)]

    def down(index):
        rows = chunks[index]
        weights = [pltpu.VMEM((peers * rows, width), BF16), sems(rows)]
        partial = chain.call(
            functools.partial(
                down_kernel, peers, share, bases[index], rows, 0 if index else len(preloaded)
            ),
            [shape((rows, share * tokens), BF16)] * peers,
            ([HBM] if index else [VMEM] * len(preloaded)) + [VMEM] * share,
            [pltpu.VMEM((width, share * tokens), BF16)] + (weights if index else []),
            cost=2 * peers * rows * width,
        )(*([w_down] if index else preloaded), *gradts)
        return swaps(partial, "seq", peers)

    def place(parts):
        rows = parts[0].shape[0]
        placed = chain.call(
            functools.partial(place_kernel, capacity, share, pieces, len(parts)),
            [shape((slots * share // pieces, rows), BF16)] * pieces,
            [VMEM] * (share + len(parts)),
        )(*gradts, *parts)
        if paired:
            return swaps(placed, "frame", owners_count, 2)
        order = jnp.arange(owners_count) ^ lax.axis_index("frame")
        split = placed[0].reshape(owners_count, capacity, rows)[order]
        split = lax.all_to_all(split, "frame", split_axis=0, concat_axis=0, tiled=True)
        return [split[order].reshape(slots, rows)]

    def group(parts):
        if not paired:
            return parts
        keep, send = chain.call(
            group_kernel,
            [shape((slots, parts[0].shape[1]), BF16)] * 2,
            [VMEM] * pieces,
        )(*parts)
        return [keep, swap(send, "frame", owners_count, 1)]

    def finish(parts, index, turn, held):
        rows = chunks[index]
        return chain.call(
            functools.partial(final_kernel, capacity, share, turn, bases[index]),
            [shape(pre_owned.shape, BF16)],
            [VMEM, VMEM] + [HBM] * len(held),
            [pltpu.VMEM((rows, slots), BF16), dma((1,))],
            {2: 0} if held else None,
            [HBM],
            final=index == len(chunks) - 1 and turn == share - 1,
        )(parts[turn], slopes, *held)

    waiting = [down(0)]
    (slopes,) = chain.call(
        functools.partial(slope_kernel, 4),
        [shape(pre_owned.shape[1:], F32)],
        [HBM],
        [pltpu.VMEM(pre_owned.shape[1:], BF16), dma((4,))],
    )(pre_owned)
    (ques_grad,) = chain.call(
        ques_kernel,
        [shape(ques_hidden.shape, BF16)],
        [HBM, VMEM, HBM],
        [pltpu.SMEM((1, 2), jnp.int32), pltpu.VMEM((tokens, width), BF16), dma((2,))],
    )(ques_span, logit, vis_proj)
    waiting.append(down(1))
    placed = [place(parts) for parts in waiting]
    first = group(placed[0])
    held = finish(first, 0, 0, [])
    second = group(placed[1])
    for turn in range(1, share):
        held = finish(first, 0, turn, held)
    for turn in range(share):
        held = finish(second, 1, turn, held)
    return (held[0], ques_grad)


def solution(mesh):
    in_specs = (
        P("frame", "seq", None),
        P("seq", None),
        P("seq"),
        P("frame", None),
        P("frame", None, None),
        P("frame", None),
        P("frame", None, "seq"),
        P("frame", None, "seq"),
        P("frame", None, "seq"),
        P(None, "seq"),
        P("frame", "seq", None),
    )
    out_specs = (P("frame", "seq", None), P("frame", None, "seq"))
    run = functools.partial(body, mesh.shape["seq"], mesh.shape["frame"])
    return jax.shard_map(run, mesh=mesh, in_specs=in_specs, out_specs=out_specs, check_vma=False)
```

```python
import functools
import math

import jax
import jax.numpy as jnp
from jax import lax
from jax.experimental import pallas as pl
from jax.experimental.pallas import tpu as pltpu
from jax.sharding import PartitionSpec as P

EPSILON = 1e-06
F32 = jnp.float32
BF16 = jnp.bfloat16
LANES = 128
AHEAD = 4
MIB = 1024 * 1024
GRANT, LOAD_GRANT, PICK_GRANT = 40, 46, 53
HBM = pl.BlockSpec(memory_space=pltpu.HBM)
VMEM = pl.BlockSpec(memory_space=pltpu.VMEM)
ANY = pl.BlockSpec(memory_space=pl.ANY)


def call(
    kernel, out_shape, in_specs, scratch=(), aliases=None, out_specs=None, grant=GRANT, cost=1024
):
    return pl.pallas_call(
        kernel,
        out_shape=out_shape,
        in_specs=in_specs,
        out_specs=jax.tree.map(lambda _: VMEM, out_shape) if out_specs is None else out_specs,
        scratch_shapes=list(scratch),
        input_output_aliases=aliases or {},
        compiler_params=pltpu.CompilerParams(vmem_limit_bytes=grant * MIB),
        cost_estimate=pl.CostEstimate(flops=256 * cost, bytes_accessed=cost, transcendentals=0),
    )


class Chain:
    def __init__(self):
        self.last = []

    def call(
        self,
        kernel,
        out_shape,
        in_specs,
        scratch=(),
        aliases=None,
        out_specs=None,
        cost=1024,
        final=False,
    ):
        given, made, linked = len(in_specs), len(out_shape), len(self.last)
        marks = [] if final else [shape((8, LANES), F32)]

        def run(*refs):
            outs = refs[given + linked :]
            for mark in outs[made : made + len(marks)]:
                mark[...] = jnp.zeros(mark.shape, F32)
            kernel(*refs[:given], *outs[:made], *outs[made + len(marks) :])

        out_specs = [VMEM] * made if out_specs is None else out_specs
        run_call = call(
            run,
            [*out_shape, *marks],
            [*in_specs, *[VMEM] * linked],
            scratch,
            aliases,
            [*out_specs, *[VMEM] * len(marks)],
            cost=cost,
        )

        def apply(*args):
            results = run_call(*args, *self.last)
            self.last = list(results[made:])
            return list(results[:made])

        return apply


def shape(dims, dtype):
    return jax.ShapeDtypeStruct(dims, dtype)


def swap(value, axis, count, step):
    return lax.ppermute(value, axis, [(i, i ^ step) for i in range(count)])


def far_first(count):
    return [0, *reversed(range(1, count))]


def swaps(values, axis, count, stride=1):
    return [
        swap(value, axis, count, step * stride) if step else value
        for value, step in zip(values, far_first(len(values)))
    ]


def to_column(row):
    return jnp.transpose(jnp.broadcast_to(row, (LANES, row.shape[1])), (1, 0))


def pick_kernel(pieces, pos_hbm, rows_hbm, own_ref, pos, rows, sems):
    tokens, shard_len = pos.shape[1], rows.shape[0]
    size = shard_len // pieces
    head = pltpu.make_async_copy(pos_hbm, pos, sems.at[pieces])
    head.start()
    copies = []
    for piece in range(pieces):
        cut = pl.ds(piece * size, size)
        copies.append(
            pltpu.make_async_copy(rows_hbm.at[0, cut], rows.at[cut], sems.at[piece])
        )
        copies[-1].start()
    offset = lax.axis_index("seq") * shard_len
    head.wait()
    column = to_column(pos[...] - offset)
    lanes = lax.broadcasted_iota(jnp.int32, (tokens, LANES), 1)
    total = None
    for piece in range(pieces):
        select = jnp.concatenate(
            [
                jnp.where(column == lanes + at, 1.0, 0.0).astype(BF16)
                for at in range(piece * size, (piece + 1) * size, LANES)
            ],
            axis=1,
        )
        copies[piece].wait()
        part = jnp.dot(
            select, rows[piece * size : (piece + 1) * size, :], preferred_element_type=F32
        )
        total = part if total is None else total + part
    own_ref[...] = total.astype(BF16)


def load_kernel(
    span_hbm, hidden_ref, proj_ref, resid_ref, weight_hbm,
    stats_ref, projt_ref, residt_ref, meant_ref, weight_ref,
    span, sems,
):
    load = pltpu.make_async_copy(weight_hbm, weight_ref, sems.at[0])
    head = pltpu.make_async_copy(span_hbm, span, sems.at[1])
    head.start()
    load.start()
    tokens, width = proj_ref.shape[1:]
    for at in range(0, width, LANES):
        cut = slice(at, at + LANES)
        projt_ref[cut, :] = jnp.transpose(proj_ref[0, :, cut], (1, 0)).astype(F32)
        residt_ref[cut, :] = jnp.transpose(resid_ref[0, :, cut], (1, 0)).astype(F32)
    head.wait()
    start, count = span[0, 0], span[0, 1]
    places = lax.broadcasted_iota(jnp.int32, (hidden_ref.shape[1], 1), 0)
    mask = ((places >= start) & (places < start + count)).astype(F32)
    query = square = cross = jnp.zeros((LANES, tokens), F32)
    for at in range(0, width, LANES):
        cut = slice(at, at + LANES)
        mean = jnp.sum(hidden_ref[0, :, cut].astype(F32) * mask, axis=0, keepdims=True)
        meant = to_column(mean / count.astype(F32))
        meant_ref[cut, :] = meant
        projt = projt_ref[cut, :]
        residt = residt_ref[cut, :]
        query = query + projt * meant
        square = square + projt * projt
        cross = cross + projt * residt
    stats_ref[...] = jnp.zeros(stats_ref.shape, F32)
    for row, value in enumerate((query, square, cross)):
        stats_ref[row : row + 1, :] = jnp.sum(value, axis=0, keepdims=True)
    load.wait()


def norm_kernel(peers, *refs):
    own_refs = refs[:peers]
    stats_ref, weight_ref, gain_ref, projt_ref, scaledt_ref, sums_ref, pickedt = refs[peers:]
    key_width = own_refs[0].shape[1]
    for at in range(0, key_width, LANES):
        cut = slice(at, at + LANES)
        picked = own_refs[0][:, cut].astype(F32)
        for ref in own_refs[1:]:
            picked = picked + ref[:, cut].astype(F32)
        pickedt[cut, :] = jnp.transpose(picked, (1, 0)).astype(BF16)
    width, tokens = projt_ref.shape
    total = jnp.zeros((LANES, tokens), F32)
    for at in range(0, width, 256):
        cut = slice(at, at + 256)
        normed = jnp.dot(weight_ref[cut, :], pickedt[...], preferred_element_type=F32)
        gain = [to_column(gain_ref[:, first : first + LANES]) for first in (at, at + LANES)]
        scaled = normed * jnp.concatenate(gain, axis=0)
        scaledt_ref[cut, :] = scaled
        terms = scaled * projt_ref[cut, :]
        total = total + terms[:LANES] + terms[LANES:]
    sums_ref[...] = stats_ref[...]
    sums_ref[3:4, :] = jnp.sum(total, axis=0, keepdims=True)


def weight_copy(weight_hbm, weights, sems, peers, share, base, rows, index, skipped=0):
    quarter = weight_hbm.shape[0] // peers
    block = min(rows, 256)
    inner = rows // block
    step = lax.rem(peers - index // inner, peers)
    first = (lax.axis_index("seq") ^ step) * quarter + base + lax.rem(index, inner) * block
    first += lax.rem(lax.axis_index("frame"), share) * (quarter // share)
    place = index - skipped
    return pltpu.make_async_copy(
        weight_hbm.at[pl.ds(pl.multiple_of(first, block), block)],
        weights.at[pl.ds(pl.multiple_of(place * block, block), block)],
        sems.at[place],
    )


def preload_kernel(skipped, count, peers, share, rows, weight_hbm, after_ref, weights_ref, sems):
    del after_ref
    copies = [
        weight_copy(weight_hbm, weights_ref, sems, peers, share, 0, rows, index, skipped)
        for index in range(skipped, skipped + count)
    ]
    for copy in copies:
        copy.start()
    for copy in copies:
        copy.wait()


def gate_kernel(features, peers, *refs):
    sums_refs = refs[:peers]
    projt_ref, residt_ref, scaledt_ref, meant_ref, owner_ref, after_ref = refs[peers : peers + 6]
    del after_ref
    gradt_ref, logit_ref = refs[peers + 6 :]
    sums = sums_refs[0][...]
    for ref in sums_refs[1:]:
        sums = sums + ref[...]
    sum_query, sum_square, sum_resid, sum_norm = (sums[i : i + 1] for i in range(4))
    gate_scale = 4.0 / math.sqrt(features)
    gate = jax.nn.sigmoid(gate_scale * sum_query)
    inv_rms = lax.rsqrt(gate * gate * sum_square / features + EPSILON)
    coef = gate * inv_rms * inv_rms * inv_rms * (gate * sum_norm) / features
    gate_grad = sum_resid + inv_rms * sum_norm - coef * sum_square
    logit = gate_grad * gate * (1.0 - gate) * gate_scale
    logit_ref[...] = jnp.broadcast_to(logit, logit_ref.shape)
    width = projt_ref.shape[0]
    for at in range(0, width, LANES):
        cut = slice(at, at + LANES)
        grad = residt_ref[cut, :] + inv_rms * scaledt_ref[cut, :] - coef * projt_ref[cut, :]
        gradt_ref[cut, :] = (gate * grad + logit * meant_ref[cut, :]).astype(BF16)
    tail = gradt_ref.shape[0] - width
    owner = owner_ref[...].astype(F32)
    gradt_ref[width:, :] = jnp.broadcast_to(owner, (tail, owner.shape[1])).astype(BF16)


def down_kernel(peers, share, base, rows, held, *refs):
    weight_refs = refs[: max(held, 1)]
    gradt_refs = refs[len(weight_refs) : len(weight_refs) + share]
    scratch = list(refs[len(weight_refs) + share :])
    out_refs = [scratch.pop(0) for _ in range(peers)]
    joined = scratch.pop(0)
    block = min(rows, 256)
    inner = rows // block
    total = peers * inner

    def copy(index):
        return weight_copy(weight_refs[0], *scratch, peers, share, base, rows, index)

    if not held:
        for index in range(min(AHEAD, total)):
            copy(index).start()
    width, tokens = joined.shape[0], gradt_refs[0].shape[1]
    for index, ref in enumerate(gradt_refs):
        joined[:, index * tokens : (index + 1) * tokens] = ref[:width, :]
    each = total // len(weight_refs)
    for peer, ref in enumerate(out_refs):
        if held:
            weights = weight_refs[peer * inner // each]
            for part in range(inner):
                at = (peer * inner + part) % each * block
                value = jnp.dot(
                    weights[at : at + block, :], joined[...], preferred_element_type=F32
                )
                ref[part * block : (part + 1) * block, :] = value.astype(BF16)
            continue

        def step(part, carry, peer=peer, ref=ref):
            index = peer * inner + part
            copy(index).wait()

            @pl.when(index + AHEAD < total)
            def _():
                copy(index + AHEAD).start()

            at = pl.multiple_of(index * block, block)
            value = jnp.dot(
                scratch[0][pl.ds(at, block), :], joined[...], preferred_element_type=F32
            )
            ref[pl.ds(pl.multiple_of(part * block, block), block), :] = value.astype(BF16)
            return carry

        lax.fori_loop(0, inner, step, 0)


def ques_kernel(span_hbm, logit_ref, proj_hbm, out_ref, span, proj, sems):
    head = pltpu.make_async_copy(span_hbm, span, sems.at[0])
    load = pltpu.make_async_copy(proj_hbm.at[0], proj, sems.at[1])
    head.start()
    load.start()
    head.wait()
    start, count = span[0, 0], span[0, 1]
    length, width = out_ref.shape[1], out_ref.shape[2]
    places = lax.broadcasted_iota(jnp.int32, (length, LANES), 0)
    mask = ((places >= start) & (places < start + count)).astype(F32)
    column = to_column(logit_ref[0:1, :])
    load.wait()
    for at in range(0, width, LANES):
        cut = slice(at, at + LANES)
        total = jnp.sum(column * proj[:, cut].astype(F32), axis=0, keepdims=True)
        out_ref[0, :, cut] = (mask * total / count.astype(F32)).astype(BF16)


def targets(owner, capacity, share, source):
    tokens = owner.shape[1]
    above = lax.broadcasted_iota(jnp.int32, (tokens, tokens), 0)
    below = lax.broadcasted_iota(jnp.int32, (tokens, tokens), 1)
    earlier = jnp.where((to_column(owner) == owner) & (above < below), 1.0, 0.0)
    rank = jnp.sum(earlier, axis=0, keepdims=True).astype(jnp.int32)
    away = owner ^ lax.axis_index("frame")
    return (away * share + source) * capacity + rank


def place_kernel(capacity, share, pieces, mine, *refs):
    gradt_refs = refs[:share]
    part_refs = refs[share : share + mine]
    out_refs = refs[-pieces:]
    target = jnp.concatenate(
        [
            targets(ref[-16:-15, :].astype(F32).astype(jnp.int32), capacity, share, source)
            for source, ref in enumerate(gradt_refs)
        ],
        axis=1,
    )
    size = out_refs[0].shape[0]
    places = lax.broadcasted_iota(jnp.int32, (size * pieces, target.shape[1]), 0)
    placing = jnp.where(places == target, 1.0, 0.0).astype(BF16)
    total = part_refs[0][...].astype(F32)
    for ref in part_refs[1:]:
        total = total + ref[...].astype(F32)
    placed = lax.dot_general(
        placing, total.astype(BF16), (((1,), (1,)), ((), ())), preferred_element_type=F32
    ).astype(BF16)
    for ref, step in zip(out_refs, far_first(pieces)):
        ref[...] = placed[step * size : (step + 1) * size, :]


def group_kernel(*refs):
    *part_refs, keep_ref, send_ref = refs
    size = part_refs[0].shape[0] // 2
    for ref, step in zip(part_refs, far_first(len(part_refs))):
        cut = slice(step * size, (step + 1) * size)
        keep_ref[cut, :] = ref[:size, :]
        send_ref[cut, :] = ref[size:, :]


def slope(pre_act):
    normal_cdf = 0.5 * (1.0 + lax.erf(pre_act * 0.7071067811865476))
    density = jnp.exp(-0.5 * pre_act * pre_act) * 0.3989422804014327
    return normal_cdf + pre_act * density


def slope_kernel(pieces, pre_hbm, slope_ref, pre, sems):
    rows = pre.shape[0] // pieces
    copies = []
    for piece in range(pieces):
        cut = pl.ds(piece * rows, rows)
        copies.append(pltpu.make_async_copy(pre_hbm.at[0, cut], pre.at[cut], sems.at[piece]))
        copies[-1].start()
    for piece, copy in enumerate(copies):
        copy.wait()
        cut = slice(piece * rows, (piece + 1) * rows)
        slope_ref[cut, :] = slope(pre[cut, :].astype(F32))


def final_kernel(capacity, share, turn, base, *refs):
    part_ref, slope_ref = refs[:2]
    out_hbm, out, sem = refs[-3:]
    rows, slots = out.shape
    part = lax.rem(lax.axis_index("frame") + turn, share) * (slope_ref.shape[0] // share)
    cut = pl.ds(pl.multiple_of(part + base, rows), rows)
    source = lax.broadcasted_iota(jnp.int32, (slots, slots), 0)
    goal = lax.broadcasted_iota(jnp.int32, (slots, slots), 1)
    moved = (goal ^ ((lax.axis_index("frame") ^ turn) * capacity)) == source
    hidden = lax.dot_general(
        part_ref[...],
        jnp.where(moved, 1.0, 0.0).astype(BF16),
        (((0,), (0,)), ((), ())),
        preferred_element_type=F32,
    )
    out[...] = (hidden * slope_ref[cut, :]).astype(BF16)
    store = pltpu.make_async_copy(out, out_hbm.at[0, cut], sem.at[0])
    store.start()
    store.wait()


def chunk_rows(quarter):
    return [quarter // 2] * 2


def body(
    peers,
    owners_count,
    value_grad,
    w_value,
    norm_gain,
    vis_pos,
    frame_owner,
    ques_span,
    vis_proj,
    vis_resid,
    ques_hidden,
    w_down,
    pre_owned,
):
    _, tokens, width = vis_proj.shape
    shard_len, key_width = value_grad.shape[1:]
    length = ques_hidden.shape[1]
    features = peers * width
    slots = pre_owned.shape[2]
    capacity = slots // owners_count
    gain = norm_gain.reshape(1, width)
    owner = frame_owner.reshape(1, tokens)
    row = shape((8, tokens), F32)
    tall = shape((width, tokens), F32)
    dma = pltpu.SemaphoreType.DMA

    pieces = max(1, shard_len // 256)
    own = call(
        functools.partial(pick_kernel, pieces),
        shape((tokens, key_width), BF16),
        [HBM, HBM],
        [
            pltpu.VMEM((1, tokens), jnp.int32),
            pltpu.VMEM((shard_len, key_width), BF16),
            dma((pieces + 1,)),
        ],
        grant=PICK_GRANT,
    )(vis_pos, value_grad)
    own_all = [own] + [swap(own, "seq", peers, k) for k in range(1, peers)]

    stats, projt, residt, meant, weight = call(
        load_kernel,
        [row, tall, tall, tall, shape(w_value.shape, BF16)],
        [HBM, VMEM, VMEM, VMEM, HBM],
        [pltpu.SMEM((1, 2), jnp.int32), dma((2,))],
        grant=LOAD_GRANT,
    )(ques_span, ques_hidden, vis_proj, vis_resid, w_value)

    scaledt, sums = call(
        functools.partial(norm_kernel, peers),
        [tall, row],
        [VMEM] * (peers + 4),
        [pltpu.VMEM((key_width, tokens), BF16)],
    )(*own_all, stats, weight, gain, projt)
    sums_all = [sums] + [swap(sums, "seq", peers, k) for k in range(1, peers)]

    paired = capacity % 16 == 0 and owners_count % 2 == 0
    share = 2 if paired else 1
    pieces = owners_count // 2 if paired else 1
    chunks = chunk_rows(w_down.shape[0] // peers // share)
    bases = [sum(chunks[:i]) for i in range(len(chunks))]
    chain = Chain()

    def sems(rows, count=peers):
        return dma((count * (rows // min(rows, 256)),))

    def preload(caller, half, after):
        count = peers // 2 * (chunks[0] // min(chunks[0], 256))
        (weights,) = caller(
            functools.partial(preload_kernel, half * count, count, peers, share, chunks[0]),
            [shape((peers // 2 * chunks[0], width), BF16)],
            [HBM, VMEM],
            [sems(chunks[0], peers // 2)],
        )(w_down, after)
        return weights

    preloaded = [preload(call, 0, sums)]
    gradt, logit = chain.call(
        functools.partial(gate_kernel, features, peers),
        [shape((width + 16, tokens), BF16), row],
        [VMEM] * (peers + 5) + [ANY],
    )(*sums_all, projt, residt, scaledt, meant, owner, preloaded[0])
    preloaded.append(preload(chain.call, 1, logit))
    gradts = [gradt] + [swap(gradt, "frame", owners_count, k) for k in range(1, share)]

    def down(index):
        rows = chunks[index]
        weights = [pltpu.VMEM((peers * rows, width), BF16), sems(rows)]
        partial = chain.call(
            functools.partial(
                down_kernel, peers, share, bases[index], rows, 0 if index else len(preloaded)
            ),
            [shape((rows, share * tokens), BF16)] * peers,
            ([HBM] if index else [VMEM] * len(preloaded)) + [VMEM] * share,
            [pltpu.VMEM((width, share * tokens), BF16)] + (weights if index else []),
            cost=2 * peers * rows * width,
        )(*([w_down] if index else preloaded), *gradts)
        return swaps(partial, "seq", peers)

    def place(parts):
        rows = parts[0].shape[0]
        placed = chain.call(
            functools.partial(place_kernel, capacity, share, pieces, len(parts)),
            [shape((slots * share // pieces, rows), BF16)] * pieces,
            [VMEM] * (share + len(parts)),
        )(*gradts, *parts)
        if paired:
            return swaps(placed, "frame", owners_count, 2)
        order = jnp.arange(owners_count) ^ lax.axis_index("frame")
        split = placed[0].reshape(owners_count, capacity, rows)[order]
        split = lax.all_to_all(split, "frame", split_axis=0, concat_axis=0, tiled=True)
        return [split[order].reshape(slots, rows)]

    def group(parts):
        if not paired:
            return parts
        keep, send = chain.call(
            group_kernel,
            [shape((slots, parts[0].shape[1]), BF16)] * 2,
            [VMEM] * pieces,
        )(*parts)
        return [keep, swap(send, "frame", owners_count, 1)]

    def finish(parts, index, turn, held):
        rows = chunks[index]
        return chain.call(
            functools.partial(final_kernel, capacity, share, turn, bases[index]),
            [shape(pre_owned.shape, BF16)],
            [VMEM, VMEM] + [HBM] * len(held),
            [pltpu.VMEM((rows, slots), BF16), dma((1,))],
            {2: 0} if held else None,
            [HBM],
            final=index == len(chunks) - 1 and turn == share - 1,
        )(parts[turn], slopes, *held)

    waiting = [down(0), down(1)]
    placed = [place(parts) for parts in waiting]
    first = group(placed[0])
    (slopes,) = chain.call(
        functools.partial(slope_kernel, 4),
        [shape(pre_owned.shape[1:], F32)],
        [HBM],
        [pltpu.VMEM(pre_owned.shape[1:], BF16), dma((4,))],
    )(pre_owned)
    (ques_grad,) = chain.call(
        ques_kernel,
        [shape(ques_hidden.shape, BF16)],
        [HBM, VMEM, HBM],
        [pltpu.SMEM((1, 2), jnp.int32), pltpu.VMEM((tokens, width), BF16), dma((2,))],
    )(ques_span, logit, vis_proj)
    held = finish(first, 0, 0, [])
    second = group(placed[1])
    for turn in range(1, share):
        held = finish(first, 0, turn, held)
    for turn in range(share):
        held = finish(second, 1, turn, held)
    return (held[0], ques_grad)


def solution(mesh):
    in_specs = (
        P("frame", "seq", None),
        P("seq", None),
        P("seq"),
        P("frame", None),
        P("frame", None, None),
        P("frame", None),
        P("frame", None, "seq"),
        P("frame", None, "seq"),
        P("frame", None, "seq"),
        P(None, "seq"),
        P("frame", "seq", None),
    )
    out_specs = (P("frame", "seq", None), P("frame", None, "seq"))
    run = functools.partial(body, mesh.shape["seq"], mesh.shape["frame"])
    return jax.shard_map(run, mesh=mesh, in_specs=in_specs, out_specs=out_specs, check_vma=False)
```
